32 devices in a mesh: dp: 4 (over y, core), seq: 8 (over z, x).
Axes of the slice: x: 2, y: 2, z: 4, core: 2. Of those that a mesh axis runs over, the one named last changes fastest.
Arguments:
- tokens: bfloat16 [8, 1536, 1536], P('dp', 'seq'), may hold values from -6 to 6
- cotangent: bfloat16 [8, 1536, 1536], P('dp', 'seq'), may hold values from -6 to 6
- norm_gains: float32 [2, 1536], P(None, ('dp', 'seq')), may hold values from 0.5 to 1.5
- in_proj: float32 [1536, 4608], P(('dp', 'seq')), may hold values from -0.15625 to 0.15625
- conv_taps: float32 [3, 1536], P(None, ('dp', 'seq')), may hold values from -3 to 3
- out_proj: float32 [1536, 1536], P(('dp', 'seq')), may hold values from -0.15625 to 0.15625
- gate_up: float32 [2, 1536, 6912], P(None, ('dp', 'seq')), may hold values from -0.15625 to 0.15625
- down_proj: float32 [6912, 1536], P(('dp', 'seq')), may hold values from -0.078125 to 0.078125
- first_gains: float32 [2, 1536], P(None, ('dp', 'seq')), may hold values from -64 to 64
- first_in: float32 [1536, 4608], P(('dp', 'seq')), may hold values from -64 to 64
- first_conv: float32 [3, 1536], P(None, ('dp', 'seq')), may hold values from -64 to 64
- first_out: float32 [1536, 1536], P(('dp', 'seq')), may hold values from -64 to 64
- first_gate_up: float32 [2, 1536, 6912], P(None, ('dp', 'seq')), may hold values from -20 to 20
- first_down: float32 [6912, 1536], P(('dp', 'seq')), may hold values from -40 to 40
- second_gains: float32 [2, 1536], P(None, ('dp', 'seq')), may hold values from 651.264 to 2580.48
- second_in: float32 [1536, 4608], P(('dp', 'seq')), may hold values from 417.792 to 1658.88
- second_conv: float32 [3, 1536], P(None, ('dp', 'seq')), may hold values from 651.264 to 2580.48
- second_out: float32 [1536, 1536], P(('dp', 'seq')), may hold values from 528.384 to 2088.96
- second_gate_up: float32 [2, 1536, 6912], P(None, ('dp', 'seq')), may hold values from 57.7536 to 233.472
- second_down: float32 [6912, 1536], P(('dp', 'seq')), may hold values from 159.744 to 651.264
Outputs:
- block_out: bfloat16 [8, 1536, 1536], P('dp', 'seq')
- token_grad: float32 [8, 1536, 1536], P('dp', 'seq')
- grad_gains: float32 [2, 1536], P(None, ('dp', 'seq'))
- grad_in: float32 [1536, 4608], P(('dp', 'seq'))
- grad_conv: float32 [3, 1536], P(None, ('dp', 'seq'))
- grad_out: float32 [1536, 1536], P(('dp', 'seq'))
- grad_gate_up: float32 [2, 1536, 6912], P(None, ('dp', 'seq'))
- grad_down: float32 [6912, 1536], P(('dp', 'seq'))
- moment_gains: float32 [2, 1536], P(None, ('dp', 'seq'))
- moment_in: float32 [1536, 4608], P(('dp', 'seq'))
- moment_conv: float32 [3, 1536], P(None, ('dp', 'seq'))
- moment_out: float32 [1536, 1536], P(('dp', 'seq'))
- moment_gate_up: float32 [2, 1536, 6912], P(None, ('dp', 'seq'))
- moment_down: float32 [6912, 1536], P(('dp', 'seq'))
- updated_gains: float32 [2, 1536], P(None, ('dp', 'seq'))
- updated_in: float32 [1536, 4608], P(('dp', 'seq'))
- updated_conv: float32 [3, 1536], P(None, ('dp', 'seq'))
- updated_out: float32 [1536, 1536], P(('dp', 'seq'))
- updated_gate_up: float32 [2, 1536, 6912], P(None, ('dp', 'seq'))
- updated_down: float32 [6912, 1536], P(('dp', 'seq'))
The draws below stay inside these ranges and needn't reach their ends.
All inputs are finite; a program needn't handle non-finite values.
Results may differ from the reference program's by a relative error of at most 0.012.
The reference program's roundings to bfloat16 on the way count: a program that leaves them out, or rounds other values in their place, can miss the bound.
Values may be sent and summed in bfloat16 or wider, within the bound.
A program may use at most 512 MiB of HBM per device.

```python
import math
import jax
import jax.numpy as jnp
from jax import lax

D = 1536
FF = 6912
KERNEL = 3
STEP = 10
SEQUENCES = 8
SEQ_LEN = 1536
TOKENS = 12288


def block_levels(own_key, extent, pieces, smallest, largest):
    level = 1.0
    for dim, shards_of in pieces:
        draws = jax.random.uniform(jax.random.fold_in(jax.random.fold_in(own_key, 6), dim), (shards_of,), jnp.float32, smallest / len(pieces), largest / len(pieces))
        level = level * jnp.repeat(jnp.exp(draws), extent[dim] // shards_of).reshape((-1,) + (1,) * (len(extent) - 1 - dim))
    return level


def gaussian(key, shape, spread, most, pieces=(), held_as=jnp.bfloat16):
    drawn = jax.random.normal(key, shape, jnp.float32) * spread
    if len(pieces) > 0:
        drawn = block_levels(key, shape, pieces, -0.22, 0.18) * drawn
    return jnp.clip(drawn, min=-most, max=most).astype(held_as)


def setup_inputs(seed: int = 0) -> dict:
    keys = jax.random.split(jax.random.key(seed), 21)
    return {
        "tokens": gaussian(keys[0], (SEQUENCES, SEQ_LEN, D), 1.0, 6.0, ((0, 4), (1, 8))),
        "cotangent": gaussian(keys[1], (SEQUENCES, SEQ_LEN, D), 1.0, 6.0, ((0, 4), (1, 8))),
        "norm_gains": jnp.clip(1.0 + 0.1 * jax.random.normal(keys[2], (2, D), jnp.float32), 0.5, 1.5),
        "in_proj": gaussian(keys[3], (D, 3 * D), D ** -0.5, 0.15625, ((0, 32),), jnp.float32),
        "conv_taps": gaussian(keys[4], (KERNEL, D), 0.5, 3.0, ((1, 32),), jnp.float32),
        "out_proj": gaussian(keys[5], (D, D), D ** -0.5, 0.15625, ((0, 32),), jnp.float32),
        "gate_up": gaussian(keys[6], (2, D, FF), D ** -0.5, 0.15625, ((1, 32),), jnp.float32),
        "down_proj": gaussian(keys[7], (FF, D), FF ** -0.5, 0.078125, ((0, 32),), jnp.float32),
        "first_gains": gaussian(keys[8], (2, D), (0.111 * TOKENS ** 0.5), 64.0, ((1, 32),), jnp.float32),
        "first_in": gaussian(keys[9], (D, 3 * D), (0.089 * TOKENS ** 0.5), 64.0, ((0, 32),), jnp.float32),
        "first_conv": gaussian(keys[10], (KERNEL, D), (0.111 * TOKENS ** 0.5), 64.0, ((1, 32),), jnp.float32),
        "first_out": gaussian(keys[11], (D, D), (0.1 * TOKENS ** 0.5), 64.0, ((0, 32),), jnp.float32),
        "first_gate_up": gaussian(keys[12], (2, D, FF), (0.033 * TOKENS ** 0.5), 20.0, ((1, 32),), jnp.float32),
        "first_down": gaussian(keys[13], (FF, D), (0.056 * TOKENS ** 0.5), 40.0, ((0, 32),), jnp.float32),
        "second_gains": jnp.clip(jnp.exp(math.log(2580.48) - 1.37681564 * jax.random.uniform(keys[14], (2, D), jnp.float32) ** block_levels(keys[14], (2, D), ((1, 32),), -0.2, 0.2)), 651.264, 2580.48),
        "second_in": jnp.clip(jnp.exp(math.log(1658.88) - 1.37891428 * jax.random.uniform(keys[15], (D, 3 * D), jnp.float32) ** block_levels(keys[15], (D, 3 * D), ((0, 32),), -0.2, 0.2)), 417.792, 1658.88),
        "second_conv": jnp.clip(jnp.exp(math.log(2580.48) - 1.37681564 * jax.random.uniform(keys[16], (KERNEL, D), jnp.float32) ** block_levels(keys[16], (KERNEL, D), ((1, 32),), -0.2, 0.2)), 651.264, 2580.48),
        "second_out": jnp.clip(jnp.exp(math.log(2088.96) - 1.3745984 * jax.random.uniform(keys[17], (D, D), jnp.float32) ** block_levels(keys[17], (D, D), ((0, 32),), -0.2, 0.2)), 528.384, 2088.96),
        "second_gate_up": jnp.clip(jnp.exp(math.log(233.472) - 1.3968765 * jax.random.uniform(keys[18], (2, D, FF), jnp.float32) ** block_levels(keys[18], (2, D, FF), ((1, 32),), -0.2, 0.2)), 57.7536, 233.472),
        "second_down": jnp.clip(jnp.exp(math.log(651.264) - 1.4053425 * jax.random.uniform(keys[19], (FF, D), jnp.float32) ** block_levels(keys[19], (FF, D), ((0, 32),), -0.2, 0.2)), 159.744, 651.264),
    }


@jax.custom_vjp
def low(v):
    return lax.optimization_barrier(v.astype(jnp.bfloat16)).astype(jnp.float32)

@jax.custom_vjp
def low_back(v):
    return v

def low_keep(v):
    return (low(v), None)

def low_pass(kept, grad):
    return (grad,)

def back_keep(v):
    return (v, None)

def back_low(kept, grad):
    return (low(grad),)
low.defvjp(low_keep, low_pass)
low_back.defvjp(back_keep, back_low)

def rms_scale(values):
    return values * lax.rsqrt(lax.optimization_barrier(jnp.mean(values * values, axis=-1, keepdims=True)) + 1e-05)

def layer(hidden, gain_set, in_mat, taps, out_mat, gu_mat, down_mat):
    highest = lax.Precision.HIGHEST
    gain_set = low(gain_set)
    in_mat = low(in_mat)
    taps = low(taps)
    out_mat = low(out_mat)
    gu_mat = low(gu_mat)
    down_mat = low(down_mat)
    normed = low(rms_scale(hidden) * gain_set[0])
    projected = low_back(jnp.dot(normed, in_mat, precision=highest))
    b_part, c_part, x_part = jnp.split(projected, 3, axis=-1)
    mixed_in = b_part * x_part
    padded = jnp.pad(mixed_in, ((2, 0), (0, 0)))
    conv_out = taps[0] * padded[:-2] + taps[1] * padded[1:-1] + taps[2] * padded[2:]
    gated = low(c_part * conv_out)
    mixer = low_back(jnp.dot(gated, out_mat, precision=highest))
    middle = hidden + mixer
    normed_two = low(rms_scale(middle) * gain_set[1])
    gate_val = low_back(jnp.dot(normed_two, gu_mat[0], precision=highest))
    up_val = low_back(jnp.dot(normed_two, gu_mat[1], precision=highest))
    active = low(jax.nn.silu(gate_val) * up_val)
    branch = low_back(jnp.dot(active, down_mat, precision=highest))
    return middle + branch

def adamw(weight, first_mom, second_mom, gradient, rate, decay):
    bias_one = 1.0 - 0.9 ** STEP
    bias_two = 1.0 - 0.95 ** STEP
    first_new = 0.9 * first_mom + 0.1 * gradient
    second_new = 0.95 * second_mom + 0.05 * gradient * gradient
    direction = first_new / bias_one / (jnp.sqrt(second_new / bias_two) + 1e-08)
    return (second_new, weight - rate * (direction + decay * weight))

def reference(tokens, cotangent, norm_gains, in_proj, conv_taps, out_proj, gate_up, down_proj, first_gains, first_in, first_conv, first_out, first_gate_up, first_down, second_gains, second_in, second_conv, second_out, second_gate_up, second_down):
    params = (norm_gains, in_proj, conv_taps, out_proj, gate_up, down_proj)

    def one_sequence(running, seq_pair):
        seq_tokens, seq_cot = seq_pair
        outputs, pullback = jax.vjp(layer, seq_tokens.astype(jnp.float32), *params)
        grad_terms = pullback(seq_cot.astype(jnp.float32))
        summed = tuple((acc + term for acc, term in zip(running, grad_terms[1:])))
        return (summed, (outputs.astype(jnp.bfloat16), grad_terms[0]))
    zero_init = tuple((jnp.zeros_like(item) for item in params))
    totals, (block_out, token_grad) = lax.scan(one_sequence, zero_init, (tokens, cotangent))
    g_gains, g_in, g_conv, g_out, g_gu, g_down = totals
    m_gains, u_gains = adamw(norm_gains, first_gains, second_gains, g_gains, 0.4, 0.0)
    m_in, u_in = adamw(in_proj, first_in, second_in, g_in, 0.02, 0.1)
    m_conv, u_conv = adamw(conv_taps, first_conv, second_conv, g_conv, 0.2, 0.1)
    m_out, u_out = adamw(out_proj, first_out, second_out, g_out, 0.02, 0.1)
    m_gu, u_gu = adamw(gate_up, first_gate_up, second_gate_up, g_gu, 0.02, 0.1)
    m_down, u_down = adamw(down_proj, first_down, second_down, g_down, 0.01, 0.1)
    return (block_out, token_grad, g_gains, g_in, g_conv, g_out, g_gu, g_down, m_gains, m_in, m_conv, m_out, m_gu, m_down, u_gains, u_in, u_conv, u_out, u_gu, u_down)
```

```python
import functools

import jax
import jax.numpy as jnp
from jax import lax
from jax.experimental import pallas as pl
from jax.experimental.pallas import tpu as pltpu
from jax.sharding import Mesh
from jax.sharding import PartitionSpec as P

STEP = 10
MESH = pl.DeviceIdType.MESH
BF16 = jnp.bfloat16
F32 = jnp.float32
FLIPS = [(dy, dc, dx) for dy in (0, 1) for dc in (0, 1) for dx in (0, 1)][1:]
ANY = pl.BlockSpec(memory_space=pl.ANY)
VMEM = pl.BlockSpec(memory_space=pltpu.VMEM)


def place():
    return tuple(lax.axis_index(a) for a in ("y", "core", "z", "x"))


def flip(value, by):
    return 1 - value if by else value


def remote(src, dst, send, recv, device):
    return pltpu.make_async_remote_copy(
        src_ref=src,
        dst_ref=dst,
        send_sem=send,
        recv_sem=recv,
        device_id=device,
        device_id_type=MESH,
    )


def meet(peers):
    barrier = pltpu.get_barrier_semaphore()
    for peer in peers:
        pl.semaphore_signal(barrier, inc=1, device_id=peer, device_id_type=MESH)
    pl.semaphore_wait(barrier, len(peers))


class Gather:
    def __init__(self, own, full, send, recv):
        self.own, self.full, self.send, self.recv = own, full, send, recv
        self.started = []

    def go(self, src, slot, sem, device):
        seq, x = slot
        copy = remote(src, self.full.at[seq, x], self.send.at[sem], self.recv.at[sem], device)
        copy.start()
        self.started.append(copy)

    def first(self):
        y, c, _, x = place()
        for i, j in ((0, 1), (1, 0)):
            self.go(self.own.at[i], ((y * 2 + c) * 2 + i, x), i, {"x": 1 - x})
            self.go(self.own.at[j], ((y * 2 + c) * 2 + j, x), 2 + j, {"y": 1 - y})
        for i in (0, 1):
            self.go(self.own.at[i], ((y * 2 + c) * 2 + i, x), 6 + i, {"core": 1 - c})

    def arrived(self, sem):
        pltpu.make_async_copy(self.own.at[0], self.own.at[0], self.recv.at[sem]).wait()

    def rest(self):
        y, c, _, x = place()
        from_x = [((y * 2 + c) * 2 + i, 1 - x) for i in (0, 1)]
        from_y = [(((1 - y) * 2 + c) * 2 + i, x) for i in (0, 1)]
        from_d = [(((1 - y) * 2 + c) * 2 + i, 1 - x) for i in (0, 1)]

        def pass_on(slot, sem, device):
            self.go(self.full.at[slot[0], slot[1]], slot, sem, device)

        self.arrived(0)
        pass_on(from_x[0], 4, {"y": 1 - y})
        pass_on(from_x[0], 8, {"core": 1 - c})
        self.arrived(3)
        pass_on(from_y[1], 5, {"x": 1 - x})
        pass_on(from_y[1], 11, {"core": 1 - c})
        self.arrived(1)
        pass_on(from_x[1], 9, {"core": 1 - c})
        self.arrived(2)
        pass_on(from_y[0], 10, {"core": 1 - c})
        self.arrived(4)
        pass_on(from_d[0], 12, {"core": 1 - c})
        self.arrived(5)
        pass_on(from_d[1], 13, {"core": 1 - c})
        for sem in range(6, 14):
            self.arrived(sem)
        for copy in self.started:
            copy.wait_send()


def neighbours():
    y, c, _, x = place()
    return [{"x": 1 - x}, {"y": 1 - y}, {"core": 1 - c}]


def gather_kernel(own, full, send, recv, local):
    y, c, _, x = place()
    meet(neighbours())
    gather = Gather(own, full, send, recv)
    gather.first()
    copies = []
    for i in (0, 1):
        copy = pltpu.make_async_copy(own.at[i], full.at[(y * 2 + c) * 2 + i, x], local.at[i])
        copy.start()
        copies.append(copy)
    gather.rest()
    for copy in copies:
        copy.wait()


def plane_gather(own, collective_id):
    seqs, piece, width = own.shape
    size = 8 * seqs * piece * width * 2
    return pl.pallas_call(
        gather_kernel,
        out_shape=jax.ShapeDtypeStruct((4 * seqs, 2, piece, width), own.dtype),
        in_specs=[ANY],
        out_specs=ANY,
        scratch_shapes=[
            pltpu.SemaphoreType.DMA((14,)),
            pltpu.SemaphoreType.DMA((14,)),
            pltpu.SemaphoreType.DMA((2,)),
        ],
        cost_estimate=pl.CostEstimate(flops=0, bytes_accessed=10 * size, transcendentals=0),
        compiler_params=pltpu.CompilerParams(collective_id=collective_id, has_side_effects=True),
    )(own)


def swap_kernel(count, *refs):
    srcs, dsts, (send, recv, local) = refs[:count], refs[count : 2 * count], refs[2 * count :]
    y, c, _, x = place()
    meet([{"y": flip(y, dy), "core": flip(c, dc), "x": flip(x, dx)} for dy, dc, dx in FLIPS])
    me = (y * 2 + c) * 2 + x
    copies = []
    for k, (src, dst) in enumerate(zip(srcs, dsts)):
        for f, (dy, dc, dx) in enumerate(FLIPS):
            peer = {"y": flip(y, dy), "core": flip(c, dc), "x": flip(x, dx)}
            to = (peer["y"] * 2 + peer["core"]) * 2 + peer["x"]
            copy = remote(src.at[to], dst.at[me], send.at[k, f], recv.at[k, f], peer)
            copy.start()
            copies.append(copy)
        copy = pltpu.make_async_copy(src.at[me], dst.at[me], local.at[k])
        copy.start()
        copies.append(copy)
    for copy in copies:
        copy.wait()


def plane_swap(arrays, collective_id):
    count = len(arrays)
    size = sum(a.size * a.dtype.itemsize for a in arrays)
    return pl.pallas_call(
        functools.partial(swap_kernel, count),
        out_shape=[jax.ShapeDtypeStruct(a.shape, a.dtype) for a in arrays],
        in_specs=[ANY] * count,
        out_specs=[ANY] * count,
        scratch_shapes=[
            pltpu.SemaphoreType.DMA((count, 7)),
            pltpu.SemaphoreType.DMA((count, 7)),
            pltpu.SemaphoreType.DMA((count,)),
        ],
        cost_estimate=pl.CostEstimate(flops=0, bytes_accessed=20 * size, transcendentals=0),
        compiler_params=pltpu.CompilerParams(collective_id=collective_id, has_side_effects=True),
    )(*arrays)


def share_kernel(planes, own, full, line, send, recv, send_z, recv_z, local):
    y, c, z, x = place()
    peers = [{"y": flip(y, dy), "core": flip(c, dc), "x": flip(x, dx)} for dy, dc, dx in FLIPS]
    line_peers = [{"z": lax.rem(z + d, planes)} for d in range(1, planes)]
    meet(peers + line_peers)
    me = (y * 2 + c) * 2 + x
    copies = []
    for d, peer in enumerate(line_peers):
        copy = remote(own, line.at[z], send_z.at[d], recv_z.at[d], peer)
        copy.start()
        copies.append(copy)
    mine = pltpu.make_async_copy(own, line.at[z], local.at[0])
    mine.start()
    for copy in copies:
        copy.wait()
    mine.wait()
    copies = []
    for f, peer in enumerate(peers):
        copy = remote(line, full.at[me], send.at[f], recv.at[f], peer)
        copy.start()
        copies.append(copy)
    mine = pltpu.make_async_copy(line, full.at[me], local.at[1])
    mine.start()
    for copy in copies:
        copy.wait()
    mine.wait()


def share(own, planes, collective_id):
    return pl.pallas_call(
        functools.partial(share_kernel, planes),
        out_shape=jax.ShapeDtypeStruct((8, planes) + own.shape, own.dtype),
        in_specs=[VMEM],
        out_specs=VMEM,
        scratch_shapes=[
            pltpu.VMEM((planes,) + own.shape, own.dtype),
            pltpu.SemaphoreType.DMA((7,)),
            pltpu.SemaphoreType.DMA((7,)),
            pltpu.SemaphoreType.DMA((planes - 1,)),
            pltpu.SemaphoreType.DMA((planes - 1,)),
            pltpu.SemaphoreType.DMA((2,)),
        ],
        compiler_params=pltpu.CompilerParams(collective_id=collective_id, has_side_effects=True),
    )(own)


def scatter_kernel(part, out, held, diag, from_x, from_y, send, recv):
    y, c, _, x = place()
    meet(neighbours())
    copies = []

    def go(src, dst, sem, device):
        copy = remote(src, dst, send.at[sem], recv.at[sem], device)
        copy.start()
        copies.append(copy)
        return copy

    def slot(dy, core, dx, i):
        return ((flip(y, dy) * 2 + core) * 2 + i, flip(x, dx))

    halves = {}
    for n, (dy, dx, i) in enumerate(
        ((1, 1, 0), (1, 1, 1), (0, 1, 1), (1, 0, 0), (0, 1, 0), (1, 0, 1), (0, 0, 0), (0, 0, 1))
    ):
        seq, xx = slot(dy, 1 - c, dx, i)
        halves[dy, dx, i] = go(part.at[seq, xx], held.at[dy, dx, i], n, {"core": 1 - c})

    def add(dy, dx, i, more=None):
        halves[dy, dx, i].wait_recv()
        seq, xx = slot(dy, c, dx, i)
        total = part[seq, xx].astype(F32) + held[dy, dx, i].astype(F32)
        if more is not None:
            total = total + more.astype(F32)
        return total

    def add_keep(dy, dx, i, more=None):
        held[dy, dx, i] = add(dy, dx, i, more).astype(BF16)

    add_keep(1, 1, 0)
    diag_y = go(held.at[1, 1, 0], diag.at[0], 8, {"y": 1 - y})
    add_keep(1, 1, 1)
    diag_x = go(held.at[1, 1, 1], diag.at[1], 9, {"x": 1 - x})
    add_keep(0, 1, 1)
    x_one = go(held.at[0, 1, 1], from_x.at[1], 10, {"x": 1 - x})
    add_keep(1, 0, 0)
    y_zero = go(held.at[1, 0, 0], from_y.at[0], 11, {"y": 1 - y})
    diag_y.wait_recv()
    add_keep(0, 1, 0, diag[0])
    x_zero = go(held.at[0, 1, 0], from_x.at[0], 12, {"x": 1 - x})
    diag_x.wait_recv()
    add_keep(1, 0, 1, diag[1])
    y_one = go(held.at[1, 0, 1], from_y.at[1], 13, {"y": 1 - y})
    for i, (one, two) in enumerate(((x_zero, y_zero), (x_one, y_one))):
        out[i] = add(0, 0, i)
        one.wait_recv()
        two.wait_recv()
        out[i] += from_x[i].astype(F32) + from_y[i].astype(F32)
    for copy in copies:
        copy.wait_send()


def plane_scatter(part, collective_id):
    _, _, piece, width = part.shape
    return pl.pallas_call(
        scatter_kernel,
        out_shape=jax.ShapeDtypeStruct((2, piece, width), F32),
        in_specs=[VMEM],
        out_specs=VMEM,
        scratch_shapes=[
            pltpu.VMEM((2, 2, 2, piece, width), BF16),
            pltpu.VMEM((2, piece, width), BF16),
            pltpu.VMEM((2, piece, width), BF16),
            pltpu.VMEM((2, piece, width), BF16),
            pltpu.SemaphoreType.DMA((14,)),
            pltpu.SemaphoreType.DMA((14,)),
        ],
        cost_estimate=pl.CostEstimate(
            flops=0, bytes_accessed=10 * part.size * 2, transcendentals=0
        ),
        compiler_params=pltpu.CompilerParams(
            collective_id=collective_id, has_side_effects=True, vmem_limit_bytes=40 * 2**20
        ),
    )(part)


def rms_parts(values):
    scale = lax.rsqrt(jnp.mean(values * values, axis=-1, keepdims=True) + 1e-05)
    return (values * scale, scale)


def rms_back(grad_hat, normal, scale):
    return scale * (grad_hat - normal * jnp.mean(grad_hat * normal, axis=-1, keepdims=True))


def times(left, right):
    return jnp.dot(left, right, preferred_element_type=F32)


def times_t(left, right):
    return lax.dot_general(left, right, (((1,), (1,)), ((), ())), preferred_element_type=F32)


def t_times(left, right):
    return lax.dot_general(left, right, (((0,), (0,)), ((), ())), preferred_element_type=F32)


def adamw(weight, first_mom, second_mom, gradient, rate, decay):
    bias_one = 1.0 - 0.9**STEP
    bias_two = 1.0 - 0.95**STEP
    first_new = 0.9 * first_mom + 0.1 * gradient
    second_new = 0.95 * second_mom + 0.05 * gradient * gradient
    direction = first_new / bias_one / (jnp.sqrt(second_new / bias_two) + 1e-08)
    return (second_new, weight - rate * (direction + decay * weight))


def on_device(
    tokens,
    cotangent,
    norm_gains,
    in_proj,
    conv_taps,
    out_proj,
    gate_up,
    down_proj,
    first_gains,
    first_in,
    first_conv,
    first_out,
    first_gate_up,
    first_down,
    second_gains,
    second_in,
    second_conv,
    second_out,
    second_gate_up,
    second_down,
):
    planes = lax.axis_size("z")
    seqs, piece, width = tokens.shape
    rows = seqs * piece
    all_rows = 8 * rows
    own_d = in_proj.shape[0]
    own_f = down_proj.shape[0]
    ff = gate_up.shape[2]
    part_d = width // 8
    part_f = ff // 8

    in_send = in_proj.astype(BF16).reshape(own_d, 3, 4, planes, 2, own_d)
    in_send = in_send.transpose(2, 4, 0, 1, 3, 5).reshape(8, own_d, 3 * part_d)
    gu_send = gate_up.astype(BF16).reshape(2, own_d, 4, planes, 2, own_f)
    gu_send = gu_send.transpose(2, 4, 0, 1, 3, 5).reshape(8, 2, own_d, part_f)
    small = jnp.concatenate([norm_gains, conv_taps], axis=0)
    small_all = share(small, planes, 0)
    in_mine, gu_mine = plane_swap([in_send, gu_send], 1)

    def along_z(value):
        return lax.all_gather(value, "z", axis=0, tiled=False)

    out_t = along_z(out_proj.astype(BF16)).reshape(part_d, width)
    in_t = along_z(in_mine).reshape(planes, 4, 2, own_d, 3 * part_d)
    in_t = in_t.transpose(1, 0, 2, 3, 4).reshape(width, 3 * part_d)
    gu_t = along_z(gu_mine).reshape(planes, 4, 2, 2, own_d, part_f)
    gu_t = gu_t.transpose(3, 1, 0, 2, 4, 5).reshape(2, width, part_f)
    down_t = along_z(down_proj.astype(BF16)).reshape(part_f, width)

    low = small_all.astype(BF16).astype(F32)
    gains = low[:, :, :2].reshape(4, 2, planes, 2, own_d).transpose(3, 0, 2, 1, 4)
    gains = gains.reshape(2, width)
    y, c, z, x = place()
    taps = lax.dynamic_index_in_dim(low[:, :, 2:], (y * 2 + c) * 2 + x, 0, keepdims=False)
    taps = taps.transpose(1, 0, 2).reshape(3, part_d)

    hidden = tokens.astype(F32).reshape(rows, width)
    hat_one, scale_one = rms_parts(hidden)
    normed = (hat_one * gains[0]).astype(BF16).reshape(seqs, piece, width)
    normed_all = plane_gather(normed, 2).reshape(all_rows, width)
    cot_all = plane_gather(cotangent, 3).reshape(all_rows, width)

    projected = times(normed_all, in_t)
    b_part = projected[:, :part_d]
    c_part = projected[:, part_d : 2 * part_d]
    x_part = projected[:, 2 * part_d :]
    count, length = 4 * seqs, 2 * piece
    mixed_in = (b_part * x_part).reshape(count, length, part_d)
    line = [(i, i + 1) for i in range(planes - 1)]
    arrived = lax.ppermute(mixed_in[:, length - 2 :, :], "z", line)
    extended = jnp.concatenate([arrived, mixed_in], axis=1)
    conv_out = (
        taps[0] * extended[:, :length]
        + taps[1] * extended[:, 1 : length + 1]
        + taps[2] * extended[:, 2:]
    )
    conv_out = conv_out.reshape(all_rows, part_d)
    gated = (c_part * conv_out).astype(BF16)

    def blocks(value):
        return value.astype(BF16).reshape(count, 2, piece, width)

    mixer = plane_scatter(blocks(times(gated, out_t)), 4).reshape(rows, width)
    middle = hidden + mixer
    hat_two, scale_two = rms_parts(middle)
    normed_two = (hat_two * gains[1]).astype(BF16).reshape(seqs, piece, width)
    normed_two_all = plane_gather(normed_two, 5).reshape(all_rows, width)
    gate_val = times(normed_two_all, gu_t[0])
    up_val = times(normed_two_all, gu_t[1])
    sigma = jax.nn.sigmoid(gate_val)
    silu_val = gate_val * sigma
    active = (silu_val * up_val).astype(BF16)

    grad_down = t_times(active, cot_all)
    grad_act = times_t(cot_all, down_t)
    dgate = (grad_act * up_val * sigma * (1.0 + gate_val * (1.0 - sigma))).astype(BF16)
    dup = (grad_act * silu_val).astype(BF16)
    grad_gu = jnp.stack([t_times(normed_two_all, dgate), t_times(normed_two_all, dup)])

    def sum_z(value):
        return lax.psum_scatter(value, "z", scatter_dimension=0, tiled=False)

    g_down = sum_z(grad_down.astype(BF16).reshape(planes, own_f, width)).astype(F32)
    grad_gu = grad_gu.astype(BF16).reshape(2, 4, planes, 2, own_d, part_f)
    grad_gu = grad_gu.transpose(2, 1, 3, 0, 4, 5).reshape(planes, 8, 2, own_d, part_f)
    gu_back = sum_z(grad_gu)

    dnorm_two = plane_scatter(blocks(times_t(dgate, gu_t[0]) + times_t(dup, gu_t[1])), 6)
    dnorm_two = dnorm_two.reshape(rows, width)
    gain_grad_two = jnp.sum(dnorm_two * hat_two, axis=0)
    cot_full = cotangent.astype(F32).reshape(rows, width)
    dmiddle = cot_full + rms_back(dnorm_two * gains[1], hat_two, scale_two)
    dmix = dmiddle.astype(BF16).reshape(seqs, piece, width)
    dmix_all = plane_gather(dmix, 7).reshape(all_rows, width)
    branch = plane_scatter(blocks(times(active, down_t)), 8).reshape(rows, width)
    block_out = (middle + branch).astype(BF16)

    grad_out = t_times(gated, dmix_all)
    dgated = times_t(dmix_all, out_t)
    dc_part = dgated * conv_out
    dconv = (dgated * c_part).reshape(count, length, part_d)
    grad_taps = jnp.stack(
        [
            jnp.sum(dconv * extended[:, :length], axis=(0, 1)),
            jnp.sum(dconv * extended[:, 1 : length + 1], axis=(0, 1)),
            jnp.sum(dconv * extended[:, 2:], axis=(0, 1)),
        ]
    )
    grad_ext = (
        taps[0] * jnp.pad(dconv, ((0, 0), (0, 2), (0, 0)))
        + taps[1] * jnp.pad(dconv, ((0, 0), (1, 1), (0, 0)))
        + taps[2] * jnp.pad(dconv, ((0, 0), (2, 0), (0, 0)))
    )
    returned = lax.ppermute(grad_ext[:, :2, :], "z", [(i + 1, i) for i in range(planes - 1)])
    grad_mixed = grad_ext[:, 2:, :] + jnp.pad(returned, ((0, 0), (length - 2, 0), (0, 0)))
    grad_mixed = grad_mixed.reshape(all_rows, part_d)
    dproj = jnp.concatenate([grad_mixed * x_part, dc_part, grad_mixed * b_part], axis=-1)
    dproj = dproj.astype(BF16)
    grad_in = t_times(normed_all, dproj)
    g_out = sum_z(grad_out.astype(BF16).reshape(planes, own_d, width)).astype(F32)
    grad_in = grad_in.astype(BF16).reshape(4, planes, 2, own_d, 3 * part_d)
    grad_in = grad_in.transpose(1, 0, 2, 3, 4).reshape(planes, 8, own_d, 3 * part_d)
    in_back = sum_z(grad_in)
    g_conv = sum_z(grad_taps.reshape(3, planes, own_d).transpose(1, 0, 2))

    dnorm_one = plane_scatter(blocks(times_t(dproj, in_t)), 9).reshape(rows, width)
    gain_grad_one = jnp.sum(dnorm_one * hat_one, axis=0)
    token_grad = dmiddle + rms_back(dnorm_one * gains[0], hat_one, scale_one)
    grad_gains = jnp.stack([gain_grad_one, gain_grad_two])
    g_gains = lax.psum_scatter(
        grad_gains, ("y", "core", "z", "x"), scatter_dimension=1, tiled=True
    )

    in_got, gu_got = plane_swap([in_back, gu_back], 10)
    g_in = in_got.reshape(4, 2, own_d, 3, planes, own_d).transpose(2, 3, 0, 4, 1, 5)
    g_in = g_in.reshape(own_d, 3 * width).astype(F32)
    g_gu = gu_got.reshape(4, 2, 2, own_d, planes, own_f).transpose(2, 3, 0, 4, 1, 5)
    g_gu = g_gu.reshape(2, own_d, ff).astype(F32)

    m_gains, u_gains = adamw(norm_gains, first_gains, second_gains, g_gains, 0.4, 0.0)
    m_in, u_in = adamw(in_proj, first_in, second_in, g_in, 0.02, 0.1)
    m_conv, u_conv = adamw(conv_taps, first_conv, second_conv, g_conv, 0.2, 0.1)
    m_out, u_out = adamw(out_proj, first_out, second_out, g_out, 0.02, 0.1)
    m_gu, u_gu = adamw(gate_up, first_gate_up, second_gate_up, g_gu, 0.02, 0.1)
    m_down, u_down = adamw(down_proj, first_down, second_down, g_down, 0.01, 0.1)
    return (
        block_out.reshape(seqs, piece, width),
        token_grad.reshape(seqs, piece, width),
        g_gains,
        g_in,
        g_conv,
        g_out,
        g_gu,
        g_down,
        m_gains,
        m_in,
        m_conv,
        m_out,
        m_gu,
        m_down,
        u_gains,
        u_in,
        u_conv,
        u_out,
        u_gu,
        u_down,
    )


def solution(mesh):
    lines = mesh.shape["seq"] // 2
    fine = Mesh(mesh.devices.reshape(2, 2, lines, 2), ("y", "core", "z", "x"))
    dp, seq = ("y", "core"), ("z", "x")
    every = dp + seq
    tokens = P(dp, seq, None)
    weights = (
        P(None, every),
        P(every, None),
        P(None, every),
        P(every, None),
        P(None, every, None),
        P(every, None),
    )
    return jax.shard_map(
        on_device,
        mesh=fine,
        in_specs=(tokens, tokens) + weights * 3,
        out_specs=(tokens, tokens) + weights * 3,
        check_vma=False,
    )
```

```python
import functools

import jax
import jax.numpy as jnp
from jax import lax
from jax.experimental import pallas as pl
from jax.experimental.pallas import tpu as pltpu
from jax.sharding import Mesh
from jax.sharding import PartitionSpec as P

STEP = 10
MESH = pl.DeviceIdType.MESH
BF16 = jnp.bfloat16
F32 = jnp.float32
FLIPS = [(dy, dc, dx) for dy in (0, 1) for dc in (0, 1) for dx in (0, 1)][1:]
ANY = pl.BlockSpec(memory_space=pl.ANY)
VMEM = pl.BlockSpec(memory_space=pltpu.VMEM)


def place():
    return tuple(lax.axis_index(a) for a in ("y", "core", "z", "x"))


def flip(value, by):
    return 1 - value if by else value


def remote(src, dst, send, recv, device):
    return pltpu.make_async_remote_copy(
        src_ref=src,
        dst_ref=dst,
        send_sem=send,
        recv_sem=recv,
        device_id=device,
        device_id_type=MESH,
    )


def meet(peers):
    barrier = pltpu.get_barrier_semaphore()
    for peer in peers:
        pl.semaphore_signal(barrier, inc=1, device_id=peer, device_id_type=MESH)
    pl.semaphore_wait(barrier, len(peers))


class Gather:
    def __init__(self, own, full, send, recv, base=0):
        self.own, self.full, self.send, self.recv, self.base = own, full, send, recv, base
        self.started = []

    def go(self, src, slot, sem, device):
        sem = self.base + sem
        copy = remote(
            src, self.full.at[slot[0], slot[1]], self.send.at[sem], self.recv.at[sem], device
        )
        copy.start()
        self.started.append(copy)

    def first(self):
        y, c, _, x = place()
        me = (y * 2 + x) * 2 + c
        for i, j in ((0, 1), (1, 0)):
            self.go(self.own.at[i], (me, i), i, {"x": 1 - x})
            self.go(self.own.at[j], (me, j), 2 + j, {"y": 1 - y})
        for i in (0, 1):
            self.go(self.own.at[i], (me, i), 6 + i, {"core": 1 - c})

    def arrived(self, *sems):
        for sem in sems:
            done = self.recv.at[self.base + sem]
            pltpu.make_async_copy(self.own.at[0], self.own.at[0], done).wait()

    def pass_on(self, dy, dx, i, sem, device):
        y, c, _, x = place()
        slot = ((flip(y, dy) * 2 + flip(x, dx)) * 2 + c, i)
        self.go(self.full.at[slot[0], slot[1]], slot, sem, device)

    def forward(self):
        y, c, _, x = place()
        self.arrived(0)
        self.pass_on(0, 1, 0, 4, {"y": 1 - y})
        self.pass_on(0, 1, 0, 8, {"core": 1 - c})
        self.arrived(3)
        self.pass_on(1, 0, 1, 5, {"x": 1 - x})
        self.pass_on(1, 0, 1, 11, {"core": 1 - c})

    def second(self):
        _, c, _, _ = place()
        self.arrived(1)
        self.pass_on(0, 1, 1, 9, {"core": 1 - c})
        self.arrived(2)
        self.pass_on(1, 0, 0, 10, {"core": 1 - c})

    def last(self):
        _, c, _, _ = place()
        self.arrived(4)
        self.pass_on(1, 1, 0, 12, {"core": 1 - c})
        self.arrived(5)
        self.pass_on(1, 1, 1, 13, {"core": 1 - c})

    def sent(self):
        for copy in self.started:
            copy.wait_send()


def neighbours():
    y, c, _, x = place()
    return [{"x": 1 - x}, {"y": 1 - y}, {"core": 1 - c}]


def others():
    y, c, _, x = place()
    return [{"y": flip(y, dy), "core": flip(c, dc), "x": flip(x, dx)} for dy, dc, dx in FLIPS]


def swap(src, dst, send, recv, local):
    y, c, _, x = place()
    me = (y * 2 + c) * 2 + x
    copies = []
    for f, peer in enumerate(others()):
        to = (peer["y"] * 2 + peer["core"]) * 2 + peer["x"]
        copies.append(remote(src.at[to], dst.at[me], send.at[f], recv.at[f], peer))
    copies.append(pltpu.make_async_copy(src.at[me], dst.at[me], local))
    for copy in copies:
        copy.start()
    return copies


def along_line(planes, own, full, send, recv, local):
    z = lax.axis_index("z")
    copies = [
        remote(own, full.at[z], send.at[d], recv.at[d], peer)
        for d, peer in enumerate(line_peers(planes))
    ]
    copies.append(pltpu.make_async_copy(own, full.at[z], local))
    for copy in copies:
        copy.start()
    return copies


def line_peers(planes):
    return [{"z": lax.rem(lax.axis_index("z") + d, planes)} for d in range(1, planes)]


def gather_kernel(own, full, send, recv, local):
    y, c, _, x = place()
    meet(neighbours())
    gather = Gather(own, full, send, recv)
    gather.first()
    mine = pltpu.make_async_copy(own, full.at[(y * 2 + x) * 2 + c], local)
    mine.start()
    gather.forward()
    gather.second()
    gather.last()
    gather.arrived(*range(6, 14))
    gather.sent()
    mine.wait()


def early_kernel(
    planes,
    own,
    block,
    out,
    full,
    got,
    outs,
    send,
    recv,
    send_s,
    recv_s,
    send_z,
    recv_z,
    local,
):
    y, c, _, x = place()
    meet(others() + line_peers(planes))
    copies = along_line(planes, out, outs, send_z, recv_z, local.at[0])
    gather = Gather(own, full, send, recv)
    gather.first()
    mine = pltpu.make_async_copy(own, full.at[(y * 2 + x) * 2 + c], local.at[1])
    mine.start()
    copies += [mine] + swap(block, got, send_s, recv_s, local.at[2])
    gather.forward()
    gather.second()
    gather.last()
    gather.arrived(*range(6, 14))
    gather.sent()
    for copy in copies:
        copy.wait()


def params(collective_id, vmem=0):
    more = {"vmem_limit_bytes": vmem * 2**20} if vmem else {}
    return pltpu.CompilerParams(collective_id=collective_id, has_side_effects=True, **more)


def cost(micros):
    return pl.CostEstimate(flops=int(micros * 1e9), bytes_accessed=0, transcendentals=0)


def sems(*shape):
    return pltpu.SemaphoreType.DMA(shape)


def plane_gather(own, collective_id):
    return pl.pallas_call(
        gather_kernel,
        out_shape=jax.ShapeDtypeStruct((8,) + own.shape, own.dtype),
        in_specs=[ANY],
        out_specs=ANY,
        scratch_shapes=[sems(14), sems(14), pltpu.SemaphoreType.DMA],
        cost_estimate=cost(45),
        compiler_params=params(collective_id),
    )(own)


def early(planes, own, block, out, collective_id):
    return pl.pallas_call(
        functools.partial(early_kernel, planes),
        out_shape=[
            jax.ShapeDtypeStruct((8,) + own.shape, own.dtype),
            jax.ShapeDtypeStruct(block.shape, block.dtype),
            jax.ShapeDtypeStruct((planes,) + out.shape, out.dtype),
        ],
        in_specs=[ANY] * 3,
        out_specs=[ANY] * 3,
        scratch_shapes=[
            sems(14), sems(14), sems(7), sems(7), sems(planes - 1), sems(planes - 1), sems(3)
        ],
        cost_estimate=cost(65),
        compiler_params=params(collective_id),
    )(own, block, out)


def finish_kernel(planes, ins, gus, gains, taps, outs, ins_got, gus_got, sums, out_sum, *scratch):
    parts, terms, got, outs_got, send, recv, send_g, recv_g = scratch[:8]
    send_z, recv_z, send_o, recv_o, local = scratch[8:]
    meet(others() + line_peers(planes))
    small = swap(gains, parts, send_g, recv_g, local.at[0])
    large = scatter_line(planes, outs, outs_got, send_o, recv_o, local.at[3])
    copies = swap(ins, ins_got, send.at[0], recv.at[0], local.at[1])
    copies += swap(gus, gus_got, send.at[1], recv.at[1], local.at[2])
    for copy in small:
        copy.wait()
    terms[:, 0:2, :] = jnp.sum(parts[...], axis=0)
    terms[:, 2:5, :] = taps[...]
    for copy in scatter_line(planes, terms, got, send_z, recv_z, local.at[0]):
        copy.wait()
    sums[...] = jnp.sum(got[...], axis=0)
    for copy in large:
        copy.wait()
    total = outs_got[0].astype(F32)
    for k in range(1, planes):
        total += outs_got[k].astype(F32)
    out_sum[...] = total
    for copy in copies:
        copy.wait()


def scatter_line(planes, terms, got, send, recv, local):
    z = lax.axis_index("z")
    copies = [
        remote(terms.at[peer["z"]], got.at[z], send.at[d], recv.at[d], peer)
        for d, peer in enumerate(line_peers(planes))
    ]
    copies.append(pltpu.make_async_copy(terms.at[z], got.at[z], local))
    for copy in copies:
        copy.start()
    return copies


def finish(planes, ins, gus, gains, taps, outs, collective_id):
    own = gains.shape[-1]
    return pl.pallas_call(
        functools.partial(finish_kernel, planes),
        out_shape=[
            jax.ShapeDtypeStruct(ins.shape, ins.dtype),
            jax.ShapeDtypeStruct(gus.shape, gus.dtype),
            jax.ShapeDtypeStruct((5, own), F32),
            jax.ShapeDtypeStruct(outs.shape[1:], F32),
        ],
        in_specs=[ANY, ANY, VMEM, VMEM, VMEM],
        out_specs=[ANY, ANY, VMEM, VMEM],
        scratch_shapes=[
            pltpu.VMEM(gains.shape, F32),
            pltpu.VMEM((planes, 5, own), F32),
            pltpu.VMEM((planes, 5, own), F32),
            pltpu.VMEM(outs.shape, BF16),
            sems(2, 7),
            sems(2, 7),
            sems(7),
            sems(7),
            sems(planes - 1),
            sems(planes - 1),
            sems(planes - 1),
            sems(planes - 1),
            sems(4),
        ],
        cost_estimate=cost(25),
        compiler_params=params(collective_id),
    )(ins, gus, gains, taps, outs)


def share_kernel(
    planes, own, block, full, got, line, send, recv, send_z, recv_z, local, send_s, recv_s
):
    y, c, _, x = place()
    meet(others() + line_peers(planes))
    me = (y * 2 + c) * 2 + x
    copies = along_line(planes, own, line, send_z, recv_z, local.at[0])
    swapped = swap(block, got, send_s, recv_s, local.at[1])
    for copy in copies:
        copy.wait()
    copies = []
    for f, peer in enumerate(others()):
        copy = remote(line, full.at[me], send.at[f], recv.at[f], peer)
        copy.start()
        copies.append(copy)
    mine = pltpu.make_async_copy(line, full.at[me], local.at[0])
    mine.start()
    for copy in copies + swapped:
        copy.wait()
    mine.wait()


def share(own, block, planes, collective_id):
    return pl.pallas_call(
        functools.partial(share_kernel, planes),
        out_shape=[
            jax.ShapeDtypeStruct((8, planes) + own.shape, own.dtype),
            jax.ShapeDtypeStruct(block.shape, block.dtype),
        ],
        in_specs=[VMEM, ANY],
        out_specs=[VMEM, ANY],
        scratch_shapes=[
            pltpu.VMEM((planes,) + own.shape, own.dtype),
            pltpu.SemaphoreType.DMA((7,)),
            pltpu.SemaphoreType.DMA((7,)),
            pltpu.SemaphoreType.DMA((planes - 1,)),
            pltpu.SemaphoreType.DMA((planes - 1,)),
            pltpu.SemaphoreType.DMA((2,)),
            pltpu.SemaphoreType.DMA((7,)),
            pltpu.SemaphoreType.DMA((7,)),
        ],
        cost_estimate=cost(12),
        compiler_params=params(collective_id),
    )(own, block)


def load_rows(planes, gathered, rows, sem):
    if len(gathered.shape) == 3:
        copy = pltpu.make_async_copy(gathered, rows, sem)
        copy.start()
        return [copy]
    own = gathered.shape[3]
    copies = []
    for z in range(planes):
        for m in range(8):
            start = (((m // 2) * planes + z) * 2 + m % 2) * own
            for j in (0, 1):
                src = gathered.at[z, m, j]
                copies.append(pltpu.make_async_copy(src, rows.at[j, pl.ds(start, own)], sem))
    for copy in copies:
        copy.start()
    return copies


def ffn_kernel(
    planes,
    cot,
    normed,
    gathered,
    down,
    act_out,
    dgate_out,
    dup_out,
    grad_out,
    full,
    near,
    weights,
    gates,
    ups,
    staged,
    total,
    send,
    recv,
    local,
    near_sem,
    out_sem,
):
    y, c, _, x = place()
    piece, width = cot.shape[1:]
    part = down.shape[0]
    chip_rows = 4 * piece
    half = 2 * piece
    chips = [flip(y, dy) * 2 + flip(x, dx) for dy, dx in ((0, 0), (0, 1), (1, 0), (1, 1))]
    loads = load_rows(planes, gathered, weights, local.at[0])
    mine = pltpu.make_async_copy(cot, full.at[(y * 2 + x) * 2 + c], local.at[1])
    mine.start()

    def fetch(k):
        copy = pltpu.make_async_copy(
            normed.at[pl.ds(chips[k] * 2, 2)], near.at[k % 2], near_sem.at[k % 2]
        )
        copy.start()
        return copy

    fetched = {0: fetch(0), 1: fetch(1)}
    meet(neighbours())
    gather = Gather(cot, full, send, recv)
    gather.first()
    for copy in loads:
        copy.wait()

    def gate_up(k, slot):
        fetched[k].wait()

        def body(i, _):
            rows = pl.ds(pl.multiple_of(i * half, half), half)
            left = near[k % 2, i].reshape(half, width)
            gates[slot, rows, :] = times(left, weights[0])
            ups[slot, rows, :] = times(left, weights[1])
            return 0

        lax.fori_loop(0, 2, body, 0)
        if k + 2 < 4:
            fetched[k + 2] = fetch(k + 2)

    written = {}

    def back(k, slot):
        if k >= 2:
            for copy in written[k - 2]:
                copy.wait()
        room = staged.at[k % 2]

        def body(i, _):
            rows = pl.ds(pl.multiple_of(i * half, half), half)
            grad = times_t(full[chips[k] * 2 + i].reshape(half, width), down[...])
            gate, up = gates[slot, rows, :], ups[slot, rows, :]
            sigma = jax.nn.sigmoid(gate)
            silu = gate * sigma
            room[0, i] = (silu * up).astype(BF16).reshape(2, piece, part)
            dgate = grad * up * sigma * (1.0 + gate * (1.0 - sigma))
            room[1, i] = dgate.astype(BF16).reshape(2, piece, part)
            room[2, i] = (grad * silu).astype(BF16).reshape(2, piece, part)
            return 0

        lax.fori_loop(0, 2, body, 0)
        written[k] = []
        for n, out in enumerate((act_out, dgate_out, dup_out)):
            copy = pltpu.make_async_copy(
                room.at[n], out.at[pl.ds(chips[k] * 2, 2)], out_sem.at[k % 2, n]
            )
            copy.start()
            written[k].append(copy)
        active = room[0].reshape(chip_rows, part)
        tile = width // 3

        def sum_up(n, _):
            columns = pl.ds(pl.multiple_of(n * tile, tile), tile)
            right = full[pl.ds(chips[k] * 2, 2), :, :, columns].reshape(chip_rows, tile)
            product = t_times(active, right)
            if k == 0:
                total[:, columns] = product
            elif k < 3:
                total[:, columns] += product
            else:
                product = total[:, columns] + product
                own = part // planes
                for z in range(planes):
                    grad_out[z, :, columns] = product[z * own : (z + 1) * own].astype(BF16)
            return 0

        lax.fori_loop(0, 3, sum_up, 0)

    gate_up(0, 0)
    mine.wait()
    gather.arrived(6, 7)
    back(0, 0)
    gather.forward()
    gate_up(1, 0)
    gate_up(2, 1)
    gather.second()
    gather.arrived(8, 9)
    back(1, 0)
    gate_up(3, 0)
    gather.arrived(10, 11)
    back(2, 1)
    gather.last()
    gather.arrived(12, 13)
    back(3, 0)
    gather.sent()
    for k in (2, 3):
        for copy in written[k]:
            copy.wait()


def ffn(planes, cot, normed, gathered, down, collective_id):
    _, piece, width = cot.shape
    part = down.shape[0]
    wide = jax.ShapeDtypeStruct((8, 2, piece, part), BF16)
    return pl.pallas_call(
        functools.partial(ffn_kernel, planes),
        out_shape=[wide, wide, wide, jax.ShapeDtypeStruct((planes, part // planes, width), BF16)],
        in_specs=[ANY, ANY, ANY, VMEM],
        out_specs=[ANY, ANY, ANY, VMEM],
        scratch_shapes=[
            pltpu.VMEM((8, 2, piece, width), BF16),
            pltpu.VMEM((2, 2, 2, piece, width), BF16),
            pltpu.VMEM((2, width, part), BF16),
            pltpu.VMEM((2, 4 * piece, part), F32),
            pltpu.VMEM((2, 4 * piece, part), F32),
            pltpu.VMEM((2, 3, 2, 2, piece, part), BF16),
            pltpu.VMEM((part, width), F32),
            pltpu.SemaphoreType.DMA((14,)),
            pltpu.SemaphoreType.DMA((14,)),
            pltpu.SemaphoreType.DMA((2,)),
            pltpu.SemaphoreType.DMA((2,)),
            pltpu.SemaphoreType.DMA((2, 3)),
        ],
        cost_estimate=cost(55),
        compiler_params=params(collective_id, 60),
    )(cot, normed, gathered, down)


def scatter_kernel(planes, pairs, transposed, with_grads, *refs):
    refs = list(refs)
    lefts = [refs.pop(0) for _ in range(pairs)]
    if with_grads:
        gathered, normed = refs.pop(0), refs.pop(0)
        out, grads = refs.pop(0), refs.pop(0)
    else:
        rights = [refs.pop(0) for _ in range(pairs)]
        out = refs.pop(0)
    staged, held, ready, keep, diag, from_x, from_y, send, recv = refs[:9]
    if with_grads:
        weights, every, local = refs[9:]
        rights = [weights.at[j] for j in range(pairs)]
        loads = load_rows(planes, gathered, weights, local.at[0])
        whole = pltpu.make_async_copy(normed, every, local.at[1])
        whole.start()
    y, c, _, x = place()
    _, piece, width = out.shape
    rows = 2 * piece
    tile = width // 3
    meet(neighbours())
    if with_grads:
        for copy in loads:
            copy.wait()
    copies = []

    def go(src, dst, sem, device):
        copy = remote(src, dst, send.at[sem], recv.at[sem], device)
        copy.start()
        copies.append(copy)
        return copy

    def product(dy, dx, core, store):
        member = (flip(y, dy) * 2 + flip(x, dx)) * 2 + core

        def body(n, _):
            columns = pl.ds(pl.multiple_of(n * tile, tile), tile)
            value = None
            for left, right in zip(lefts, rights):
                a = left[member].reshape(rows, left.shape[-1])
                if transposed:
                    term = times_t(a, right[columns, :])
                else:
                    term = times(a, right[:, columns])
                value = term if value is None else value + term
            store(columns, value.reshape(2, piece, tile))
            return 0

        lax.fori_loop(0, 3, body, 0)

    order = ((1, 1), (0, 1), (1, 0), (0, 0))
    over = []

    def to_other_core(n):
        dy, dx = order[n]

        def store(columns, value):
            staged[n, :, :, columns] = value.astype(BF16)

        product(dy, dx, 1 - c, store)
        over.append(go(staged.at[n], held.at[n], n, {"core": 1 - c}))

    def own_core(n, store):
        dy, dx = order[n]
        over[n].wait_recv()

        def add(columns, value):
            store(columns, value + held[n, :, :, columns].astype(F32))

        product(dy, dx, c, add)

    def store_diag(columns, value):
        ready[0, :, :, columns] = value.astype(BF16)

    def store_x(columns, value):
        ready[1, 1, :, columns] = value[1].astype(BF16)
        keep[0, :, columns] = value[0]

    def store_y(columns, value):
        ready[2, 0, :, columns] = value[0].astype(BF16)
        keep[1, :, columns] = value[1]

    def store_own(columns, value):
        out[:, :, columns] = value

    to_other_core(0)
    to_other_core(1)
    own_core(0, store_diag)
    diag_y = go(ready.at[0, 0], diag.at[0], 4, {"y": 1 - y})
    diag_x = go(ready.at[0, 1], diag.at[1], 5, {"x": 1 - x})
    to_other_core(2)
    own_core(1, store_x)
    x_one = go(ready.at[1, 1], from_x.at[1], 6, {"x": 1 - x})
    own_core(2, store_y)
    y_zero = go(ready.at[2, 0], from_y.at[0], 7, {"y": 1 - y})
    to_other_core(3)
    own_core(3, store_own)

    quarter = width // 4

    def gradient(j):
        own = grads.shape[-2]

        def body(q, _):
            columns = pl.ds(pl.multiple_of(q * quarter, quarter), quarter)
            left = every[:, :, :, columns].reshape(8 * rows, quarter)
            right = lefts[j][...].reshape(8 * rows, lefts[j].shape[-1])
            value = t_times(left, right).astype(BF16)
            if len(grads.shape) == 3:
                grads[j, columns, :] = value
                return 0
            for z in range(planes):
                for xx in (0, 1):
                    start = (z * 2 + xx) * own
                    grads[z, q * 2 + xx, j] = value[start : start + own]
            return 0

        lax.fori_loop(0, 4, body, 0)

    if with_grads:
        whole.wait()
        gradient(0)
    diag_y.wait_recv()
    ready[1, 0] = (keep[0] + diag[0].astype(F32)).astype(BF16)
    x_zero = go(ready.at[1, 0], from_x.at[0], 8, {"x": 1 - x})
    diag_x.wait_recv()
    ready[2, 1] = (keep[1] + diag[1].astype(F32)).astype(BF16)
    y_one = go(ready.at[2, 1], from_y.at[1], 9, {"y": 1 - y})
    if with_grads:
        gradient(1)
    for i, (one, two) in enumerate(((x_zero, y_zero), (x_one, y_one))):
        one.wait_recv()
        two.wait_recv()
        out[i] += from_x[i].astype(F32) + from_y[i].astype(F32)
    for copy in copies:
        copy.wait_send()


def plane_scatter(lefts, rights, transposed, collective_id, gathered=None, normed=None):
    piece = lefts[0].shape[2]
    with_grads = gathered is not None
    if with_grads:
        planes, part = gathered.shape[0], gathered.shape[-1]
        width = normed.shape[3]
        operands = [*lefts, gathered, normed]
        in_specs = [VMEM] * len(lefts) + [ANY, ANY]
    else:
        planes = 0
        width = rights[0].shape[0 if transposed else 1]
        operands = [*lefts, *rights]
        in_specs = [VMEM] * len(operands)
    out_shape = [jax.ShapeDtypeStruct((2, piece, width), F32)]
    scratch = [
        pltpu.VMEM((4, 2, piece, width), BF16),
        pltpu.VMEM((4, 2, piece, width), BF16),
        pltpu.VMEM((3, 2, piece, width), BF16),
        pltpu.VMEM((2, piece, width), F32),
        pltpu.VMEM((2, piece, width), BF16),
        pltpu.VMEM((2, piece, width), BF16),
        pltpu.VMEM((2, piece, width), BF16),
        pltpu.SemaphoreType.DMA((10,)),
        pltpu.SemaphoreType.DMA((10,)),
    ]
    if with_grads:
        out_shape.append(jax.ShapeDtypeStruct(gathered.shape, BF16))
        scratch += [
            pltpu.VMEM((2, width, part), BF16),
            pltpu.VMEM((8, 2, piece, width), BF16),
            pltpu.SemaphoreType.DMA((2,)),
        ]
    got = pl.pallas_call(
        functools.partial(scatter_kernel, planes, len(lefts), transposed, with_grads),
        out_shape=out_shape,
        in_specs=in_specs,
        out_specs=[VMEM] * len(out_shape),
        scratch_shapes=scratch,
        cost_estimate=cost(55 if with_grads else 48),
        compiler_params=params(collective_id, 60 if with_grads else 44),
    )(*operands)
    return got if with_grads else got[0]


def rms_parts(values):
    scale = lax.rsqrt(jnp.mean(values * values, axis=-1, keepdims=True) + 1e-05)
    return (values * scale, scale)


def rms_back(grad_hat, normal, scale):
    return scale * (grad_hat - normal * jnp.mean(grad_hat * normal, axis=-1, keepdims=True))


def times(left, right):
    return jnp.dot(left, right, preferred_element_type=F32)


def times_t(left, right):
    return lax.dot_general(left, right, (((1,), (1,)), ((), ())), preferred_element_type=F32)


def t_times(left, right):
    return lax.dot_general(left, right, (((0,), (0,)), ((), ())), preferred_element_type=F32)


def adamw(weight, first_mom, second_mom, gradient, rate, decay):
    bias_one = 1.0 - 0.9**STEP
    bias_two = 1.0 - 0.95**STEP
    first_new = 0.9 * first_mom + 0.1 * gradient
    second_new = 0.95 * second_mom + 0.05 * gradient * gradient
    direction = first_new / bias_one / (jnp.sqrt(second_new / bias_two) + 1e-08)
    return (second_new, weight - rate * (direction + decay * weight))


def on_device(
    tokens,
    cotangent,
    norm_gains,
    in_proj,
    conv_taps,
    out_proj,
    gate_up,
    down_proj,
    first_gains,
    first_in,
    first_conv,
    first_out,
    first_gate_up,
    first_down,
    second_gains,
    second_in,
    second_conv,
    second_out,
    second_gate_up,
    second_down,
):
    planes = lax.axis_size("z")
    seqs, piece, width = tokens.shape
    rows = seqs * piece
    all_rows = 8 * rows
    own_d = in_proj.shape[0]
    own_f = down_proj.shape[0]
    ff = gate_up.shape[2]
    part_d = width // 8
    part_f = ff // 8

    in_send = in_proj.astype(BF16).reshape(own_d, 3, 4, planes, 2, own_d)
    in_send = in_send.transpose(2, 4, 0, 1, 3, 5).reshape(8, own_d, 3 * part_d)
    gu_send = gate_up.astype(BF16).reshape(2, own_d, 4, planes, 2, own_f)
    gu_send = gu_send.transpose(2, 4, 0, 1, 3, 5).reshape(8, 2, own_d, part_f)
    small = jnp.concatenate([norm_gains, conv_taps], axis=0)
    small_all, in_mine = share(small, in_send, planes, 0)

    def along_z(value):
        return lax.all_gather(value, "z", axis=0, tiled=False)

    in_t = along_z(in_mine).reshape(planes, 4, 2, own_d, 3 * part_d)
    in_t = in_t.transpose(1, 0, 2, 3, 4).reshape(width, 3 * part_d)
    down_t = along_z(down_proj.astype(BF16)).reshape(part_f, width)

    low = small_all.astype(BF16).astype(F32)
    gains = low[:, :, :2].reshape(4, 2, planes, 2, own_d).transpose(3, 0, 2, 1, 4)
    gains = gains.reshape(2, width)
    y, c, z, x = place()
    taps = lax.dynamic_index_in_dim(low[:, :, 2:], (y * 2 + c) * 2 + x, 0, keepdims=False)
    taps = taps.transpose(1, 0, 2).reshape(3, part_d)

    hidden = tokens.astype(F32).reshape(rows, width)
    hat_one, scale_one = rms_parts(hidden)
    normed = (hat_one * gains[0]).astype(BF16).reshape(seqs, piece, width)
    normed_all, gu_mine, out_t = early(planes, normed, gu_send, out_proj.astype(BF16), 1)
    normed_all = normed_all.reshape(all_rows, width)
    out_t = out_t.reshape(part_d, width)
    gu_t = along_z(gu_mine)
    in_tiles = own_d % 16 == 0
    if not in_tiles:
        gu_t = gu_t.reshape(planes, 4, 2, 2, own_d, part_f).transpose(3, 1, 0, 2, 4, 5)
        gu_t = gu_t.reshape(2, width, part_f)

    projected = times(normed_all, in_t)
    b_part = projected[:, :part_d]
    c_part = projected[:, part_d : 2 * part_d]
    x_part = projected[:, 2 * part_d :]
    lay = (2, 2, 2, seqs, piece, part_d)
    mixed_in = (b_part * x_part).reshape(lay)
    ends = mixed_in[..., piece - 2 :, :]
    before = lax.ppermute(ends[:, 1], "z", [(i, i + 1) for i in range(planes - 1)])
    arrived = jnp.stack([before, ends[:, 0]], axis=1)
    extended = jnp.concatenate([arrived, mixed_in], axis=-2)
    conv_out = (
        taps[0] * extended[..., :piece, :]
        + taps[1] * extended[..., 1 : piece + 1, :]
        + taps[2] * extended[..., 2:, :]
    )
    conv_out = conv_out.reshape(all_rows, part_d)
    gated = (c_part * conv_out).astype(BF16)

    def members(value):
        return value.reshape(8, seqs, piece, value.shape[-1])

    mixer = plane_scatter([members(gated)], [out_t], False, 2).reshape(rows, width)
    middle = hidden + mixer
    hat_two, scale_two = rms_parts(middle)
    normed_two = (hat_two * gains[1]).astype(BF16).reshape(seqs, piece, width)
    normed_two_all = plane_gather(normed_two, 3)
    active, dgate, dup, grad_down = ffn(planes, cotangent, normed_two_all, gu_t, down_t, 4)

    def sum_z(value):
        return lax.psum_scatter(value, "z", scatter_dimension=0, tiled=False)

    g_down = sum_z(grad_down)
    dnorm_two, grad_gu = plane_scatter([dgate, dup], None, True, 5, gu_t, normed_two_all)
    if not in_tiles:
        grad_gu = grad_gu.reshape(2, 4, planes, 2, own_d, part_f).transpose(2, 1, 3, 0, 4, 5)
        grad_gu = grad_gu.reshape(planes, 8, 2, own_d, part_f)
    grad_gu, g_down = lax.optimization_barrier((grad_gu, g_down))
    g_down = g_down.astype(F32)
    gu_back = sum_z(grad_gu)

    dnorm_two = dnorm_two.reshape(rows, width)
    gain_grad_two = jnp.sum(dnorm_two * hat_two, axis=0)
    cot_full = cotangent.astype(F32).reshape(rows, width)
    dmiddle = cot_full + rms_back(dnorm_two * gains[1], hat_two, scale_two)
    dmix = dmiddle.astype(BF16).reshape(seqs, piece, width)
    dmix_all = plane_gather(dmix, 6).reshape(all_rows, width)

    grad_out = t_times(gated, dmix_all)
    dgated = times_t(dmix_all, out_t)
    dc_part = dgated * conv_out
    dconv = (dgated * c_part).reshape(lay)
    grad_taps = jnp.stack(
        [
            jnp.sum(dconv * extended[..., k : piece + k, :], axis=(0, 1, 2, 3, 4))
            for k in range(3)
        ]
    )

    def padded(before, after):
        return jnp.pad(dconv, [(0, 0)] * 4 + [(before, after), (0, 0)])

    grad_ext = taps[0] * padded(0, 2) + taps[1] * padded(1, 1) + taps[2] * padded(2, 0)
    starts = grad_ext[..., :2, :]
    after = lax.ppermute(starts[:, 0], "z", [(i + 1, i) for i in range(planes - 1)])
    returned = jnp.stack([starts[:, 1], after], axis=1)
    returned = jnp.pad(returned, [(0, 0)] * 4 + [(piece - 2, 0), (0, 0)])
    grad_mixed = (grad_ext[..., 2:, :] + returned).reshape(all_rows, part_d)
    dproj = jnp.concatenate([grad_mixed * x_part, dc_part, grad_mixed * b_part], axis=-1)
    dproj = dproj.astype(BF16)
    grad_in = t_times(normed_all, dproj).astype(BF16)
    grad_in = grad_in.reshape(4, planes, 2, own_d, 3 * part_d).transpose(1, 0, 2, 3, 4)
    grad_in = grad_in.reshape(planes, 8, own_d, 3 * part_d)
    grad_out = grad_out.astype(BF16).reshape(planes, own_d, width)
    grad_in, gu_back, dproj = lax.optimization_barrier((grad_in, gu_back, dproj))
    in_back = sum_z(grad_in)
    taps_parts = grad_taps.reshape(3, planes, own_d).transpose(1, 0, 2)

    dnorm_one = plane_scatter([members(dproj)], [in_t], True, 7).reshape(rows, width)
    gain_grad_one = jnp.sum(dnorm_one * hat_one, axis=0)
    token_grad = dmiddle + rms_back(dnorm_one * gains[0], hat_one, scale_one)
    active, token_grad = lax.optimization_barrier((active, token_grad))
    branch = plane_scatter([active], [down_t], False, 8).reshape(rows, width)
    block_out = (middle + branch).astype(BF16)
    grad_gains = jnp.stack([gain_grad_one, gain_grad_two])
    gains_parts = grad_gains.reshape(2, 4, planes, 2, own_d).transpose(1, 3, 2, 0, 4)
    gains_parts = gains_parts.reshape(8, planes, 2, own_d)
    in_got, gu_got, sums, g_out = finish(
        planes, in_back, gu_back, gains_parts, taps_parts, grad_out, 9
    )
    g_gains, g_conv = sums[:2], sums[2:]
    g_in = in_got.reshape(4, 2, own_d, 3, planes, own_d).transpose(2, 3, 0, 4, 1, 5)
    g_in = g_in.reshape(own_d, 3 * width).astype(F32)
    g_gu = gu_got.reshape(4, 2, 2, own_d, planes, own_f).transpose(2, 3, 0, 4, 1, 5)
    g_gu = g_gu.reshape(2, own_d, ff).astype(F32)

    m_gains, u_gains = adamw(norm_gains, first_gains, second_gains, g_gains, 0.4, 0.0)
    m_in, u_in = adamw(in_proj, first_in, second_in, g_in, 0.02, 0.1)
    m_conv, u_conv = adamw(conv_taps, first_conv, second_conv, g_conv, 0.2, 0.1)
    m_out, u_out = adamw(out_proj, first_out, second_out, g_out, 0.02, 0.1)
    m_gu, u_gu = adamw(gate_up, first_gate_up, second_gate_up, g_gu, 0.02, 0.1)
    m_down, u_down = adamw(down_proj, first_down, second_down, g_down, 0.01, 0.1)
    return (
        block_out.reshape(seqs, piece, width),
        token_grad.reshape(seqs, piece, width),
        g_gains,
        g_in,
        g_conv,
        g_out,
        g_gu,
        g_down,
        m_gains,
        m_in,
        m_conv,
        m_out,
        m_gu,
        m_down,
        u_gains,
        u_in,
        u_conv,
        u_out,
        u_gu,
        u_down,
    )


def solution(mesh):
    lines = mesh.shape["seq"] // 2
    fine = Mesh(mesh.devices.reshape(2, 2, lines, 2), ("y", "core", "z", "x"))
    dp, seq = ("y", "core"), ("z", "x")
    every = dp + seq
    tokens = P(dp, seq, None)
    weights = (
        P(None, every),
        P(every, None),
        P(None, every),
        P(every, None),
        P(None, every, None),
        P(every, None),
    )
    return jax.shard_map(
        on_device,
        mesh=fine,
        in_specs=(tokens, tokens) + weights * 3,
        out_specs=(tokens, tokens) + weights * 3,
        check_vma=False,
    )
```

```python
import functools

import jax
import jax.numpy as jnp
from jax import lax
from jax.experimental import pallas as pl
from jax.experimental.pallas import tpu as pltpu
from jax.sharding import Mesh
from jax.sharding import PartitionSpec as P

STEP = 10
MESH = pl.DeviceIdType.MESH
BF16 = jnp.bfloat16
F32 = jnp.float32
FLIPS = [(dy, dc, dx) for dy in (0, 1) for dc in (0, 1) for dx in (0, 1)][1:]
ANY = pl.BlockSpec(memory_space=pl.ANY)
VMEM = pl.BlockSpec(memory_space=pltpu.VMEM)


def place():
    return tuple(lax.axis_index(a) for a in ("y", "core", "z", "x"))


def flip(value, by):
    return 1 - value if by else value


def remote(src, dst, send, recv, device):
    return pltpu.make_async_remote_copy(
        src_ref=src,
        dst_ref=dst,
        send_sem=send,
        recv_sem=recv,
        device_id=device,
        device_id_type=MESH,
    )


def meet(peers):
    barrier = pltpu.get_barrier_semaphore()
    for peer in peers:
        pl.semaphore_signal(barrier, inc=1, device_id=peer, device_id_type=MESH)
    pl.semaphore_wait(barrier, len(peers))


class Gather:
    def __init__(self, own, full, send, recv, base=0):
        self.own, self.full, self.send, self.recv, self.base = own, full, send, recv, base
        self.started = []

    def go(self, src, slot, sem, device):
        sem = self.base + sem
        copy = remote(
            src, self.full.at[slot[0], slot[1]], self.send.at[sem], self.recv.at[sem], device
        )
        copy.start()
        self.started.append(copy)

    def first(self):
        y, c, _, x = place()
        me = (y * 2 + x) * 2 + c
        for i, j in ((0, 1), (1, 0)):
            self.go(self.own.at[i], (me, i), i, {"x": 1 - x})
            self.go(self.own.at[j], (me, j), 2 + j, {"y": 1 - y})
        for i in (0, 1):
            self.go(self.own.at[i], (me, i), 6 + i, {"core": 1 - c})

    def arrived(self, *sems):
        for sem in sems:
            done = self.recv.at[self.base + sem]
            pltpu.make_async_copy(self.own.at[0], self.own.at[0], done).wait()

    def pass_on(self, dy, dx, i, sem, device):
        y, c, _, x = place()
        slot = ((flip(y, dy) * 2 + flip(x, dx)) * 2 + c, i)
        self.go(self.full.at[slot[0], slot[1]], slot, sem, device)

    def forward(self):
        y, c, _, x = place()
        self.arrived(0)
        self.pass_on(0, 1, 0, 4, {"y": 1 - y})
        self.pass_on(0, 1, 0, 8, {"core": 1 - c})
        self.arrived(3)
        self.pass_on(1, 0, 1, 5, {"x": 1 - x})
        self.pass_on(1, 0, 1, 11, {"core": 1 - c})

    def second(self):
        _, c, _, _ = place()
        self.arrived(1)
        self.pass_on(0, 1, 1, 9, {"core": 1 - c})
        self.arrived(2)
        self.pass_on(1, 0, 0, 10, {"core": 1 - c})

    def last(self):
        _, c, _, _ = place()
        self.arrived(4)
        self.pass_on(1, 1, 0, 12, {"core": 1 - c})
        self.arrived(5)
        self.pass_on(1, 1, 1, 13, {"core": 1 - c})

    def sent(self):
        for copy in self.started:
            copy.wait_send()


def neighbours():
    y, c, _, x = place()
    return [{"x": 1 - x}, {"y": 1 - y}, {"core": 1 - c}]


def others():
    y, c, _, x = place()
    return [{"y": flip(y, dy), "core": flip(c, dc), "x": flip(x, dx)} for dy, dc, dx in FLIPS]


def swap(src, dst, send, recv, local):
    y, c, _, x = place()
    me = (y * 2 + c) * 2 + x
    copies = []
    for f, peer in enumerate(others()):
        to = (peer["y"] * 2 + peer["core"]) * 2 + peer["x"]
        copies.append(remote(src.at[to], dst.at[me], send.at[f], recv.at[f], peer))
    copies.append(pltpu.make_async_copy(src.at[me], dst.at[me], local))
    for copy in copies:
        copy.start()
    return copies


def along_line(planes, own, full, send, recv, local):
    z = lax.axis_index("z")
    copies = [
        remote(own, full.at[z], send.at[d], recv.at[d], peer)
        for d, peer in enumerate(line_peers(planes))
    ]
    copies.append(pltpu.make_async_copy(own, full.at[z], local))
    for copy in copies:
        copy.start()
    return copies


def line_peers(planes):
    return [{"z": lax.rem(lax.axis_index("z") + d, planes)} for d in range(1, planes)]


class Line:
    def __init__(self, planes, own, full, send, recv, local):
        self.planes, self.own, self.full, self.send, self.recv = planes, own, full, send, recv
        self.mine = pltpu.make_async_copy(own, full.at[lax.axis_index("z")], local)

    def ways(self):
        z, planes = lax.axis_index("z"), self.planes
        return (
            (0, 1, z, planes - 1 - z),
            (1, planes - 1, planes - 1 - z, z),
        )

    def pass_on(self, d):
        z, planes = lax.axis_index("z"), self.planes
        for way, by, come, left in self.ways():
            block = lax.rem(z + d * (planes - by) + planes, planes)

            @pl.when(jnp.logical_and(come >= d, left >= 1))
            def _():
                src = self.own if d == 0 else self.full.at[block]
                device = {"z": lax.rem(z + by, planes)}
                sem = self.send.at[way, d], self.recv.at[way, d]
                remote(src, self.full.at[block], *sem, device).start()

    def start(self):
        self.mine.start()
        self.pass_on(0)

    def arrived(self, d):
        for way, _, come, _ in self.ways():

            @pl.when(come >= d)
            def _():
                pltpu.make_async_copy(self.own, self.own, self.recv.at[way, d - 1]).wait()

    def step(self, d):
        self.arrived(d)
        self.pass_on(d)

    def finish(self):
        self.arrived(self.planes - 1)
        for d in range(self.planes - 1):
            for way, _, come, left in self.ways():

                @pl.when(jnp.logical_and(come >= d, left >= 1))
                def _():
                    pltpu.make_async_copy(self.own, self.own, self.send.at[way, d]).wait()

        self.mine.wait()


def gather_kernel(own, full, send, recv, local):
    y, c, _, x = place()
    meet(neighbours())
    gather = Gather(own, full, send, recv)
    gather.first()
    mine = pltpu.make_async_copy(own, full.at[(y * 2 + x) * 2 + c], local)
    mine.start()
    gather.forward()
    gather.second()
    gather.last()
    gather.arrived(*range(6, 14))
    gather.sent()
    mine.wait()


def by_owner(planes):
    for owner in range(8 * planes):
        yield owner, owner // (2 * planes) * 2 + owner % 2, owner // 2 % planes


def early_kernel(
    planes,
    small,
    tokens,
    in_proj,
    gate_up,
    out_proj,
    full,
    gu_got,
    ins,
    outs,
    gains,
    taps,
    in_block,
    in_got,
    gu_block,
    out_block,
    line,
    smalls,
    send,
    recv,
    send_i,
    recv_i,
    send_g,
    recv_g,
    send_s,
    recv_s,
    send_z,
    recv_z,
    send_l,
    recv_l,
    local,
):
    y, c, z, x = place()
    me = (y * 2 + c) * 2 + x
    own = small.shape[1]
    meet(others() + line_peers(planes))
    tiny = along_line(planes, small, line, send_z, recv_z, local.at[0])
    out_block[...] = out_proj[...].astype(BF16)
    out_line = Line(planes, out_block, outs, send_l.at[1], recv_l.at[1], local.at[4])
    out_line.start()
    for k in range(3):
        for owner, member, zz in by_owner(planes):
            start, to = (k * 8 * planes + owner) * own, (k * planes + zz) * own
            block = in_proj[:, start : start + own].astype(BF16)
            in_block[member, :, to : to + own] = block
    in_copies = swap(in_block, in_got, send_i, recv_i, local.at[1])
    gather = Gather(tokens, full, send, recv)
    gather.first()
    mine = pltpu.make_async_copy(tokens, full.at[(y * 2 + x) * 2 + c], local.at[2])
    mine.start()
    for copy in tiny:
        copy.wait()
    tiny = []
    for f, peer in enumerate(others()):
        tiny.append(remote(line, smalls.at[me], send_s.at[f], recv_s.at[f], peer))
    tiny.append(pltpu.make_async_copy(line, smalls.at[me], local.at[0]))
    for copy in tiny:
        copy.start()
    for copy in in_copies:
        copy.wait()
    ahead = Line(planes, in_got, ins, send_l.at[0], recv_l.at[0], local.at[1])
    ahead.start()
    if planes > 2:
        out_line.step(1)
    wide = gate_up.shape[2] // (8 * planes)
    for j in (0, 1):
        for owner, member, zz in by_owner(planes):
            block = gate_up[j, :, owner * wide : (owner + 1) * wide].astype(BF16)
            gu_block[member, j, :, zz * wide : (zz + 1) * wide] = block
    gu_copies = swap(gu_block, gu_got, send_g, recv_g, local.at[3])
    for copy in tiny:
        copy.wait()
    for owner, member, zz in by_owner(planes):
        row = smalls[member, zz, 0:2, :].astype(BF16).astype(F32)
        gains[:, owner * own : (owner + 1) * own] = row
    for zz in range(planes):
        row = line[zz, 2:5, :].astype(BF16).astype(F32)
        taps[:, zz * own : (zz + 1) * own] = row
    ahead.step(1)
    gather.forward()
    for d in range(2, planes - 1):
        out_line.step(d)
        ahead.step(d)
    gather.second()
    gather.last()
    gather.arrived(*range(6, 14))
    gather.sent()
    for copy in gu_copies:
        copy.wait()
    mine.wait()
    ahead.finish()
    out_line.finish()


def params(collective_id, vmem=0):
    more = {"vmem_limit_bytes": vmem * 2**20} if vmem else {}
    return pltpu.CompilerParams(collective_id=collective_id, has_side_effects=True, **more)


def cost(micros):
    return pl.CostEstimate(flops=int(micros * 1e9), bytes_accessed=0, transcendentals=0)


def sems(*shape):
    return pltpu.SemaphoreType.DMA(shape)


def plane_gather(own, collective_id):
    return pl.pallas_call(
        gather_kernel,
        out_shape=jax.ShapeDtypeStruct((8,) + own.shape, own.dtype),
        in_specs=[ANY],
        out_specs=ANY,
        scratch_shapes=[sems(14), sems(14), pltpu.SemaphoreType.DMA],
        cost_estimate=cost(45),
        compiler_params=params(collective_id),
    )(own)


def early(planes, small, tokens, in_proj, gate_up, out_proj, collective_id):
    own, width = out_proj.shape
    in_block = (8, own, in_proj.shape[1] // 8)
    gu_block = (8, 2, own, gate_up.shape[2] // 8)
    return pl.pallas_call(
        functools.partial(early_kernel, planes),
        out_shape=[
            jax.ShapeDtypeStruct((8,) + tokens.shape, BF16),
            jax.ShapeDtypeStruct(gu_block, BF16),
            jax.ShapeDtypeStruct((planes,) + in_block, BF16),
            jax.ShapeDtypeStruct((planes, own, width), BF16),
            jax.ShapeDtypeStruct((2, width), F32),
            jax.ShapeDtypeStruct((3, planes * own), F32),
        ],
        in_specs=[VMEM, ANY, VMEM, VMEM, VMEM],
        out_specs=[ANY] * 4 + [VMEM] * 2,
        scratch_shapes=[
            pltpu.VMEM(in_block, BF16),
            pltpu.VMEM(in_block, BF16),
            pltpu.VMEM(gu_block, BF16),
            pltpu.VMEM((own, width), BF16),
            pltpu.VMEM((planes,) + small.shape, F32),
            pltpu.VMEM((8, planes) + small.shape, F32),
            sems(14),
            sems(14),
            sems(7),
            sems(7),
            sems(7),
            sems(7),
            sems(7),
            sems(7),
            sems(planes - 1),
            sems(planes - 1),
            sems(2, 2, planes - 1),
            sems(2, 2, planes - 1),
            sems(5),
        ],
        cost_estimate=cost(70),
        compiler_params=params(collective_id, 40),
    )(small, tokens, in_proj, gate_up, out_proj)


def finish_kernel(planes, ins, gus, gains, taps, outs, ins_got, gus_got, sums, out_sum, *scratch):
    parts, terms, got, outs_got, send, recv, send_g, recv_g = scratch[:8]
    send_z, recv_z, send_o, recv_o, local = scratch[8:]
    meet(others() + line_peers(planes))
    small = swap(gains, parts, send_g, recv_g, local.at[0])
    large = scatter_line(planes, outs, outs_got, send_o, recv_o, local.at[3])
    copies = swap(ins, ins_got, send.at[0], recv.at[0], local.at[1])
    copies += swap(gus, gus_got, send.at[1], recv.at[1], local.at[2])
    for copy in small:
        copy.wait()
    terms[:, 0:2, :] = jnp.sum(parts[...], axis=0)
    terms[:, 2:5, :] = taps[...]
    for copy in scatter_line(planes, terms, got, send_z, recv_z, local.at[0]):
        copy.wait()
    sums[...] = jnp.sum(got[...], axis=0)
    for copy in large:
        copy.wait()
    total = outs_got[0].astype(F32)
    for k in range(1, planes):
        total += outs_got[k].astype(F32)
    out_sum[...] = total
    for copy in copies:
        copy.wait()


def scatter_line(planes, terms, got, send, recv, local):
    z = lax.axis_index("z")
    copies = [
        remote(terms.at[peer["z"]], got.at[z], send.at[d], recv.at[d], peer)
        for d, peer in enumerate(line_peers(planes))
    ]
    copies.append(pltpu.make_async_copy(terms.at[z], got.at[z], local))
    for copy in copies:
        copy.start()
    return copies


def finish(planes, ins, gus, gains, taps, outs, collective_id):
    own = gains.shape[-1]
    return pl.pallas_call(
        functools.partial(finish_kernel, planes),
        out_shape=[
            jax.ShapeDtypeStruct(ins.shape, ins.dtype),
            jax.ShapeDtypeStruct(gus.shape, gus.dtype),
            jax.ShapeDtypeStruct((5, own), F32),
            jax.ShapeDtypeStruct(outs.shape[1:], F32),
        ],
        in_specs=[ANY, ANY, VMEM, VMEM, VMEM],
        out_specs=[ANY, ANY, VMEM, VMEM],
        scratch_shapes=[
            pltpu.VMEM(gains.shape, F32),
            pltpu.VMEM((planes, 5, own), F32),
            pltpu.VMEM((planes, 5, own), F32),
            pltpu.VMEM(outs.shape, BF16),
            sems(2, 7),
            sems(2, 7),
            sems(7),
            sems(7),
            sems(planes - 1),
            sems(planes - 1),
            sems(planes - 1),
            sems(planes - 1),
            sems(4),
        ],
        cost_estimate=cost(25),
        compiler_params=params(collective_id),
    )(ins, gus, gains, taps, outs)


def load_rows(planes, gathered, rows, sem):
    if len(gathered.shape) == 3:
        copy = pltpu.make_async_copy(gathered, rows, sem)
        copy.start()
        return [copy]
    own = gathered.shape[3]
    copies = []
    for z in range(planes):
        for m in range(8):
            start = (((m // 2) * planes + z) * 2 + m % 2) * own
            for j in (0, 1):
                src = gathered.at[z, m, j]
                copies.append(pltpu.make_async_copy(src, rows.at[j, pl.ds(start, own)], sem))
    for copy in copies:
        copy.start()
    return copies


def ffn_kernel(
    planes,
    cot,
    normed,
    gathered,
    down_most,
    down_own,
    act_out,
    dgate_out,
    dup_out,
    grad_out,
    down,
    down_rest,
    down_rows,
    full,
    near,
    weights,
    gates,
    ups,
    staged,
    total,
    send,
    recv,
    local,
    near_sem,
    out_sem,
    send_l,
    recv_l,
):
    y, c, _, x = place()
    piece, width = cot.shape[1:]
    part = down.shape[0]
    most = down_most.shape[1]
    chip_rows = 4 * piece
    half = 2 * piece
    chips = [flip(y, dy) * 2 + flip(x, dx) for dy, dx in ((0, 0), (0, 1), (1, 0), (1, 1))]
    loads = load_rows(planes, gathered, weights, local.at[0])
    mine = pltpu.make_async_copy(cot, full.at[(y * 2 + x) * 2 + c], local.at[1])
    mine.start()
    first_part = pltpu.make_async_copy(down_most, down.at[:, pl.ds(0, most)], local.at[2])

    def fetch(k):
        copy = pltpu.make_async_copy(
            normed.at[pl.ds(chips[k] * 2, 2)], near.at[k % 2], near_sem.at[k % 2]
        )
        copy.start()
        return copy

    fetched = {0: fetch(0), 1: fetch(1)}
    first_part.start()
    meet(neighbours() + list(ring()))
    ahead = Line(planes, down_own, down_rest, send_l, recv_l, local.at[3])
    ahead.start()
    gather = Gather(cot, full, send, recv)
    gather.first()
    for copy in loads:
        copy.wait()

    def gate_up(k, slot):
        fetched[k].wait()

        def body(i, _):
            rows = pl.ds(pl.multiple_of(i * half, half), half)
            left = near[k % 2, i].reshape(half, width)
            gates[slot, rows, :] = times(left, weights[0])
            ups[slot, rows, :] = times(left, weights[1])
            return 0

        lax.fori_loop(0, 2, body, 0)
        if k + 2 < 4:
            fetched[k + 2] = fetch(k + 2)

    written = {}

    def back(k, slot):
        if k >= 2:
            for copy in written[k - 2]:
                copy.wait()
        room = staged.at[k % 2]

        def body(i, _):
            rows = pl.ds(pl.multiple_of(i * half, half), half)
            grad = times_t(full[chips[k] * 2 + i].reshape(half, width), down[...])
            gate, up = gates[slot, rows, :], ups[slot, rows, :]
            sigma = jax.nn.sigmoid(gate)
            silu = gate * sigma
            room[0, i] = (silu * up).astype(BF16).reshape(2, piece, part)
            dgate = grad * up * sigma * (1.0 + gate * (1.0 - sigma))
            room[1, i] = dgate.astype(BF16).reshape(2, piece, part)
            room[2, i] = (grad * silu).astype(BF16).reshape(2, piece, part)
            return 0

        lax.fori_loop(0, 2, body, 0)
        written[k] = []
        for n, out in enumerate((act_out, dgate_out, dup_out)):
            copy = pltpu.make_async_copy(
                room.at[n], out.at[pl.ds(chips[k] * 2, 2)], out_sem.at[k % 2, n]
            )
            copy.start()
            written[k].append(copy)
        active = room[0].reshape(chip_rows, part)
        tile = width // 3

        def sum_up(n, _):
            columns = pl.ds(pl.multiple_of(n * tile, tile), tile)
            right = full[pl.ds(chips[k] * 2, 2), :, :, columns].reshape(chip_rows, tile)
            product = t_times(active, right)
            if k == 0:
                total[:, columns] = product
            elif k < 3:
                total[:, columns] += product
            else:
                product = total[:, columns] + product
                own = part // planes
                for z in range(planes):
                    grad_out[z, :, columns] = product[z * own : (z + 1) * own].astype(BF16)
            return 0

        lax.fori_loop(0, 3, sum_up, 0)

    gate_up(0, 0)
    if planes > 2:
        ahead.step(1)
    gate_up(1, 1)
    for d in range(2, planes - 1):
        ahead.step(d)
    gather.forward()
    gate_up(2, 2)
    mine.wait()
    gather.arrived(6, 7)
    first_part.wait()
    ahead.finish()
    for zz in range(planes):
        count = part // planes
        down_rows[zz * count : (zz + 1) * count, :] = down_rest[zz].astype(F32)
    down[:, most:] = down_rows[...].astype(BF16)
    back(0, 0)
    gather.second()
    gather.arrived(8, 9)
    back(1, 1)
    gate_up(3, 0)
    gather.arrived(10, 11)
    back(2, 2)
    gather.last()
    gather.arrived(12, 13)
    back(3, 0)
    gather.sent()
    for k in (2, 3):
        for copy in written[k]:
            copy.wait()


def ffn(planes, cot, normed, gathered, down_most, down_own, collective_id):
    _, piece, width = cot.shape
    part, most = down_most.shape
    rest = width - most
    wide = jax.ShapeDtypeStruct((8, 2, piece, part), BF16)
    return pl.pallas_call(
        functools.partial(ffn_kernel, planes),
        out_shape=[
            wide,
            wide,
            wide,
            jax.ShapeDtypeStruct((planes, part // planes, width), BF16),
            jax.ShapeDtypeStruct((part, width), BF16),
        ],
        in_specs=[ANY] * 5,
        out_specs=[ANY, ANY, ANY, VMEM, VMEM],
        scratch_shapes=[
            pltpu.VMEM((planes, part // planes, rest), BF16),
            pltpu.VMEM((part, rest), F32),
            pltpu.VMEM((8, 2, piece, width), BF16),
            pltpu.VMEM((2, 2, 2, piece, width), BF16),
            pltpu.VMEM((2, width, part), BF16),
            pltpu.VMEM((3, 4 * piece, part), F32),
            pltpu.VMEM((3, 4 * piece, part), F32),
            pltpu.VMEM((2, 3, 2, 2, piece, part), BF16),
            pltpu.VMEM((part, width), F32),
            sems(14),
            sems(14),
            sems(4),
            sems(2),
            sems(2, 3),
            sems(2, planes - 1),
            sems(2, planes - 1),
        ],
        cost_estimate=cost(55),
        compiler_params=params(collective_id, 62),
    )(cot, normed, gathered, down_most, down_own)


def room(piece, width):
    return [
        pltpu.VMEM((4, 2, piece, width), BF16),
        pltpu.VMEM((4, 2, piece, width), BF16),
        pltpu.VMEM((3, 2, piece, width), BF16),
        pltpu.VMEM((2, piece, width), F32),
        pltpu.VMEM((2, piece, width), BF16),
        pltpu.VMEM((2, piece, width), BF16),
        pltpu.VMEM((2, piece, width), BF16),
        sems(10),
        sems(10),
    ]


def scatter(lefts, rights, transposed, out, scratch, fills=()):
    staged, held, ready, keep, diag, from_x, from_y, send, recv = scratch
    y, c, _, x = place()
    _, piece, width = out.shape
    rows = 2 * piece
    tile = width // 3
    copies = []

    def go(src, dst, sem, device):
        copy = remote(src, dst, send.at[sem], recv.at[sem], device)
        copy.start()
        copies.append(copy)
        return copy

    def product(dy, dx, core, store):
        member = (flip(y, dy) * 2 + flip(x, dx)) * 2 + core

        def body(n, _):
            columns = pl.ds(pl.multiple_of(n * tile, tile), tile)
            value = None
            for left, right in zip(lefts, rights):
                a = left[member].reshape(rows, left.shape[-1])
                if transposed:
                    term = times_t(a, right[columns, :])
                else:
                    term = times(a, right[:, columns])
                value = term if value is None else value + term
            store(columns, value.reshape(2, piece, tile))
            return 0

        lax.fori_loop(0, 3, body, 0)

    order = ((1, 1), (0, 1), (1, 0), (0, 0))
    over = []

    def to_other_core(n):
        dy, dx = order[n]

        def store(columns, value):
            staged[n, :, :, columns] = value.astype(BF16)

        product(dy, dx, 1 - c, store)
        over.append(go(staged.at[n], held.at[n], n, {"core": 1 - c}))

    def own_core(n, store):
        dy, dx = order[n]
        over[n].wait_recv()

        def add(columns, value):
            store(columns, value + held[n, :, :, columns].astype(F32))

        product(dy, dx, c, add)

    def store_diag(columns, value):
        ready[0, :, :, columns] = value.astype(BF16)

    def store_x(columns, value):
        ready[1, 1, :, columns] = value[1].astype(BF16)
        keep[0, :, columns] = value[0]

    def store_y(columns, value):
        ready[2, 0, :, columns] = value[0].astype(BF16)
        keep[1, :, columns] = value[1]

    def store_own(columns, value):
        out[:, :, columns] = value

    to_other_core(0)
    to_other_core(1)
    own_core(0, store_diag)
    diag_y = go(ready.at[0, 0], diag.at[0], 4, {"y": 1 - y})
    diag_x = go(ready.at[0, 1], diag.at[1], 5, {"x": 1 - x})
    to_other_core(2)
    own_core(1, store_x)
    x_one = go(ready.at[1, 1], from_x.at[1], 6, {"x": 1 - x})
    own_core(2, store_y)
    y_zero = go(ready.at[2, 0], from_y.at[0], 7, {"y": 1 - y})
    to_other_core(3)
    own_core(3, store_own)
    if fills:
        fills[0]()
    diag_y.wait_recv()
    ready[1, 0] = (keep[0] + diag[0].astype(F32)).astype(BF16)
    x_zero = go(ready.at[1, 0], from_x.at[0], 8, {"x": 1 - x})
    diag_x.wait_recv()
    ready[2, 1] = (keep[1] + diag[1].astype(F32)).astype(BF16)
    y_one = go(ready.at[2, 1], from_y.at[1], 9, {"y": 1 - y})
    if fills:
        fills[1]()
    for i, (one, two) in enumerate(((x_zero, y_zero), (x_one, y_one))):
        one.wait_recv()
        two.wait_recv()
        out[i] += from_x[i].astype(F32) + from_y[i].astype(F32)
    for copy in copies:
        copy.wait_send()


def by_rows(piece, work):
    step = 16

    def body(n, _):
        rows = pl.ds(pl.multiple_of(n * step, step), step)
        for i in (0, 1):
            work(i, rows)
        return 0

    lax.fori_loop(0, piece // step, body, 0)


def norm_back(i, rows, source, gain, grad, base, sums):
    normal, scale = rms_parts(source)
    term = grad * normal
    sums[...] += term[:8] + term[8:]
    return base + rms_back(grad * gain, normal, scale)


def last_kernel(left, right, tokens, dmiddle, gain, token_grad, sums, out, *scratch):
    meet(neighbours())
    scatter([left], [right], True, out, scratch)
    sums[...] = jnp.zeros_like(sums)

    def work(i, rows):
        source = tokens[i, rows, :].astype(F32)
        token_grad[i, rows, :] = norm_back(
            i, rows, source, gain[...], out[i, rows, :], dmiddle[i, rows, :], sums
        )

    by_rows(tokens.shape[1], work)


def last(left, right, tokens, dmiddle, gain, collective_id):
    piece, width = left.shape[2], right.shape[0]
    return pl.pallas_call(
        last_kernel,
        out_shape=[
            jax.ShapeDtypeStruct((2, piece, width), F32),
            jax.ShapeDtypeStruct((8, width), F32),
        ],
        in_specs=[VMEM] * 5,
        out_specs=[VMEM] * 2,
        scratch_shapes=[pltpu.VMEM((2, piece, width), F32)] + room(piece, width),
        cost_estimate=cost(50),
        compiler_params=params(collective_id, 50),
    )(left, right, tokens, dmiddle, gain)


def ffn_back_kernel(
    planes,
    dgate,
    dup,
    gathered,
    normed,
    middle,
    cot,
    gain,
    grads,
    dmiddle,
    dmix,
    sums,
    out,
    weights,
    every,
    local,
    *scratch,
):
    loads = load_rows(planes, gathered, weights, local.at[0])
    whole = pltpu.make_async_copy(normed, every, local.at[1])
    whole.start()
    meet(neighbours())
    lefts = (dgate, dup)
    width, part = weights.shape[1:]
    quarter = width // 4
    all_rows = 8 * 2 * normed.shape[2]

    def gradient(j):
        own = grads.shape[-2]

        def body(q, _):
            columns = pl.ds(pl.multiple_of(q * quarter, quarter), quarter)
            left = every[:, :, :, columns].reshape(all_rows, quarter)
            right = lefts[j][...].reshape(all_rows, part)
            value = t_times(left, right).astype(BF16)
            if len(grads.shape) == 3:
                grads[j, columns, :] = value
                return 0
            for z in range(planes):
                for xx in (0, 1):
                    start = (z * 2 + xx) * own
                    grads[z, q * 2 + xx, j] = value[start : start + own]
            return 0

        lax.fori_loop(0, 4, body, 0)

    def first():
        whole.wait()
        gradient(0)

    for copy in loads:
        copy.wait()
    rights = [weights.at[0], weights.at[1]]
    scatter(lefts, rights, True, out, scratch, (first, lambda: gradient(1)))
    sums[...] = jnp.zeros_like(sums)

    def work(i, rows):
        value = norm_back(
            i,
            rows,
            middle[i, rows, :],
            gain[...],
            out[i, rows, :],
            cot[i, rows, :].astype(F32),
            sums,
        )
        dmiddle[i, rows, :] = value
        dmix[i, rows, :] = value.astype(BF16)

    by_rows(middle.shape[1], work)


def ffn_back(planes, dgate, dup, gathered, normed, middle, cot, gain, collective_id):
    piece, part = dgate.shape[2:]
    width = normed.shape[3]
    return pl.pallas_call(
        functools.partial(ffn_back_kernel, planes),
        out_shape=[
            jax.ShapeDtypeStruct(gathered.shape, BF16),
            jax.ShapeDtypeStruct((2, piece, width), F32),
            jax.ShapeDtypeStruct((2, piece, width), BF16),
            jax.ShapeDtypeStruct((8, width), F32),
        ],
        in_specs=[VMEM, VMEM, ANY, ANY, VMEM, VMEM, VMEM],
        out_specs=[VMEM] * 4,
        scratch_shapes=[
            pltpu.VMEM((2, piece, width), F32),
            pltpu.VMEM((2, width, part), BF16),
            pltpu.VMEM((8, 2, piece, width), BF16),
            sems(2),
        ]
        + room(piece, width),
        cost_estimate=cost(60),
        compiler_params=params(collective_id, 60),
    )(dgate, dup, gathered, normed, middle, cot, gain)


def ring():
    z, planes = lax.axis_index("z"), lax.axis_size("z")
    return {"z": lax.rem(z + 1, planes)}, {"z": lax.rem(z + planes - 1, planes)}


def load_in(planes, gathered, rows, sem):
    if len(gathered.shape) == 2:
        copies = [pltpu.make_async_copy(gathered, rows, sem)]
    else:
        own = gathered.shape[2]
        copies = []
        for z in range(planes):
            for m in range(8):
                start = (((m // 2) * planes + z) * 2 + m % 2) * own
                to = rows.at[pl.ds(start, own)]
                copies.append(pltpu.make_async_copy(gathered.at[z, m], to, sem))
    for copy in copies:
        copy.start()
    return copies


def mixer_kernel(
    planes,
    tokens_all,
    gathered,
    taps,
    blocks,
    tokens,
    gain,
    out,
    normed_two,
    normed_out,
    proj_out,
    conv_out,
    gated_out,
    weights_out,
    right,
    rows_out,
    own,
    every,
    weights,
    proj,
    conv,
    gated,
    tall,
    ends,
    before,
    local,
    ends_sem,
    send,
    recv,
    rights,
    got,
    send_o,
    recv_o,
    send_s,
    recv_s,
):
    y, c, z, x = place()
    me = (y * 2 + x) * 2 + c
    _, _, piece, width = every.shape
    part = conv.shape[-1]
    loads = load_in(planes, gathered, weights, local.at[0])
    chips = {}
    for n, chip in enumerate((1, 3, 0, 2)):
        rows = pl.ds(chip * 2, 2)
        chips[chip] = pltpu.make_async_copy(tokens_all.at[rows], every.at[rows], local.at[1 + n])
        chips[chip].start()
    after, prior = ring()
    meet(others() + [after, prior])
    count = blocks.shape[1]
    for zz in range(planes):
        rows_out[zz * count : (zz + 1) * count, :] = blocks[zz].astype(F32)
    right[...] = rows_out[...].astype(BF16).reshape(right.shape)
    whole = Gather(right, rights, send_o, recv_o)
    whole.first()
    own_right = pltpu.make_async_copy(right, rights.at[me], local.at[11])
    own_right.start()
    for copy in loads:
        copy.wait()
    saved = [pltpu.make_async_copy(weights, weights_out, local.at[5])]

    def project(member):
        value = every[member].reshape(2 * piece, width).astype(F32)
        value = (rms_parts(value)[0] * gain[0:1, :]).astype(BF16)
        every[member] = value.reshape(2, piece, width)
        a = every[member].reshape(2 * piece, width)
        proj[member] = times(a, weights[...]).reshape(2, piece, 3 * part)

    def inner(member, i, rows):
        return proj[member, i, rows, :part] * proj[member, i, rows, 2 * part :]

    last = slice(piece - 2, piece)
    for yy in (0, 1):
        chips[yy * 2 + 1].wait()

        def second(core, _):
            member = (yy * 2 + 1) * 2 + core
            project(member)
            for i in (0, 1):
                ends[(yy * 2 + core) * 2 + i] = inner(member, i, last)
            return 0

        lax.fori_loop(0, 2, second, 0)
    to_next = remote(ends, before, ends_sem.at[0], ends_sem.at[1], after)
    to_next.start()
    for yy in (0, 1):
        chips[yy * 2].wait()

        def first(core, _):
            project((yy * 2) * 2 + core)
            return 0

        lax.fori_loop(0, 2, first, 0)
        if yy == 0:
            whole.forward()
    whole.second()
    saved.append(pltpu.make_async_copy(proj, proj_out, local.at[6]))
    saved.append(pltpu.make_async_copy(every, normed_out, local.at[10]))
    for copy in saved:
        copy.start()

    def convolve(member, i, start):
        tall[6:8, :] = start
        now = inner(member, i, slice(0, piece))
        tall[8 : 8 + piece, :] = now
        value = taps[0:1] * tall[6 : 6 + piece, :] + taps[1:2] * tall[7 : 7 + piece, :]
        value += taps[2:3] * now
        conv[member, i] = value
        gate = proj[member, i, :, part : 2 * part]
        gated[member, i] = (gate * value).astype(BF16)

    def right_half(n, _):
        member = (n // 2) * 4 + 2 + n % 2
        for i in (0, 1):
            convolve(member, i, inner(member - 2, i, last))
        return 0

    lax.fori_loop(0, 4, right_half, 0)
    whole.last()
    to_next.wait_recv()

    def left_half(n, _):
        member = (n // 2) * 4 + n % 2
        for i in (0, 1):
            start = before[n * 2 + i]
            convolve(member, i, jnp.where(z > 0, start, jnp.zeros_like(start)))
        return 0

    lax.fori_loop(0, 4, left_half, 0)
    swapped = [pltpu.make_async_copy(gated.at[me], got.at[me], local.at[12])]
    for f, peer in enumerate(others()):
        to = (peer["y"] * 2 + peer["x"]) * 2 + peer["core"]
        swapped.append(remote(gated.at[to], got.at[me], send_s.at[f], recv_s.at[f], peer))
    for copy in swapped:
        copy.start()
    for n, (src, dst) in enumerate(((conv, conv_out), (gated, gated_out))):
        saved.append(pltpu.make_async_copy(src, dst, local.at[7 + n]))
        saved[-1].start()
    whole.arrived(*range(6, 14))
    whole.sent()
    own_right.wait()
    for copy in swapped:
        copy.wait()
    third = width // 3

    def mix(n, _):
        columns = pl.ds(pl.multiple_of(n * third, third), third)
        total = tokens[:, :, columns].astype(F32).reshape(2 * piece, third)
        for member in range(8):
            left = got[member].reshape(2 * piece, part)
            total += times(left, rights[member, :, :, columns].reshape(part, third))
        out[:, :, columns] = total.reshape(2, piece, third)
        return 0

    lax.fori_loop(0, 3, mix, 0)

    def work(i, rows):
        own[i, rows, :] = (rms_parts(out[i, rows, :])[0] * gain[1:2, :]).astype(BF16)

    by_rows(piece, work)
    gather = Gather(own, normed_two, send, recv)
    gather.first()
    mine = pltpu.make_async_copy(own, normed_two.at[(y * 2 + x) * 2 + c], local.at[9])
    mine.start()
    saved.append(mine)
    gather.forward()
    gather.second()
    gather.last()
    gather.arrived(*range(6, 14))
    gather.sent()
    to_next.wait_send()
    for copy in saved:
        copy.wait()


def mixer_forward(planes, tokens_all, gathered, taps, blocks, tokens, gain, collective_id):
    _, _, piece, width = tokens_all.shape
    part = blocks.shape[1] * planes
    saved = [
        (tokens_all.shape, BF16),
        (tokens_all.shape, BF16),
        ((8, 2, piece, 3 * part), F32),
        ((8, 2, piece, part), F32),
        ((8, 2, piece, part), BF16),
        ((width, 3 * part), BF16),
    ]
    return pl.pallas_call(
        functools.partial(mixer_kernel, planes),
        out_shape=[jax.ShapeDtypeStruct((2, piece, width), F32)]
        + [jax.ShapeDtypeStruct(*item) for item in saved]
        + [jax.ShapeDtypeStruct((2, part // 2, width), BF16)],
        in_specs=[ANY, ANY] + [VMEM] * 4,
        out_specs=[VMEM] + [ANY] * 6 + [VMEM],
        scratch_shapes=[
            pltpu.VMEM((part, width), F32),
            pltpu.VMEM((2, piece, width), BF16),
            pltpu.VMEM((8, 2, piece, width), BF16),
            pltpu.VMEM((width, 3 * part), BF16),
            pltpu.VMEM((8, 2, piece, 3 * part), F32),
            pltpu.VMEM((8, 2, piece, part), F32),
            pltpu.VMEM((8, 2, piece, part), BF16),
            pltpu.VMEM((8 + piece, part), F32),
            pltpu.VMEM((8, 2, part), F32),
            pltpu.VMEM((8, 2, part), F32),
            sems(13),
            sems(2),
            sems(14),
            sems(14),
            pltpu.VMEM((8, 2, part // 2, width), BF16),
            pltpu.VMEM((8, 2, piece, part), BF16),
            sems(14),
            sems(14),
            sems(7),
            sems(7),
        ],
        cost_estimate=cost(95),
        compiler_params=params(collective_id, 60),
    )(tokens_all, gathered, taps, blocks, tokens, gain)


def branch_kernel(
    planes,
    active,
    down,
    own,
    right,
    proj_in,
    conv_in,
    gated,
    normed,
    taps,
    out,
    dmix,
    dproj,
    grad_in,
    grad_out,
    grad_taps,
    near,
    proj,
    conv,
    tall,
    starts,
    beyond,
    total_out,
    total_in,
    near_sem,
    local,
    ends_sem,
    send,
    recv,
    *scratch,
):
    y, c, z, x = place()
    _, _, piece, part = conv.shape
    width = out.shape[2]
    chips = [flip(y, dy) * 2 + flip(x, dx) for dy, dx in ((0, 0), (0, 1), (1, 0), (1, 1))]
    half = 2 * piece
    loads = [
        pltpu.make_async_copy(proj_in, proj, local.at[0]),
        pltpu.make_async_copy(conv_in, conv, local.at[1]),
    ]
    for copy in loads:
        copy.start()

    def fetch(source, k):
        copy = pltpu.make_async_copy(
            source.at[pl.ds(chips[k] * 2, 2)], near.at[k % 2], near_sem.at[k % 2]
        )
        copy.start()
        return copy

    after, prior = ring()
    meet(neighbours() + [after, prior])
    gather = Gather(own, dmix, send, recv)
    gather.first()
    mine = pltpu.make_async_copy(own, dmix.at[(y * 2 + x) * 2 + c], local.at[2])
    mine.start()
    to_prior = remote(starts.at[0], beyond, ends_sem.at[0], ends_sem.at[1], prior)
    grad_taps[...] = jnp.zeros_like(grad_taps)
    third = width // 3

    def gradients(k):
        chip, other = chips[k], flip(x, k % 2)

        def body(core, _):
            member = chip * 2 + core
            grad = times_t(near[k % 2, core].reshape(half, width), right[...])
            grad = grad.reshape(2, piece, part)
            for i in (0, 1):
                dproj[member, i, :, part : 2 * part] = (grad[i] * conv[member, i]).astype(BF16)
                dconv = grad[i] * proj[member, i, :, part : 2 * part]
                conv[member, i] = dconv
                starts[other, (flip(y, k // 2) * 2 + core) * 2 + i] = dconv[:2]
            return 0

        lax.fori_loop(0, 2, body, 0)

        def sum_up(n, _):
            columns = pl.ds(pl.multiple_of(n * third, third), third)
            left = gated[pl.ds(chip * 2, 2)].reshape(2 * half, part)
            product = t_times(left, near[k % 2, :, :, :, columns].reshape(2 * half, third))
            if k == 0:
                total_out[:, columns] = product
            elif k < 3:
                total_out[:, columns] += product
            else:
                product = total_out[:, columns] + product
                own_rows = part // planes
                for zz in range(planes):
                    block = product[zz * own_rows : (zz + 1) * own_rows]
                    grad_out[zz, :, columns] = block.astype(BF16)
            return 0

        lax.fori_loop(0, 3, sum_up, 0)

    def through(member, i, end):
        tall[0:piece, :] = conv[member, i]
        tall[piece : piece + 2, :] = end
        now, one, two = conv[member, i], tall[1 : piece + 1, :], tall[2 : piece + 2, :]
        b_part, x_part = proj[member, i, :, :part], proj[member, i, :, 2 * part :]
        dmixed = taps[2:3] * now + taps[1:2] * one + taps[0:1] * two
        dproj[member, i, :, :part] = (dmixed * x_part).astype(BF16)
        dproj[member, i, :, 2 * part :] = (dmixed * b_part).astype(BF16)
        mixed = b_part * x_part
        for k, shifted in enumerate((two, one, now)):
            grad_taps[k : k + 1, :] += jnp.sum(mixed * shifted, axis=0, keepdims=True)

    def left_half(n, _):
        member = (n // 2) * 4 + n % 2
        for i in (0, 1):
            through(member, i, conv[member + 2, i, 0:2, :])
        return 0

    def right_half(n, _):
        member = (n // 2) * 4 + 2 + n % 2
        for i in (0, 1):
            end = beyond[n * 2 + i]
            through(member, i, jnp.where(z < planes - 1, end, jnp.zeros_like(end)))
        return 0

    def one():
        for copy in loads:
            copy.wait()
        mine.wait()
        gather.arrived(6, 7)
        fetch(dmix, 0).wait()
        gradients(0)
        gather.second()
        gather.arrived(8, 9)
        fetched = fetch(dmix, 1)
        gather.arrived(10, 11)
        following = fetch(dmix, 2)
        fetched.wait()
        gradients(1)
        following.wait()
        gradients(2)
        gather.last()
        gather.arrived(12, 13)
        fetch(dmix, 3).wait()
        to_normed.append(fetch(normed, 0))
        gradients(3)
        to_normed.append(fetch(normed, 1))
        to_prior.start()
        lax.fori_loop(0, 4, left_half, 0)

    quarter = width // 4

    def two():
        to_prior.wait_recv()
        lax.fori_loop(0, 4, right_half, 0)
        for k in range(4):
            to_normed[k].wait()

            def sum_up(q, _):
                columns = pl.ds(pl.multiple_of(q * quarter, quarter), quarter)
                left = near[k % 2, :, :, :, columns].reshape(2 * half, quarter)
                right_side = dproj[pl.ds(chips[k] * 2, 2)].reshape(2 * half, 3 * part)
                product = t_times(left, right_side)
                if k == 0:
                    total_in[columns, :] = product
                elif k < 3:
                    total_in[columns, :] += product
                else:
                    product = (total_in[columns, :] + product).astype(BF16)
                    if len(grad_in.shape) == 2:
                        grad_in[columns, :] = product
                        return 0
                    own_rows = grad_in.shape[2]
                    for zz in range(planes):
                        for xx in (0, 1):
                            start = (zz * 2 + xx) * own_rows
                            grad_in[zz, q * 2 + xx] = product[start : start + own_rows]
                return 0

            lax.fori_loop(0, 4, sum_up, 0)
            if k < 2:
                to_normed.append(fetch(normed, k + 2))

    to_normed = []
    gather.forward()
    scatter([active], [down], False, out, scratch, (one, two))
    gather.sent()
    to_prior.wait_send()


def branch_forward(
    planes, active, down, dmix, right, proj, conv, gated, normed, taps, in_shape, collective_id
):
    _, piece, width = dmix.shape
    part = right.shape[0]
    outs = [
        ((2, piece, width), F32),
        (normed.shape, BF16),
        ((8, 2, piece, 3 * part), BF16),
        (in_shape, BF16),
        ((planes, part // planes, width), BF16),
        ((3, part), F32),
    ]
    got = pl.pallas_call(
        functools.partial(branch_kernel, planes),
        out_shape=[jax.ShapeDtypeStruct(*item) for item in outs],
        in_specs=[VMEM, VMEM, ANY, VMEM, ANY, ANY, VMEM, ANY, VMEM],
        out_specs=[VMEM, ANY] + [VMEM] * 4,
        scratch_shapes=[
            pltpu.VMEM((2, 2, 2, piece, width), BF16),
            pltpu.VMEM((8, 2, piece, 3 * part), F32),
            pltpu.VMEM((8, 2, piece, part), F32),
            pltpu.VMEM((8 + piece, part), F32),
            pltpu.VMEM((2, 8, 2, part), F32),
            pltpu.VMEM((8, 2, part), F32),
            pltpu.VMEM((part, width), F32),
            pltpu.VMEM((width, 3 * part), F32),
            sems(2),
            sems(3),
            sems(2),
            sems(14),
            sems(14),
        ]
        + room(piece, width),
        cost_estimate=cost(90),
        compiler_params=params(collective_id, 62),
    )(active, down, dmix, right, proj, conv, gated, normed, taps)
    return got[:1] + got[2:]


def update_kernel(planes, three, rate, decay, got, weight, first, second, grad, moment, updated):
    wide = got.shape[-1] // planes
    parts = 1
    if three:
        wide, parts = wide // 3, 3
    for k in range(parts):
        for owner in range(8 * planes):
            pair, z, xx = owner // (2 * planes), owner // 2 % planes, owner % 2
            start = (k * planes + z) * wide
            to = (k * 8 * planes + owner) * wide
            if three:
                value = got[pair * 2 + xx, :, start : start + wide]
            else:
                value = got[pair * 2 + xx, 0, :, start : start + wide]
            if three:
                grad[:, to : to + wide] = value.astype(F32)
            else:
                grad[0, :, to : to + wide] = value.astype(F32)
    moment[...], updated[...] = adamw(
        weight[...], first[...], second[...], grad[...], rate, decay
    )


def update(planes, got, weight, first, second, rate, decay):
    three = weight.ndim == 2
    rows = weight.shape[-2]
    step = 16 if rows % 16 == 0 else rows
    part = got.shape[-1]
    columns = weight.shape[-1]
    if three:
        grid = (rows // step,)
        got_spec = pl.BlockSpec((8, step, part), lambda n: (0, n, 0))
        spec = pl.BlockSpec((step, columns), lambda n: (n, 0))
    else:
        grid = (2, rows // step)
        got_spec = pl.BlockSpec((8, 1, step, part), lambda j, n: (0, j, n, 0))
        spec = pl.BlockSpec((1, step, columns), lambda j, n: (j, n, 0))
    size = weight.size * 4
    return pl.pallas_call(
        functools.partial(update_kernel, planes, three, rate, decay),
        out_shape=[jax.ShapeDtypeStruct(weight.shape, F32)] * 3,
        grid=grid,
        in_specs=[got_spec, spec, spec, spec],
        out_specs=[spec] * 3,
        cost_estimate=pl.CostEstimate(
            flops=12 * size, bytes_accessed=7 * size, transcendentals=0
        ),
        compiler_params=pltpu.CompilerParams(vmem_limit_bytes=32 * 2**20),
    )(got, weight, first, second)


def rms_parts(values):
    scale = lax.rsqrt(jnp.mean(values * values, axis=-1, keepdims=True) + 1e-05)
    return (values * scale, scale)


def rms_back(grad_hat, normal, scale):
    return scale * (grad_hat - normal * jnp.mean(grad_hat * normal, axis=-1, keepdims=True))


def times(left, right):
    return jnp.dot(left, right, preferred_element_type=F32)


def times_t(left, right):
    return lax.dot_general(left, right, (((1,), (1,)), ((), ())), preferred_element_type=F32)


def t_times(left, right):
    return lax.dot_general(left, right, (((0,), (0,)), ((), ())), preferred_element_type=F32)


def adamw(weight, first_mom, second_mom, gradient, rate, decay):
    bias_one = 1.0 - 0.9**STEP
    bias_two = 1.0 - 0.95**STEP
    first_new = 0.9 * first_mom + 0.1 * gradient
    second_new = 0.95 * second_mom + 0.05 * gradient * gradient
    direction = first_new / bias_one / (jnp.sqrt(second_new / bias_two) + 1e-08)
    return (second_new, weight - rate * (direction + decay * weight))


def on_device(
    tokens,
    cotangent,
    norm_gains,
    in_proj,
    conv_taps,
    out_proj,
    gate_up,
    down_proj,
    first_gains,
    first_in,
    first_conv,
    first_out,
    first_gate_up,
    first_down,
    second_gains,
    second_in,
    second_conv,
    second_out,
    second_gate_up,
    second_down,
):
    planes = lax.axis_size("z")
    seqs, piece, width = tokens.shape
    rows = seqs * piece
    all_rows = 8 * rows
    own_d = in_proj.shape[0]
    own_f = down_proj.shape[0]
    ff = gate_up.shape[2]
    part_d = width // 8
    part_f = ff // 8

    in_tiles = own_d % 16 == 0

    def along_z(value):
        return lax.all_gather(value, "z", axis=0, tiled=False)

    most = width // 3 * 2
    down_low = down_proj.astype(BF16)
    down_most = along_z(down_low[:, :most]).reshape(part_f, most)
    small = jnp.concatenate([norm_gains, conv_taps], axis=0)
    tokens_all, gu_mine, in_t, out_blocks, gains, taps = early(
        planes, small, tokens, in_proj, gate_up, out_proj, 0
    )
    if not in_tiles:
        in_t = in_t.reshape(planes, 4, 2, own_d, 3 * part_d).transpose(1, 0, 2, 3, 4)
        in_t = in_t.reshape(width, 3 * part_d)
    gu_t = along_z(gu_mine)
    if not in_tiles:
        gu_t = gu_t.reshape(planes, 4, 2, 2, own_d, part_f).transpose(3, 1, 0, 2, 4, 5)
        gu_t = gu_t.reshape(2, width, part_f)

    middle, normed_two_all, normed_all, proj, conv, gated, in_whole, out_t = mixer_forward(
        planes, tokens_all, in_t, taps, out_blocks, tokens, gains, 2
    )
    out_t = out_t.reshape(part_d, width)
    active, dgate, dup, grad_down, down_t = ffn(
        planes, cotangent, normed_two_all, gu_t, down_most, down_low[:, most:], 4
    )

    def sum_z(value):
        return lax.psum_scatter(value, "z", scatter_dimension=0, tiled=False)

    g_down = sum_z(grad_down)
    grad_gu, dmiddle, dmix, gain_two = ffn_back(
        planes, dgate, dup, gu_t, normed_two_all, middle, cotangent, gains[1:], 5
    )
    if not in_tiles:
        grad_gu = grad_gu.reshape(2, 4, planes, 2, own_d, part_f).transpose(2, 1, 3, 0, 4, 5)
        grad_gu = grad_gu.reshape(planes, 8, 2, own_d, part_f)
    grad_gu, g_down = lax.optimization_barrier((grad_gu, g_down))
    g_down = g_down.astype(F32)
    gu_back = sum_z(grad_gu)

    branch, dproj, grad_in, grad_out, grad_taps = branch_forward(
        planes,
        active,
        down_t,
        dmix,
        out_t,
        proj,
        conv,
        gated,
        normed_all,
        taps,
        in_t.shape,
        7,
    )
    block_out = (middle + branch).astype(BF16)
    if not in_tiles:
        grad_in = grad_in.reshape(4, planes, 2, own_d, 3 * part_d).transpose(1, 0, 2, 3, 4)
        grad_in = grad_in.reshape(planes, 8, own_d, 3 * part_d)
    grad_in, gu_back, dproj = lax.optimization_barrier((grad_in, gu_back, dproj))
    in_back = sum_z(grad_in)
    taps_parts = grad_taps.reshape(3, planes, own_d).transpose(1, 0, 2)

    token_grad, gain_one = last(dproj, in_whole, tokens, dmiddle, gains[:1], 8)
    grad_gains = jnp.stack([jnp.sum(gain_one, axis=0), jnp.sum(gain_two, axis=0)])
    gains_parts = grad_gains.reshape(2, 4, planes, 2, own_d).transpose(1, 3, 2, 0, 4)
    gains_parts = gains_parts.reshape(8, planes, 2, own_d)
    in_got, gu_got, sums, g_out = finish(
        planes, in_back, gu_back, gains_parts, taps_parts, grad_out, 9
    )
    g_gains, g_conv = sums[:2], sums[2:]
    m_gains, u_gains = adamw(norm_gains, first_gains, second_gains, g_gains, 0.4, 0.0)
    g_in, m_in, u_in = update(planes, in_got, in_proj, first_in, second_in, 0.02, 0.1)
    m_conv, u_conv = adamw(conv_taps, first_conv, second_conv, g_conv, 0.2, 0.1)
    m_out, u_out = adamw(out_proj, first_out, second_out, g_out, 0.02, 0.1)
    g_gu, m_gu, u_gu = update(
        planes, gu_got, gate_up, first_gate_up, second_gate_up, 0.02, 0.1
    )
    m_down, u_down = adamw(down_proj, first_down, second_down, g_down, 0.01, 0.1)
    return (
        block_out,
        token_grad,
        g_gains,
        g_in,
        g_conv,
        g_out,
        g_gu,
        g_down,
        m_gains,
        m_in,
        m_conv,
        m_out,
        m_gu,
        m_down,
        u_gains,
        u_in,
        u_conv,
        u_out,
        u_gu,
        u_down,
    )


def solution(mesh):
    lines = mesh.shape["seq"] // 2
    fine = Mesh(mesh.devices.reshape(2, 2, lines, 2), ("y", "core", "z", "x"))
    dp, seq = ("y", "core"), ("z", "x")
    every = dp + seq
    tokens = P(dp, seq, None)
    weights = (
        P(None, every),
        P(every, None),
        P(None, every),
        P(every, None),
        P(None, every, None),
        P(every, None),
    )
    return jax.shard_map(
        on_device,
        mesh=fine,
        in_specs=(tokens, tokens) + weights * 3,
        out_specs=(tokens, tokens) + weights * 3,
        check_vma=False,
    )
```

```python
import functools

import jax
import jax.numpy as jnp
from jax import lax
from jax.experimental import pallas as pl
from jax.experimental.pallas import tpu as pltpu
from jax.sharding import Mesh
from jax.sharding import PartitionSpec as P

STEP = 10
MESH = pl.DeviceIdType.MESH
BF16 = jnp.bfloat16
F32 = jnp.float32
FLIPS = [(dy, dc, dx) for dy in (0, 1) for dc in (0, 1) for dx in (0, 1)][1:]
ANY = pl.BlockSpec(memory_space=pl.ANY)
VMEM = pl.BlockSpec(memory_space=pltpu.VMEM)


def place():
    return tuple(lax.axis_index(a) for a in ("y", "core", "z", "x"))


def flip(value, by):
    return 1 - value if by else value


def remote(src, dst, send, recv, device):
    return pltpu.make_async_remote_copy(
        src_ref=src,
        dst_ref=dst,
        send_sem=send,
        recv_sem=recv,
        device_id=device,
        device_id_type=MESH,
    )


def meet(peers):
    barrier = pltpu.get_barrier_semaphore()
    for peer in peers:
        pl.semaphore_signal(barrier, inc=1, device_id=peer, device_id_type=MESH)
    pl.semaphore_wait(barrier, len(peers))


class Gather:
    def __init__(self, own, full, send, recv, base=0):
        self.own, self.full, self.send, self.recv, self.base = own, full, send, recv, base
        self.started = []

    def go(self, src, slot, sem, device):
        sem = self.base + sem
        copy = remote(
            src, self.full.at[slot[0], slot[1]], self.send.at[sem], self.recv.at[sem], device
        )
        copy.start()
        self.started.append(copy)

    def first(self):
        y, c, _, x = place()
        me = (y * 2 + x) * 2 + c
        for i, j in ((0, 1), (1, 0)):
            self.go(self.own.at[i], (me, i), i, {"x": 1 - x})
            self.go(self.own.at[j], (me, j), 2 + j, {"y": 1 - y})
        for i in (0, 1):
            self.go(self.own.at[i], (me, i), 6 + i, {"core": 1 - c})

    def arrived(self, *sems):
        for sem in sems:
            done = self.recv.at[self.base + sem]
            pltpu.make_async_copy(self.own.at[0], self.own.at[0], done).wait()

    def pass_on(self, dy, dx, i, sem, device):
        y, c, _, x = place()
        slot = ((flip(y, dy) * 2 + flip(x, dx)) * 2 + c, i)
        self.go(self.full.at[slot[0], slot[1]], slot, sem, device)

    def forward(self):
        y, c, _, x = place()
        self.arrived(0)
        self.pass_on(0, 1, 0, 4, {"y": 1 - y})
        self.pass_on(0, 1, 0, 8, {"core": 1 - c})
        self.arrived(3)
        self.pass_on(1, 0, 1, 5, {"x": 1 - x})
        self.pass_on(1, 0, 1, 11, {"core": 1 - c})

    def second(self):
        _, c, _, _ = place()
        self.arrived(1)
        self.pass_on(0, 1, 1, 9, {"core": 1 - c})
        self.arrived(2)
        self.pass_on(1, 0, 0, 10, {"core": 1 - c})

    def last(self):
        _, c, _, _ = place()
        self.arrived(4)
        self.pass_on(1, 1, 0, 12, {"core": 1 - c})
        self.arrived(5)
        self.pass_on(1, 1, 1, 13, {"core": 1 - c})

    def sent(self):
        for copy in self.started:
            copy.wait_send()


def neighbours():
    y, c, _, x = place()
    return [{"x": 1 - x}, {"y": 1 - y}, {"core": 1 - c}]


def others():
    y, c, _, x = place()
    return [{"y": flip(y, dy), "core": flip(c, dc), "x": flip(x, dx)} for dy, dc, dx in FLIPS]


def swap(src, dst, send, recv, local):
    y, c, _, x = place()
    me = (y * 2 + c) * 2 + x
    copies = []
    for f, peer in enumerate(others()):
        to = (peer["y"] * 2 + peer["core"]) * 2 + peer["x"]
        copies.append(remote(src.at[to], dst.at[me], send.at[f], recv.at[f], peer))
    copies.append(pltpu.make_async_copy(src.at[me], dst.at[me], local))
    for copy in copies:
        copy.start()
    return copies


def along_line(planes, own, full, send, recv, local):
    z = lax.axis_index("z")
    copies = [
        remote(own, full.at[z], send.at[d], recv.at[d], peer)
        for d, peer in enumerate(line_peers(planes))
    ]
    copies.append(pltpu.make_async_copy(own, full.at[z], local))
    for copy in copies:
        copy.start()
    return copies


def line_peers(planes):
    return [{"z": lax.rem(lax.axis_index("z") + d, planes)} for d in range(1, planes)]


class Line:
    def __init__(self, planes, own, full, send, recv, local):
        self.planes, self.own, self.full, self.send, self.recv = planes, own, full, send, recv
        self.mine = pltpu.make_async_copy(own, full.at[lax.axis_index("z")], local)

    def ways(self):
        z, planes = lax.axis_index("z"), self.planes
        return (
            (0, 1, z, planes - 1 - z),
            (1, planes - 1, planes - 1 - z, z),
        )

    def pass_on(self, d):
        z, planes = lax.axis_index("z"), self.planes
        for way, by, come, left in self.ways():
            block = lax.rem(z + d * (planes - by) + planes, planes)

            @pl.when(jnp.logical_and(come >= d, left >= 1))
            def _():
                src = self.own if d == 0 else self.full.at[block]
                device = {"z": lax.rem(z + by, planes)}
                sem = self.send.at[way, d], self.recv.at[way, d]
                remote(src, self.full.at[block], *sem, device).start()

    def start(self):
        self.mine.start()
        self.pass_on(0)

    def arrived(self, d):
        for way, _, come, _ in self.ways():

            @pl.when(come >= d)
            def _():
                pltpu.make_async_copy(self.own, self.own, self.recv.at[way, d - 1]).wait()

    def step(self, d):
        self.arrived(d)
        self.pass_on(d)

    def finish(self):
        self.arrived(self.planes - 1)
        for d in range(self.planes - 1):
            for way, _, come, left in self.ways():

                @pl.when(jnp.logical_and(come >= d, left >= 1))
                def _():
                    pltpu.make_async_copy(self.own, self.own, self.send.at[way, d]).wait()

        self.mine.wait()


def gather_kernel(own, full, send, recv, local):
    y, c, _, x = place()
    meet(neighbours())
    gather = Gather(own, full, send, recv)
    gather.first()
    mine = pltpu.make_async_copy(own, full.at[(y * 2 + x) * 2 + c], local)
    mine.start()
    gather.forward()
    gather.second()
    gather.last()
    gather.arrived(*range(6, 14))
    gather.sent()
    mine.wait()


def by_owner(planes):
    for owner in range(8 * planes):
        yield owner, owner // (2 * planes) * 2 + owner % 2, owner // 2 % planes


def early_kernel(
    planes,
    small,
    tokens,
    in_proj,
    gate_up,
    out_proj,
    full,
    gu_got,
    ins,
    outs,
    gains,
    taps,
    in_block,
    in_got,
    gu_block,
    out_block,
    line,
    smalls,
    send,
    recv,
    send_i,
    recv_i,
    send_g,
    recv_g,
    send_s,
    recv_s,
    send_z,
    recv_z,
    send_l,
    recv_l,
    local,
):
    y, c, z, x = place()
    me = (y * 2 + c) * 2 + x
    own = small.shape[1]
    meet(others() + line_peers(planes))
    tiny = along_line(planes, small, line, send_z, recv_z, local.at[0])
    out_block[...] = out_proj[...].astype(BF16)
    out_line = Line(planes, out_block, outs, send_l.at[1], recv_l.at[1], local.at[4])
    out_line.start()
    for k in range(3):
        for owner, member, zz in by_owner(planes):
            start, to = (k * 8 * planes + owner) * own, (k * planes + zz) * own
            block = in_proj[:, start : start + own].astype(BF16)
            in_block[member, :, to : to + own] = block
    in_copies = swap(in_block, in_got, send_i, recv_i, local.at[1])
    gather = Gather(tokens, full, send, recv)
    gather.first()
    mine = pltpu.make_async_copy(tokens, full.at[(y * 2 + x) * 2 + c], local.at[2])
    mine.start()
    for copy in tiny:
        copy.wait()
    tiny = []
    for f, peer in enumerate(others()):
        tiny.append(remote(line, smalls.at[me], send_s.at[f], recv_s.at[f], peer))
    tiny.append(pltpu.make_async_copy(line, smalls.at[me], local.at[0]))
    for copy in tiny:
        copy.start()
    for copy in in_copies:
        copy.wait()
    ahead = Line(planes, in_got, ins, send_l.at[0], recv_l.at[0], local.at[1])
    ahead.start()
    if planes > 2:
        out_line.step(1)
    wide = gate_up.shape[2] // (8 * planes)
    for j in (0, 1):
        for owner, member, zz in by_owner(planes):
            block = gate_up[j, :, owner * wide : (owner + 1) * wide].astype(BF16)
            gu_block[member, j, :, zz * wide : (zz + 1) * wide] = block
    gu_copies = swap(gu_block, gu_got, send_g, recv_g, local.at[3])
    for copy in tiny:
        copy.wait()
    for owner, member, zz in by_owner(planes):
        row = smalls[member, zz, 0:2, :].astype(BF16).astype(F32)
        gains[:, owner * own : (owner + 1) * own] = row
    for zz in range(planes):
        row = line[zz, 2:5, :].astype(BF16).astype(F32)
        taps[:, zz * own : (zz + 1) * own] = row
    ahead.step(1)
    gather.forward()
    for d in range(2, planes - 1):
        out_line.step(d)
        ahead.step(d)
    gather.second()
    gather.last()
    gather.arrived(*range(6, 14))
    gather.sent()
    for copy in gu_copies:
        copy.wait()
    mine.wait()
    ahead.finish()
    out_line.finish()


def params(collective_id, vmem=0):
    more = {"vmem_limit_bytes": vmem * 2**20} if vmem else {}
    return pltpu.CompilerParams(collective_id=collective_id, has_side_effects=True, **more)


def cost(micros):
    return pl.CostEstimate(flops=int(micros * 1e9), bytes_accessed=0, transcendentals=0)


def sems(*shape):
    return pltpu.SemaphoreType.DMA(shape)


def plane_gather(own, collective_id):
    return pl.pallas_call(
        gather_kernel,
        out_shape=jax.ShapeDtypeStruct((8,) + own.shape, own.dtype),
        in_specs=[ANY],
        out_specs=ANY,
        scratch_shapes=[sems(14), sems(14), pltpu.SemaphoreType.DMA],
        cost_estimate=cost(45),
        compiler_params=params(collective_id),
    )(own)


def early(planes, small, tokens, in_proj, gate_up, out_proj, collective_id):
    own, width = out_proj.shape
    in_block = (8, own, in_proj.shape[1] // 8)
    gu_block = (8, 2, own, gate_up.shape[2] // 8)
    return pl.pallas_call(
        functools.partial(early_kernel, planes),
        out_shape=[
            jax.ShapeDtypeStruct((8,) + tokens.shape, BF16),
            jax.ShapeDtypeStruct(gu_block, BF16),
            jax.ShapeDtypeStruct((planes,) + in_block, BF16),
            jax.ShapeDtypeStruct((planes, own, width), BF16),
            jax.ShapeDtypeStruct((2, width), F32),
            jax.ShapeDtypeStruct((3, planes * own), F32),
        ],
        in_specs=[VMEM, ANY, VMEM, VMEM, VMEM],
        out_specs=[ANY] * 4 + [VMEM] * 2,
        scratch_shapes=[
            pltpu.VMEM(in_block, BF16),
            pltpu.VMEM(in_block, BF16),
            pltpu.VMEM(gu_block, BF16),
            pltpu.VMEM((own, width), BF16),
            pltpu.VMEM((planes,) + small.shape, F32),
            pltpu.VMEM((8, planes) + small.shape, F32),
            sems(14),
            sems(14),
            sems(7),
            sems(7),
            sems(7),
            sems(7),
            sems(7),
            sems(7),
            sems(planes - 1),
            sems(planes - 1),
            sems(2, 2, planes - 1),
            sems(2, 2, planes - 1),
            sems(5),
        ],
        cost_estimate=cost(70),
        compiler_params=params(collective_id, 40),
    )(small, tokens, in_proj, gate_up, out_proj)


def finish_kernel(planes, ins, gus, gains, taps, outs, ins_got, gus_got, sums, out_sum, *scratch):
    parts, terms, got, outs_got, send, recv, send_g, recv_g = scratch[:8]
    send_z, recv_z, send_o, recv_o, local = scratch[8:]
    meet(others() + line_peers(planes))
    small = swap(gains, parts, send_g, recv_g, local.at[0])
    large = scatter_line(planes, outs, outs_got, send_o, recv_o, local.at[3])
    copies = swap(ins, ins_got, send.at[0], recv.at[0], local.at[1])
    copies += swap(gus, gus_got, send.at[1], recv.at[1], local.at[2])
    for copy in small:
        copy.wait()
    terms[:, 0:2, :] = jnp.sum(parts[...], axis=0)
    terms[:, 2:5, :] = taps[...]
    for copy in scatter_line(planes, terms, got, send_z, recv_z, local.at[0]):
        copy.wait()
    sums[...] = jnp.sum(got[...], axis=0)
    for copy in large:
        copy.wait()
    total = outs_got[0].astype(F32)
    for k in range(1, planes):
        total += outs_got[k].astype(F32)
    out_sum[...] = total
    for copy in copies:
        copy.wait()


def scatter_line(planes, terms, got, send, recv, local):
    z = lax.axis_index("z")
    copies = [
        remote(terms.at[peer["z"]], got.at[z], send.at[d], recv.at[d], peer)
        for d, peer in enumerate(line_peers(planes))
    ]
    copies.append(pltpu.make_async_copy(terms.at[z], got.at[z], local))
    for copy in copies:
        copy.start()
    return copies


def finish(planes, ins, gus, gains, taps, outs, collective_id):
    own = gains.shape[-1]
    return pl.pallas_call(
        functools.partial(finish_kernel, planes),
        out_shape=[
            jax.ShapeDtypeStruct(ins.shape, ins.dtype),
            jax.ShapeDtypeStruct(gus.shape, gus.dtype),
            jax.ShapeDtypeStruct((5, own), F32),
            jax.ShapeDtypeStruct(outs.shape[1:], F32),
        ],
        in_specs=[ANY, ANY, VMEM, VMEM, VMEM],
        out_specs=[ANY, ANY, VMEM, VMEM],
        scratch_shapes=[
            pltpu.VMEM(gains.shape, F32),
            pltpu.VMEM((planes, 5, own), F32),
            pltpu.VMEM((planes, 5, own), F32),
            pltpu.VMEM(outs.shape, BF16),
            sems(2, 7),
            sems(2, 7),
            sems(7),
            sems(7),
            sems(planes - 1),
            sems(planes - 1),
            sems(planes - 1),
            sems(planes - 1),
            sems(4),
        ],
        cost_estimate=cost(25),
        compiler_params=params(collective_id),
    )(ins, gus, gains, taps, outs)


def load_rows(planes, gathered, rows, sem):
    if len(gathered.shape) == 3:
        copy = pltpu.make_async_copy(gathered, rows, sem)
        copy.start()
        return [copy]
    own = gathered.shape[3]
    copies = []
    for z in range(planes):
        for m in range(8):
            start = (((m // 2) * planes + z) * 2 + m % 2) * own
            for j in (0, 1):
                src = gathered.at[z, m, j]
                copies.append(pltpu.make_async_copy(src, rows.at[j, pl.ds(start, own)], sem))
    for copy in copies:
        copy.start()
    return copies


def ffn_kernel(
    planes,
    cot,
    normed,
    gathered,
    down_most,
    down_own,
    act_out,
    dgate_out,
    dup_out,
    grad_out,
    down,
    down_rest,
    down_rows,
    full,
    near,
    weights,
    gates,
    ups,
    staged,
    total,
    send,
    recv,
    local,
    near_sem,
    out_sem,
    send_l,
    recv_l,
):
    y, c, _, x = place()
    piece, width = cot.shape[1:]
    part = down.shape[0]
    most = down_most.shape[1]
    chip_rows = 4 * piece
    half = 2 * piece
    chips = [flip(y, dy) * 2 + flip(x, dx) for dy, dx in ((0, 0), (0, 1), (1, 0), (1, 1))]
    loads = load_rows(planes, gathered, weights, local.at[0])
    mine = pltpu.make_async_copy(cot, full.at[(y * 2 + x) * 2 + c], local.at[1])
    mine.start()
    first_part = pltpu.make_async_copy(down_most, down.at[:, pl.ds(0, most)], local.at[2])

    def fetch(k):
        copy = pltpu.make_async_copy(
            normed.at[pl.ds(chips[k] * 2, 2)], near.at[k % 2], near_sem.at[k % 2]
        )
        copy.start()
        return copy

    fetched = {0: fetch(0), 1: fetch(1)}
    first_part.start()
    meet(neighbours() + list(ring()))
    ahead = Line(planes, down_own, down_rest, send_l, recv_l, local.at[3])
    ahead.start()
    gather = Gather(cot, full, send, recv)
    gather.first()
    for copy in loads:
        copy.wait()

    def gate_up(k, slot):
        fetched[k].wait()

        def body(i, _):
            rows = pl.ds(pl.multiple_of(i * half, half), half)
            left = near[k % 2, i].reshape(half, width)
            gates[slot, rows, :] = times(left, weights[0])
            ups[slot, rows, :] = times(left, weights[1])
            return 0

        lax.fori_loop(0, 2, body, 0)
        if k + 2 < 4:
            fetched[k + 2] = fetch(k + 2)

    written = {}

    def back(k, slot):
        if k >= 2:
            for copy in written[k - 2]:
                copy.wait()
        room = staged.at[k % 2]

        def body(i, _):
            rows = pl.ds(pl.multiple_of(i * half, half), half)
            grad = times_t(full[chips[k] * 2 + i].reshape(half, width), down[...])
            gate, up = gates[slot, rows, :], ups[slot, rows, :]
            sigma = jax.nn.sigmoid(gate)
            silu = gate * sigma
            room[0, i] = (silu * up).astype(BF16).reshape(2, piece, part)
            dgate = grad * up * sigma * (1.0 + gate * (1.0 - sigma))
            room[1, i] = dgate.astype(BF16).reshape(2, piece, part)
            room[2, i] = (grad * silu).astype(BF16).reshape(2, piece, part)
            return 0

        lax.fori_loop(0, 2, body, 0)
        written[k] = []
        for n, out in enumerate((act_out, dgate_out, dup_out)):
            copy = pltpu.make_async_copy(
                room.at[n], out.at[pl.ds(chips[k] * 2, 2)], out_sem.at[k % 2, n]
            )
            copy.start()
            written[k].append(copy)
        active = room[0].reshape(chip_rows, part)
        tile = width // 3

        def sum_up(n, _):
            columns = pl.ds(pl.multiple_of(n * tile, tile), tile)
            right = full[pl.ds(chips[k] * 2, 2), :, :, columns].reshape(chip_rows, tile)
            product = t_times(active, right)
            if k == 0:
                total[:, columns] = product
            elif k < 3:
                total[:, columns] += product
            else:
                product = total[:, columns] + product
                own = part // planes
                for z in range(planes):
                    grad_out[z, :, columns] = product[z * own : (z + 1) * own].astype(BF16)
            return 0

        lax.fori_loop(0, 3, sum_up, 0)

    gate_up(0, 0)
    if planes > 2:
        ahead.step(1)
    gate_up(1, 1)
    for d in range(2, planes - 1):
        ahead.step(d)
    gather.forward()
    gate_up(2, 2)
    mine.wait()
    gather.arrived(6, 7)
    first_part.wait()
    ahead.finish()
    for zz in range(planes):
        count = part // planes
        down_rows[zz * count : (zz + 1) * count, :] = down_rest[zz].astype(F32)
    down[:, most:] = down_rows[...].astype(BF16)
    back(0, 0)
    gather.second()
    gather.arrived(8, 9)
    back(1, 1)
    gate_up(3, 0)
    gather.arrived(10, 11)
    back(2, 2)
    gather.last()
    gather.arrived(12, 13)
    back(3, 0)
    gather.sent()
    for k in (2, 3):
        for copy in written[k]:
            copy.wait()


def ffn(planes, cot, normed, gathered, down_most, down_own, collective_id):
    _, piece, width = cot.shape
    part, most = down_most.shape
    rest = width - most
    wide = jax.ShapeDtypeStruct((8, 2, piece, part), BF16)
    return pl.pallas_call(
        functools.partial(ffn_kernel, planes),
        out_shape=[
            wide,
            wide,
            wide,
            jax.ShapeDtypeStruct((planes, part // planes, width), BF16),
            jax.ShapeDtypeStruct((part, width), BF16),
        ],
        in_specs=[ANY] * 5,
        out_specs=[ANY, ANY, ANY, VMEM, VMEM],
        scratch_shapes=[
            pltpu.VMEM((planes, part // planes, rest), BF16),
            pltpu.VMEM((part, rest), F32),
            pltpu.VMEM((8, 2, piece, width), BF16),
            pltpu.VMEM((2, 2, 2, piece, width), BF16),
            pltpu.VMEM((2, width, part), BF16),
            pltpu.VMEM((3, 4 * piece, part), F32),
            pltpu.VMEM((3, 4 * piece, part), F32),
            pltpu.VMEM((2, 3, 2, 2, piece, part), BF16),
            pltpu.VMEM((part, width), F32),
            sems(14),
            sems(14),
            sems(4),
            sems(2),
            sems(2, 3),
            sems(2, planes - 1),
            sems(2, planes - 1),
        ],
        cost_estimate=cost(55),
        compiler_params=params(collective_id, 62),
    )(cot, normed, gathered, down_most, down_own)


def room(piece, width):
    return [
        pltpu.VMEM((4, 2, piece, width), BF16),
        pltpu.VMEM((4, 2, piece, width), BF16),
        pltpu.VMEM((3, 2, piece, width), BF16),
        pltpu.VMEM((2, piece, width), F32),
        pltpu.VMEM((2, piece, width), BF16),
        pltpu.VMEM((2, piece, width), BF16),
        pltpu.VMEM((2, piece, width), BF16),
        sems(11),
        sems(11),
    ]


def scatter(lefts, rights, transposed, out, scratch, fills=(), loaded=None):
    staged, held, ready, keep, diag, from_x, from_y, send, recv = scratch
    y, c, _, x = place()
    _, piece, width = out.shape
    rows = 2 * piece
    tile = width // 3
    copies = []

    def go(src, dst, sem, device):
        copy = remote(src, dst, send.at[sem], recv.at[sem], device)
        copy.start()
        copies.append(copy)
        return copy

    def product(dy, dx, core, store, i=None):
        member = (flip(y, dy) * 2 + flip(x, dx)) * 2 + core

        def body(n, _):
            columns = pl.ds(pl.multiple_of(n * tile, tile), tile)
            value = None
            for left, right in zip(lefts, rights):
                a = left[member].reshape(rows, left.shape[-1]) if i is None else left[member, i]
                if transposed:
                    term = times_t(a, right[columns, :])
                else:
                    term = times(a, right[:, columns])
                value = term if value is None else value + term
            store(columns, value.reshape(2, piece, tile) if i is None else value)
            return 0

        lax.fori_loop(0, 3, body, 0)

    order = ((1, 1), (0, 1), (1, 0), (0, 0))
    over = []

    def to_other_core(n):
        dy, dx = order[n]

        def store(columns, value):
            staged[n, :, :, columns] = value.astype(BF16)

        product(dy, dx, 1 - c, store)
        over.append(go(staged.at[n], held.at[n], n, {"core": 1 - c}))

    def own_core(n, store):
        dy, dx = order[n]
        over[n].wait_recv()

        def add(columns, value):
            store(columns, value + held[n, :, :, columns].astype(F32))

        product(dy, dx, c, add)

    def store_x(columns, value):
        ready[1, 1, :, columns] = value[1].astype(BF16)
        keep[0, :, columns] = value[0]

    def store_y(columns, value):
        ready[2, 0, :, columns] = value[0].astype(BF16)
        keep[1, :, columns] = value[1]

    def store_own(columns, value):
        out[:, :, columns] = value

    def diag_half(i):
        dy, dx = order[0]

        def store(columns, value):
            staged[0, i, :, columns] = value.astype(BF16)

        product(dy, dx, 1 - c, store, i)
        return go(staged.at[0, i], held.at[0, i], 0 if i == 0 else 10, {"core": 1 - c})

    def diag_sum(i, copy):
        dy, dx = order[0]

        def store(columns, value):
            copy_in = held[0, i, :, columns].astype(F32)
            ready[0, i, :, columns] = (value + copy_in).astype(BF16)

        copy.wait_recv()
        product(dy, dx, c, store, i)

    if loaded:
        loaded(0)
    halves = [diag_half(0), diag_half(1)]
    diag_sum(0, halves[0])
    diag_y = go(ready.at[0, 0], diag.at[0], 4, {"y": 1 - y})
    diag_sum(1, halves[1])
    diag_x = go(ready.at[0, 1], diag.at[1], 5, {"x": 1 - x})
    over.append(None)
    if loaded:
        loaded(1)
    to_other_core(1)
    if loaded:
        loaded(2)
    to_other_core(2)
    own_core(1, store_x)
    x_one = go(ready.at[1, 1], from_x.at[1], 6, {"x": 1 - x})
    own_core(2, store_y)
    y_zero = go(ready.at[2, 0], from_y.at[0], 7, {"y": 1 - y})
    if loaded:
        loaded(3)
    to_other_core(3)
    own_core(3, store_own)
    if fills and fills[0]:
        fills[0]()
    diag_y.wait_recv()
    ready[1, 0] = (keep[0] + diag[0].astype(F32)).astype(BF16)
    x_zero = go(ready.at[1, 0], from_x.at[0], 8, {"x": 1 - x})
    diag_x.wait_recv()
    ready[2, 1] = (keep[1] + diag[1].astype(F32)).astype(BF16)
    y_one = go(ready.at[2, 1], from_y.at[1], 9, {"y": 1 - y})
    if fills:
        fills[1]()
    for i, (one, two) in enumerate(((x_zero, y_zero), (x_one, y_one))):
        one.wait_recv()
        two.wait_recv()
        out[i] += from_x[i].astype(F32) + from_y[i].astype(F32)
    for copy in copies:
        copy.wait_send()


def by_rows(piece, work):
    step = 32

    def body(n, _):
        rows = pl.ds(pl.multiple_of(n * step, step), step)
        for i in (0, 1):
            work(i, rows)
        return 0

    lax.fori_loop(0, piece // step, body, 0)


def norm_back(i, rows, source, gain, grad, base, sums):
    normal, scale = rms_parts(source)
    term = grad * normal
    sums[...] += (term[:8] + term[8:16]) + (term[16:24] + term[24:])
    return base + rms_back(grad * gain, normal, scale)


def load(pairs, sem):
    copies = [pltpu.make_async_copy(src, dst, sem.at[n]) for n, (src, dst) in enumerate(pairs)]
    for copy in copies:
        copy.start()
    return copies


def far_first():
    y, _, _, x = place()
    return [flip(y, dy) * 2 + flip(x, dx) for dy, dx in ((1, 1), (0, 1), (1, 0), (0, 0))]


def last_kernel(
    planes,
    left_in,
    right_in,
    tokens_in,
    dmiddle_in,
    ins,
    gain,
    token_grad,
    sums,
    in_sum,
    out,
    left,
    right,
    tokens,
    dmiddle,
    ins_got,
    sem,
    send_z,
    recv_z,
    *scratch,
):
    parts = [(right_in, right)]
    parts += [(left_in.at[pl.ds(n * 2, 2)], left.at[pl.ds(n * 2, 2)]) for n in far_first()]
    copies = load(parts + [(tokens_in, tokens), (dmiddle_in, dmiddle)], sem)
    meet(neighbours() + line_peers(planes))
    line = scatter_line(planes, ins, ins_got, send_z, recv_z, sem.at[7])
    copies[0].wait()
    scatter([left], [right], True, out, scratch, loaded=lambda n: copies[1 + n].wait())
    copies[5].wait()
    copies[6].wait()
    sums[...] = jnp.zeros_like(sums)

    def work(i, rows):
        source = tokens[i, rows, :].astype(F32)
        token_grad[i, rows, :] = norm_back(
            i, rows, source, gain[...], out[i, rows, :], dmiddle[i, rows, :], sums
        )

    by_rows(tokens.shape[1], work)
    for copy in line:
        copy.wait()
    for member in range(8):
        total = ins_got[0, member].astype(F32)
        for k in range(1, planes):
            total += ins_got[k, member].astype(F32)
        in_sum[member] = total.astype(BF16)


def last(planes, left, right, tokens, dmiddle, ins, gain, collective_id):
    piece, width = left.shape[2], right.shape[0]
    return pl.pallas_call(
        functools.partial(last_kernel, planes),
        out_shape=[
            jax.ShapeDtypeStruct((2, piece, width), F32),
            jax.ShapeDtypeStruct((8, width), F32),
            jax.ShapeDtypeStruct(ins.shape[1:], BF16),
        ],
        in_specs=[ANY] * 5 + [VMEM],
        out_specs=[VMEM] * 3,
        scratch_shapes=[
            pltpu.VMEM((2, piece, width), F32),
            pltpu.VMEM(left.shape, BF16),
            pltpu.VMEM(right.shape, BF16),
            pltpu.VMEM(tokens.shape, BF16),
            pltpu.VMEM(dmiddle.shape, F32),
            pltpu.VMEM(ins.shape, BF16),
            sems(8),
            sems(planes - 1),
            sems(planes - 1),
        ]
        + room(piece, width),
        cost_estimate=cost(50),
        compiler_params=params(collective_id, 50),
    )(left, right, tokens, dmiddle, ins, gain)


def ffn_back_kernel(
    planes,
    dgate_in,
    dup_in,
    gathered,
    normed,
    middle_in,
    cot_in,
    gain,
    grads,
    dmiddle,
    dmix,
    sums,
    out,
    weights,
    every,
    dgate,
    dup,
    middle,
    cot,
    local,
    sem,
    *scratch,
):
    loads = load_rows(planes, gathered, weights, local.at[0])
    lefts = (dgate, dup)
    parts = []
    for n in far_first():
        rows = pl.ds(n * 2, 2)
        parts += [(dgate_in.at[rows], dgate.at[rows]), (dup_in.at[rows], dup.at[rows])]
    copies = load(parts + [(middle_in, middle), (cot_in, cot)], sem)
    whole = pltpu.make_async_copy(normed, every, local.at[1])
    whole.start()
    meet(neighbours())
    width, part = weights.shape[1:]
    quarter = width // 4
    all_rows = 8 * 2 * normed.shape[2]

    def gradient(j):
        own = grads.shape[-2]

        def body(q, _):
            columns = pl.ds(pl.multiple_of(q * quarter, quarter), quarter)
            left = every[:, :, :, columns].reshape(all_rows, quarter)
            right = lefts[j][...].reshape(all_rows, part)
            value = t_times(left, right).astype(BF16)
            if len(grads.shape) == 3:
                grads[j, columns, :] = value
                return 0
            for z in range(planes):
                for xx in (0, 1):
                    start = (z * 2 + xx) * own
                    grads[z, q * 2 + xx, j] = value[start : start + own]
            return 0

        lax.fori_loop(0, 4, body, 0)

    def both():
        whole.wait()
        gradient(0)
        gradient(1)

    for copy in loads:
        copy.wait()
    rights = [weights.at[0], weights.at[1]]

    def loaded(n):
        copies[2 * n].wait()
        copies[2 * n + 1].wait()

    scatter(lefts, rights, True, out, scratch, (None, both), loaded)
    copies[8].wait()
    copies[9].wait()
    sums[...] = jnp.zeros_like(sums)

    def work(i, rows):
        value = norm_back(
            i,
            rows,
            middle[i, rows, :],
            gain[...],
            out[i, rows, :],
            cot[i, rows, :].astype(F32),
            sums,
        )
        dmiddle[i, rows, :] = value
        dmix[i, rows, :] = value.astype(BF16)

    by_rows(middle.shape[1], work)


def ffn_back(planes, dgate, dup, gathered, normed, middle, cot, gain, collective_id):
    piece, part = dgate.shape[2:]
    width = normed.shape[3]
    return pl.pallas_call(
        functools.partial(ffn_back_kernel, planes),
        out_shape=[
            jax.ShapeDtypeStruct(gathered.shape, BF16),
            jax.ShapeDtypeStruct((2, piece, width), F32),
            jax.ShapeDtypeStruct((2, piece, width), BF16),
            jax.ShapeDtypeStruct((8, width), F32),
        ],
        in_specs=[ANY] * 6 + [VMEM],
        out_specs=[VMEM] * 4,
        scratch_shapes=[
            pltpu.VMEM((2, piece, width), F32),
            pltpu.VMEM((2, width, part), BF16),
            pltpu.VMEM((8, 2, piece, width), BF16),
            pltpu.VMEM(dgate.shape, BF16),
            pltpu.VMEM(dup.shape, BF16),
            pltpu.VMEM(middle.shape, F32),
            pltpu.VMEM(cot.shape, BF16),
            sems(2),
            sems(10),
        ]
        + room(piece, width),
        cost_estimate=cost(60),
        compiler_params=params(collective_id, 60),
    )(dgate, dup, gathered, normed, middle, cot, gain)


def ring():
    z, planes = lax.axis_index("z"), lax.axis_size("z")
    return {"z": lax.rem(z + 1, planes)}, {"z": lax.rem(z + planes - 1, planes)}


def load_in(planes, gathered, rows, sem):
    if len(gathered.shape) == 2:
        copies = [pltpu.make_async_copy(gathered, rows, sem)]
    else:
        own = gathered.shape[2]
        copies = []
        for z in range(planes):
            for m in range(8):
                start = (((m // 2) * planes + z) * 2 + m % 2) * own
                to = rows.at[pl.ds(start, own)]
                copies.append(pltpu.make_async_copy(gathered.at[z, m], to, sem))
    for copy in copies:
        copy.start()
    return copies


def mixer_kernel(
    planes,
    tokens_all,
    gathered,
    taps,
    blocks,
    tokens,
    gain,
    out,
    normed_two,
    normed_out,
    proj_out,
    conv_out,
    gated_out,
    weights_out,
    right,
    rows_out,
    own,
    every,
    weights,
    proj,
    conv,
    gated,
    tall,
    ends,
    before,
    local,
    ends_sem,
    send,
    recv,
    rights,
    got,
    send_o,
    recv_o,
    send_s,
    recv_s,
):
    y, c, z, x = place()
    me = (y * 2 + x) * 2 + c
    _, _, piece, width = every.shape
    part = conv.shape[-1]
    loads = load_in(planes, gathered, weights, local.at[0])
    chips = {}
    for n, chip in enumerate((1, 3, 0, 2)):
        rows = pl.ds(chip * 2, 2)
        chips[chip] = pltpu.make_async_copy(tokens_all.at[rows], every.at[rows], local.at[1 + n])
        chips[chip].start()
    after, prior = ring()
    meet(others() + [after, prior])
    count = blocks.shape[1]
    for zz in range(planes):
        rows_out[zz * count : (zz + 1) * count, :] = blocks[zz].astype(F32)
    right[...] = rows_out[...].astype(BF16).reshape(right.shape)
    whole = Gather(right, rights, send_o, recv_o)
    whole.first()
    own_right = pltpu.make_async_copy(right, rights.at[me], local.at[11])
    own_right.start()
    for copy in loads:
        copy.wait()
    saved = [pltpu.make_async_copy(weights, weights_out, local.at[5])]

    def project(member):
        value = every[member].reshape(2 * piece, width).astype(F32)
        value = (rms_parts(value)[0] * gain[0:1, :]).astype(BF16)
        every[member] = value.reshape(2, piece, width)
        a = every[member].reshape(2 * piece, width)
        proj[member] = times(a, weights[...]).reshape(2, piece, 3 * part)

    def inner(member, i, rows):
        return proj[member, i, rows, :part] * proj[member, i, rows, 2 * part :]

    last = slice(piece - 2, piece)
    for yy in (0, 1):
        chips[yy * 2 + 1].wait()

        def second(core, _):
            member = (yy * 2 + 1) * 2 + core
            project(member)
            for i in (0, 1):
                ends[(yy * 2 + core) * 2 + i] = inner(member, i, last)
            return 0

        lax.fori_loop(0, 2, second, 0)
    to_next = remote(ends, before, ends_sem.at[0], ends_sem.at[1], after)
    to_next.start()
    for yy in (0, 1):
        chips[yy * 2].wait()

        def first(core, _):
            project((yy * 2) * 2 + core)
            return 0

        lax.fori_loop(0, 2, first, 0)
        if yy == 0:
            whole.forward()
    whole.second()
    saved.append(pltpu.make_async_copy(proj, proj_out, local.at[6]))
    saved.append(pltpu.make_async_copy(every, normed_out, local.at[10]))
    for copy in saved:
        copy.start()

    def convolve(member, i, start):
        tall[6:8, :] = start
        now = inner(member, i, slice(0, piece))
        tall[8 : 8 + piece, :] = now
        value = taps[0:1] * tall[6 : 6 + piece, :] + taps[1:2] * tall[7 : 7 + piece, :]
        value += taps[2:3] * now
        conv[member, i] = value
        gate = proj[member, i, :, part : 2 * part]
        gated[member, i] = (gate * value).astype(BF16)

    def right_half(n, _):
        member = (n // 2) * 4 + 2 + n % 2
        for i in (0, 1):
            convolve(member, i, inner(member - 2, i, last))
        return 0

    lax.fori_loop(0, 4, right_half, 0)
    whole.last()
    to_next.wait_recv()

    def left_half(n, _):
        member = (n // 2) * 4 + n % 2
        for i in (0, 1):
            start = before[n * 2 + i]
            convolve(member, i, jnp.where(z > 0, start, jnp.zeros_like(start)))
        return 0

    lax.fori_loop(0, 4, left_half, 0)
    swapped = [pltpu.make_async_copy(gated.at[me], got.at[me], local.at[12])]
    for f, peer in enumerate(others()):
        to = (peer["y"] * 2 + peer["x"]) * 2 + peer["core"]
        swapped.append(remote(gated.at[to], got.at[me], send_s.at[f], recv_s.at[f], peer))
    for copy in swapped:
        copy.start()
    for n, (src, dst) in enumerate(((conv, conv_out), (gated, gated_out))):
        saved.append(pltpu.make_async_copy(src, dst, local.at[7 + n]))
        saved[-1].start()
    whole.arrived(*range(6, 14))
    whole.sent()
    own_right.wait()
    for copy in swapped:
        copy.wait()
    third = width // 3

    def mix(n, _):
        columns = pl.ds(pl.multiple_of(n * third, third), third)
        total = tokens[:, :, columns].astype(F32).reshape(2 * piece, third)
        for member in range(8):
            left = got[member].reshape(2 * piece, part)
            total += times(left, rights[member, :, :, columns].reshape(part, third))
        out[:, :, columns] = total.reshape(2, piece, third)
        return 0

    lax.fori_loop(0, 3, mix, 0)

    def work(i, rows):
        own[i, rows, :] = (rms_parts(out[i, rows, :])[0] * gain[1:2, :]).astype(BF16)

    by_rows(piece, work)
    gather = Gather(own, normed_two, send, recv)
    gather.first()
    mine = pltpu.make_async_copy(own, normed_two.at[(y * 2 + x) * 2 + c], local.at[9])
    mine.start()
    saved.append(mine)
    gather.forward()
    gather.second()
    gather.last()
    gather.arrived(*range(6, 14))
    gather.sent()
    to_next.wait_send()
    for copy in saved:
        copy.wait()


def mixer_forward(planes, tokens_all, gathered, taps, blocks, tokens, gain, collective_id):
    _, _, piece, width = tokens_all.shape
    part = blocks.shape[1] * planes
    saved = [
        (tokens_all.shape, BF16),
        (tokens_all.shape, BF16),
        ((8, 2, piece, 3 * part), F32),
        ((8, 2, piece, part), F32),
        ((8, 2, piece, part), BF16),
        ((width, 3 * part), BF16),
    ]
    return pl.pallas_call(
        functools.partial(mixer_kernel, planes),
        out_shape=[jax.ShapeDtypeStruct((2, piece, width), F32)]
        + [jax.ShapeDtypeStruct(*item) for item in saved]
        + [jax.ShapeDtypeStruct((2, part // 2, width), BF16)],
        in_specs=[ANY, ANY] + [VMEM] * 4,
        out_specs=[VMEM] + [ANY] * 6 + [VMEM],
        scratch_shapes=[
            pltpu.VMEM((part, width), F32),
            pltpu.VMEM((2, piece, width), BF16),
            pltpu.VMEM((8, 2, piece, width), BF16),
            pltpu.VMEM((width, 3 * part), BF16),
            pltpu.VMEM((8, 2, piece, 3 * part), F32),
            pltpu.VMEM((8, 2, piece, part), F32),
            pltpu.VMEM((8, 2, piece, part), BF16),
            pltpu.VMEM((8 + piece, part), F32),
            pltpu.VMEM((8, 2, part), F32),
            pltpu.VMEM((8, 2, part), F32),
            sems(13),
            sems(2),
            sems(14),
            sems(14),
            pltpu.VMEM((8, 2, part // 2, width), BF16),
            pltpu.VMEM((8, 2, piece, part), BF16),
            sems(14),
            sems(14),
            sems(7),
            sems(7),
        ],
        cost_estimate=cost(95),
        compiler_params=params(collective_id, 60),
    )(tokens_all, gathered, taps, blocks, tokens, gain)


def branch_kernel(
    planes,
    active_in,
    down_in,
    own,
    right,
    proj_in,
    conv_in,
    gated_in,
    normed,
    taps,
    out,
    dmix,
    dproj,
    grad_in,
    grad_out,
    grad_taps,
    near,
    active,
    down,
    gated,
    proj,
    conv,
    tall,
    starts,
    beyond,
    total_out,
    total_in,
    near_sem,
    local,
    ends_sem,
    send,
    recv,
    *scratch,
):
    y, c, z, x = place()
    _, _, piece, part = conv.shape
    width = out.shape[2]
    chips = [flip(y, dy) * 2 + flip(x, dx) for dy, dx in ((0, 0), (0, 1), (1, 0), (1, 1))]
    half = 2 * piece

    def fetch(source, k):
        copy = pltpu.make_async_copy(
            source.at[pl.ds(chips[k] * 2, 2)], near.at[k % 2], near_sem.at[k % 2]
        )
        copy.start()
        return copy

    after, prior = ring()
    meet(neighbours() + [after, prior])
    gather = Gather(own, dmix, send, recv)
    gather.first()
    mine = pltpu.make_async_copy(own, dmix.at[(y * 2 + x) * 2 + c], local.at[5])
    mine.start()
    pairs = [(active_in, active), (down_in, down), (proj_in, proj), (conv_in, conv)]
    loads = load(pairs + [(gated_in, gated)], local)
    to_prior = remote(starts.at[0], beyond, ends_sem.at[0], ends_sem.at[1], prior)
    grad_taps[...] = jnp.zeros_like(grad_taps)
    third = width // 3

    def gradients(k):
        chip, other = chips[k], flip(x, k % 2)

        def body(core, _):
            member = chip * 2 + core
            grad = times_t(near[k % 2, core].reshape(half, width), right[...])
            grad = grad.reshape(2, piece, part)
            for i in (0, 1):
                dproj[member, i, :, part : 2 * part] = (grad[i] * conv[member, i]).astype(BF16)
                dconv = grad[i] * proj[member, i, :, part : 2 * part]
                conv[member, i] = dconv
                starts[other, (flip(y, k // 2) * 2 + core) * 2 + i] = dconv[:2]
            return 0

        lax.fori_loop(0, 2, body, 0)

        def sum_up(n, _):
            columns = pl.ds(pl.multiple_of(n * third, third), third)
            left = gated[pl.ds(chip * 2, 2)].reshape(2 * half, part)
            product = t_times(left, near[k % 2, :, :, :, columns].reshape(2 * half, third))
            if k == 0:
                total_out[:, columns] = product
            elif k < 3:
                total_out[:, columns] += product
            else:
                product = total_out[:, columns] + product
                own_rows = part // planes
                for zz in range(planes):
                    block = product[zz * own_rows : (zz + 1) * own_rows]
                    grad_out[zz, :, columns] = block.astype(BF16)
            return 0

        lax.fori_loop(0, 3, sum_up, 0)

    def through(member, i, end):
        tall[0:piece, :] = conv[member, i]
        tall[piece : piece + 2, :] = end
        now, one, two = conv[member, i], tall[1 : piece + 1, :], tall[2 : piece + 2, :]
        b_part, x_part = proj[member, i, :, :part], proj[member, i, :, 2 * part :]
        dmixed = taps[2:3] * now + taps[1:2] * one + taps[0:1] * two
        dproj[member, i, :, :part] = (dmixed * x_part).astype(BF16)
        dproj[member, i, :, 2 * part :] = (dmixed * b_part).astype(BF16)
        mixed = b_part * x_part
        for k, shifted in enumerate((two, one, now)):
            grad_taps[k : k + 1, :] += jnp.sum(mixed * shifted, axis=0, keepdims=True)

    def left_half(n, _):
        member = (n // 2) * 4 + n % 2
        for i in (0, 1):
            through(member, i, conv[member + 2, i, 0:2, :])
        return 0

    def right_half(n, _):
        member = (n // 2) * 4 + 2 + n % 2
        for i in (0, 1):
            end = beyond[n * 2 + i]
            through(member, i, jnp.where(z < planes - 1, end, jnp.zeros_like(end)))
        return 0

    def one():
        for copy in loads[2:]:
            copy.wait()
        mine.wait()
        gather.arrived(6, 7)
        fetch(dmix, 0).wait()
        gradients(0)
        gather.second()
        gather.arrived(8, 9)
        fetched = fetch(dmix, 1)
        gather.arrived(10, 11)
        following = fetch(dmix, 2)
        fetched.wait()
        gradients(1)
        following.wait()
        gradients(2)

    def one_more():
        gather.last()
        gather.arrived(12, 13)
        fetch(dmix, 3).wait()
        to_normed.append(fetch(normed, 0))
        gradients(3)
        to_normed.append(fetch(normed, 1))
        to_prior.start()
        lax.fori_loop(0, 4, left_half, 0)

    quarter = width // 4

    def two():
        one_more()
        to_prior.wait_recv()
        lax.fori_loop(0, 4, right_half, 0)
        for k in range(4):
            to_normed[k].wait()

            def sum_up(q, _):
                columns = pl.ds(pl.multiple_of(q * quarter, quarter), quarter)
                left = near[k % 2, :, :, :, columns].reshape(2 * half, quarter)
                right_side = dproj[pl.ds(chips[k] * 2, 2)].reshape(2 * half, 3 * part)
                product = t_times(left, right_side)
                if k == 0:
                    total_in[columns, :] = product
                elif k < 3:
                    total_in[columns, :] += product
                else:
                    product = (total_in[columns, :] + product).astype(BF16)
                    if len(grad_in.shape) == 2:
                        grad_in[columns, :] = product
                        return 0
                    own_rows = grad_in.shape[2]
                    for zz in range(planes):
                        for xx in (0, 1):
                            start = (zz * 2 + xx) * own_rows
                            grad_in[zz, q * 2 + xx] = product[start : start + own_rows]
                return 0

            lax.fori_loop(0, 4, sum_up, 0)
            if k < 2:
                to_normed.append(fetch(normed, k + 2))

    to_normed = []
    gather.forward()
    loads[0].wait()
    loads[1].wait()
    scatter([active], [down], False, out, scratch, (one, two))
    gather.sent()
    to_prior.wait_send()


def branch_forward(
    planes, active, down, dmix, right, proj, conv, gated, normed, taps, in_shape, collective_id
):
    _, piece, width = dmix.shape
    part = right.shape[0]
    outs = [
        ((2, piece, width), F32),
        (normed.shape, BF16),
        ((8, 2, piece, 3 * part), BF16),
        (in_shape, BF16),
        ((planes, part // planes, width), BF16),
        ((3, part), F32),
    ]
    got = pl.pallas_call(
        functools.partial(branch_kernel, planes),
        out_shape=[jax.ShapeDtypeStruct(*item) for item in outs],
        in_specs=[ANY, ANY, ANY, VMEM, ANY, ANY, ANY, ANY, VMEM],
        out_specs=[VMEM, ANY] + [VMEM] * 4,
        scratch_shapes=[
            pltpu.VMEM((2, 2, 2, piece, width), BF16),
            pltpu.VMEM(active.shape, BF16),
            pltpu.VMEM(down.shape, BF16),
            pltpu.VMEM(gated.shape, BF16),
            pltpu.VMEM((8, 2, piece, 3 * part), F32),
            pltpu.VMEM((8, 2, piece, part), F32),
            pltpu.VMEM((8 + piece, part), F32),
            pltpu.VMEM((2, 8, 2, part), F32),
            pltpu.VMEM((8, 2, part), F32),
            pltpu.VMEM((part, width), F32),
            pltpu.VMEM((width, 3 * part), F32),
            sems(2),
            sems(6),
            sems(2),
            sems(14),
            sems(14),
        ]
        + room(piece, width),
        cost_estimate=cost(90),
        compiler_params=params(collective_id, 62),
    )(active, down, dmix, right, proj, conv, gated, normed, taps)
    return got[:1] + got[2:]


def update_kernel(planes, three, rate, decay, got, weight, first, second, grad, moment, updated):
    wide = got.shape[-1] // planes
    parts = 1
    if three:
        wide, parts = wide // 3, 3
    for k in range(parts):
        for owner in range(8 * planes):
            pair, z, xx = owner // (2 * planes), owner // 2 % planes, owner % 2
            start = (k * planes + z) * wide
            to = (k * 8 * planes + owner) * wide
            if three:
                value = got[pair * 2 + xx, :, start : start + wide]
            else:
                value = got[pair * 2 + xx, 0, :, start : start + wide]
            if three:
                grad[:, to : to + wide] = value.astype(F32)
            else:
                grad[0, :, to : to + wide] = value.astype(F32)
    moment[...], updated[...] = adamw(
        weight[...], first[...], second[...], grad[...], rate, decay
    )


def update(planes, got, weight, first, second, rate, decay):
    three = weight.ndim == 2
    rows = weight.shape[-2]
    step = 16 if rows % 16 == 0 else rows
    part = got.shape[-1]
    columns = weight.shape[-1]
    if three:
        grid = (rows // step,)
        got_spec = pl.BlockSpec((8, step, part), lambda n: (0, n, 0))
        spec = pl.BlockSpec((step, columns), lambda n: (n, 0))
    else:
        grid = (2, rows // step)
        got_spec = pl.BlockSpec((8, 1, step, part), lambda j, n: (0, j, n, 0))
        spec = pl.BlockSpec((1, step, columns), lambda j, n: (j, n, 0))
    size = weight.size * 4
    return pl.pallas_call(
        functools.partial(update_kernel, planes, three, rate, decay),
        out_shape=[jax.ShapeDtypeStruct(weight.shape, F32)] * 3,
        grid=grid,
        in_specs=[got_spec, spec, spec, spec],
        out_specs=[spec] * 3,
        cost_estimate=pl.CostEstimate(
            flops=12 * size, bytes_accessed=7 * size, transcendentals=0
        ),
        compiler_params=pltpu.CompilerParams(vmem_limit_bytes=32 * 2**20),
    )(got, weight, first, second)


def rms_parts(values):
    scale = lax.rsqrt(jnp.mean(values * values, axis=-1, keepdims=True) + 1e-05)
    return (values * scale, scale)


def rms_back(grad_hat, normal, scale):
    return scale * (grad_hat - normal * jnp.mean(grad_hat * normal, axis=-1, keepdims=True))


def times(left, right):
    return jnp.dot(left, right, preferred_element_type=F32)


def times_t(left, right):
    return lax.dot_general(left, right, (((1,), (1,)), ((), ())), preferred_element_type=F32)


def t_times(left, right):
    return lax.dot_general(left, right, (((0,), (0,)), ((), ())), preferred_element_type=F32)


def adamw(weight, first_mom, second_mom, gradient, rate, decay):
    bias_one = 1.0 - 0.9**STEP
    bias_two = 1.0 - 0.95**STEP
    first_new = 0.9 * first_mom + 0.1 * gradient
    second_new = 0.95 * second_mom + 0.05 * gradient * gradient
    direction = first_new / bias_one / (jnp.sqrt(second_new / bias_two) + 1e-08)
    return (second_new, weight - rate * (direction + decay * weight))


def on_device(
    tokens,
    cotangent,
    norm_gains,
    in_proj,
    conv_taps,
    out_proj,
    gate_up,
    down_proj,
    first_gains,
    first_in,
    first_conv,
    first_out,
    first_gate_up,
    first_down,
    second_gains,
    second_in,
    second_conv,
    second_out,
    second_gate_up,
    second_down,
):
    planes = lax.axis_size("z")
    seqs, piece, width = tokens.shape
    rows = seqs * piece
    all_rows = 8 * rows
    own_d = in_proj.shape[0]
    own_f = down_proj.shape[0]
    ff = gate_up.shape[2]
    part_d = width // 8
    part_f = ff // 8

    in_tiles = own_d % 16 == 0

    def along_z(value):
        return lax.all_gather(value, "z", axis=0, tiled=False)

    most = width // 3 * 2
    down_low = down_proj.astype(BF16)
    down_most = along_z(down_low[:, :most]).reshape(part_f, most)
    small = jnp.concatenate([norm_gains, conv_taps], axis=0)
    tokens_all, gu_mine, in_t, out_blocks, gains, taps = early(
        planes, small, tokens, in_proj, gate_up, out_proj, 0
    )
    if not in_tiles:
        in_t = in_t.reshape(planes, 4, 2, own_d, 3 * part_d).transpose(1, 0, 2, 3, 4)
        in_t = in_t.reshape(width, 3 * part_d)
    gu_t = along_z(gu_mine)
    if not in_tiles:
        gu_t = gu_t.reshape(planes, 4, 2, 2, own_d, part_f).transpose(3, 1, 0, 2, 4, 5)
        gu_t = gu_t.reshape(2, width, part_f)

    middle, normed_two_all, normed_all, proj, conv, gated, in_whole, out_t = mixer_forward(
        planes, tokens_all, in_t, taps, out_blocks, tokens, gains, 2
    )
    out_t = out_t.reshape(part_d, width)
    active, dgate, dup, grad_down, down_t = ffn(
        planes, cotangent, normed_two_all, gu_t, down_most, down_low[:, most:], 4
    )

    def sum_z(value):
        return lax.psum_scatter(value, "z", scatter_dimension=0, tiled=False)

    g_down = sum_z(grad_down)
    grad_gu, dmiddle, dmix, gain_two = ffn_back(
        planes, dgate, dup, gu_t, normed_two_all, middle, cotangent, gains[1:], 5
    )
    if not in_tiles:
        grad_gu = grad_gu.reshape(2, 4, planes, 2, own_d, part_f).transpose(2, 1, 3, 0, 4, 5)
        grad_gu = grad_gu.reshape(planes, 8, 2, own_d, part_f)
    grad_gu, g_down = lax.optimization_barrier((grad_gu, g_down))
    g_down = g_down.astype(F32)
    gu_back = sum_z(grad_gu)

    branch, dproj, grad_in, grad_out, grad_taps = branch_forward(
        planes,
        active,
        down_t,
        dmix,
        out_t,
        proj,
        conv,
        gated,
        normed_all,
        taps,
        in_t.shape,
        7,
    )
    block_out = (middle + branch).astype(BF16)
    if not in_tiles:
        grad_in = grad_in.reshape(4, planes, 2, own_d, 3 * part_d).transpose(1, 0, 2, 3, 4)
        grad_in = grad_in.reshape(planes, 8, own_d, 3 * part_d)
    taps_parts = grad_taps.reshape(3, planes, own_d).transpose(1, 0, 2)

    token_grad, gain_one, in_back = last(
        planes, dproj, in_whole, tokens, dmiddle, grad_in, gains[:1], 8
    )
    grad_gains = jnp.stack([jnp.sum(gain_one, axis=0), jnp.sum(gain_two, axis=0)])
    gains_parts = grad_gains.reshape(2, 4, planes, 2, own_d).transpose(1, 3, 2, 0, 4)
    gains_parts = gains_parts.reshape(8, planes, 2, own_d)
    in_got, gu_got, sums, g_out = finish(
        planes, in_back, gu_back, gains_parts, taps_parts, grad_out, 9
    )
    g_gains, g_conv = sums[:2], sums[2:]
    m_gains, u_gains = adamw(norm_gains, first_gains, second_gains, g_gains, 0.4, 0.0)
    g_in, m_in, u_in = update(planes, in_got, in_proj, first_in, second_in, 0.02, 0.1)
    m_conv, u_conv = adamw(conv_taps, first_conv, second_conv, g_conv, 0.2, 0.1)
    m_out, u_out = adamw(out_proj, first_out, second_out, g_out, 0.02, 0.1)
    g_gu, m_gu, u_gu = update(
        planes, gu_got, gate_up, first_gate_up, second_gate_up, 0.02, 0.1
    )
    m_down, u_down = adamw(down_proj, first_down, second_down, g_down, 0.01, 0.1)
    return (
        block_out,
        token_grad,
        g_gains,
        g_in,
        g_conv,
        g_out,
        g_gu,
        g_down,
        m_gains,
        m_in,
        m_conv,
        m_out,
        m_gu,
        m_down,
        u_gains,
        u_in,
        u_conv,
        u_out,
        u_gu,
        u_down,
    )


def solution(mesh):
    lines = mesh.shape["seq"] // 2
    fine = Mesh(mesh.devices.reshape(2, 2, lines, 2), ("y", "core", "z", "x"))
    dp, seq = ("y", "core"), ("z", "x")
    every = dp + seq
    tokens = P(dp, seq, None)
    weights = (
        P(None, every),
        P(every, None),
        P(None, every),
        P(every, None),
        P(None, every, None),
        P(every, None),
    )
    return jax.shard_map(
        on_device,
        mesh=fine,
        in_specs=(tokens, tokens) + weights * 3,
        out_specs=(tokens, tokens) + weights * 3,
        check_vma=False,
    )
```

```python
import functools

import jax
import jax.numpy as jnp
from jax import lax
from jax.experimental import pallas as pl
from jax.experimental.pallas import tpu as pltpu
from jax.sharding import Mesh
from jax.sharding import PartitionSpec as P

STEP = 10
MESH = pl.DeviceIdType.MESH
BF16 = jnp.bfloat16
F32 = jnp.float32
FLIPS = [(dy, dc, dx) for dy in (0, 1) for dc in (0, 1) for dx in (0, 1)][1:]
ANY = pl.BlockSpec(memory_space=pl.ANY)
VMEM = pl.BlockSpec(memory_space=pltpu.VMEM)


def place():
    return tuple(lax.axis_index(a) for a in ("y", "core", "z", "x"))


def flip(value, by):
    return 1 - value if by else value


def remote(src, dst, send, recv, device):
    return pltpu.make_async_remote_copy(
        src_ref=src,
        dst_ref=dst,
        send_sem=send,
        recv_sem=recv,
        device_id=device,
        device_id_type=MESH,
    )


def meet(peers):
    barrier = pltpu.get_barrier_semaphore()
    for peer in peers:
        pl.semaphore_signal(barrier, inc=1, device_id=peer, device_id_type=MESH)
    pl.semaphore_wait(barrier, len(peers))


class Gather:
    def __init__(self, own, full, send, recv, base=0):
        self.own, self.full, self.send, self.recv, self.base = own, full, send, recv, base
        self.started = []

    def go(self, src, slot, sem, device):
        sem = self.base + sem
        copy = remote(
            src, self.full.at[slot[0], slot[1]], self.send.at[sem], self.recv.at[sem], device
        )
        copy.start()
        self.started.append(copy)

    def first(self):
        y, c, _, x = place()
        me = (y * 2 + x) * 2 + c
        for i, j in ((0, 1), (1, 0)):
            self.go(self.own.at[i], (me, i), i, {"x": 1 - x})
            self.go(self.own.at[j], (me, j), 2 + j, {"y": 1 - y})
        for i in (0, 1):
            self.go(self.own.at[i], (me, i), 6 + i, {"core": 1 - c})

    def arrived(self, *sems):
        for sem in sems:
            done = self.recv.at[self.base + sem]
            pltpu.make_async_copy(self.own.at[0], self.own.at[0], done).wait()

    def pass_on(self, dy, dx, i, sem, device):
        y, c, _, x = place()
        slot = ((flip(y, dy) * 2 + flip(x, dx)) * 2 + c, i)
        self.go(self.full.at[slot[0], slot[1]], slot, sem, device)

    def forward(self):
        y, c, _, x = place()
        self.arrived(0)
        self.pass_on(0, 1, 0, 4, {"y": 1 - y})
        self.pass_on(0, 1, 0, 8, {"core": 1 - c})
        self.arrived(3)
        self.pass_on(1, 0, 1, 5, {"x": 1 - x})
        self.pass_on(1, 0, 1, 11, {"core": 1 - c})

    def second(self):
        _, c, _, _ = place()
        self.arrived(1)
        self.pass_on(0, 1, 1, 9, {"core": 1 - c})
        self.arrived(2)
        self.pass_on(1, 0, 0, 10, {"core": 1 - c})

    def last(self):
        _, c, _, _ = place()
        self.arrived(4)
        self.pass_on(1, 1, 0, 12, {"core": 1 - c})
        self.arrived(5)
        self.pass_on(1, 1, 1, 13, {"core": 1 - c})

    def sent(self):
        for copy in self.started:
            copy.wait_send()


def neighbours():
    y, c, _, x = place()
    return [{"x": 1 - x}, {"y": 1 - y}, {"core": 1 - c}]


def others():
    y, c, _, x = place()
    return [{"y": flip(y, dy), "core": flip(c, dc), "x": flip(x, dx)} for dy, dc, dx in FLIPS]


def swap(src, dst, send, recv, local):
    y, c, _, x = place()
    me = (y * 2 + c) * 2 + x
    copies = []
    for f, peer in enumerate(others()):
        to = (peer["y"] * 2 + peer["core"]) * 2 + peer["x"]
        copies.append(remote(src.at[to], dst.at[me], send.at[f], recv.at[f], peer))
    copies.append(pltpu.make_async_copy(src.at[me], dst.at[me], local))
    for copy in copies:
        copy.start()
    return copies


def along_line(planes, own, full, send, recv, local):
    z = lax.axis_index("z")
    copies = [
        remote(own, full.at[z], send.at[d], recv.at[d], peer)
        for d, peer in enumerate(line_peers(planes))
    ]
    copies.append(pltpu.make_async_copy(own, full.at[z], local))
    for copy in copies:
        copy.start()
    return copies


def line_peers(planes):
    return [{"z": lax.rem(lax.axis_index("z") + d, planes)} for d in range(1, planes)]


class Line:
    def __init__(self, planes, own, full, send, recv, local):
        self.planes, self.own, self.full, self.send, self.recv = planes, own, full, send, recv
        self.mine = pltpu.make_async_copy(own, full.at[lax.axis_index("z")], local)

    def ways(self):
        z, planes = lax.axis_index("z"), self.planes
        return (
            (0, 1, z, planes - 1 - z),
            (1, planes - 1, planes - 1 - z, z),
        )

    def pass_on(self, d):
        z, planes = lax.axis_index("z"), self.planes
        for way, by, come, left in self.ways():
            block = lax.rem(z + d * (planes - by) + planes, planes)

            @pl.when(jnp.logical_and(come >= d, left >= 1))
            def _():
                src = self.own if d == 0 else self.full.at[block]
                device = {"z": lax.rem(z + by, planes)}
                sem = self.send.at[way, d], self.recv.at[way, d]
                remote(src, self.full.at[block], *sem, device).start()

    def start(self):
        self.mine.start()
        self.pass_on(0)

    def arrived(self, d):
        for way, _, come, _ in self.ways():

            @pl.when(come >= d)
            def _():
                pltpu.make_async_copy(self.own, self.own, self.recv.at[way, d - 1]).wait()

    def step(self, d):
        self.arrived(d)
        self.pass_on(d)

    def finish(self):
        self.arrived(self.planes - 1)
        for d in range(self.planes - 1):
            for way, _, come, left in self.ways():

                @pl.when(jnp.logical_and(come >= d, left >= 1))
                def _():
                    pltpu.make_async_copy(self.own, self.own, self.send.at[way, d]).wait()

        self.mine.wait()


def gather_kernel(own, full, send, recv, local):
    y, c, _, x = place()
    meet(neighbours())
    gather = Gather(own, full, send, recv)
    gather.first()
    mine = pltpu.make_async_copy(own, full.at[(y * 2 + x) * 2 + c], local)
    mine.start()
    gather.forward()
    gather.second()
    gather.last()
    gather.arrived(*range(6, 14))
    gather.sent()
    mine.wait()


def by_owner(planes):
    for owner in range(8 * planes):
        yield owner, owner // (2 * planes) * 2 + owner % 2, owner // 2 % planes


def early_kernel(
    planes,
    small,
    tokens,
    in_proj,
    gate_up,
    out_proj,
    full,
    gu_got,
    ins,
    outs,
    gains,
    taps,
    in_block,
    in_got,
    gu_block,
    out_block,
    line,
    smalls,
    send,
    recv,
    send_i,
    recv_i,
    send_g,
    recv_g,
    send_s,
    recv_s,
    send_z,
    recv_z,
    send_l,
    recv_l,
    local,
):
    y, c, z, x = place()
    me = (y * 2 + c) * 2 + x
    own = small.shape[1]
    meet(others() + line_peers(planes))
    tiny = along_line(planes, small, line, send_z, recv_z, local.at[0])
    out_block[...] = out_proj[...].astype(BF16)
    out_line = Line(planes, out_block, outs, send_l.at[1], recv_l.at[1], local.at[4])
    out_line.start()
    for k in range(3):
        for owner, member, zz in by_owner(planes):
            start, to = (k * 8 * planes + owner) * own, (k * planes + zz) * own
            block = in_proj[:, start : start + own].astype(BF16)
            in_block[member, :, to : to + own] = block
    in_copies = swap(in_block, in_got, send_i, recv_i, local.at[1])
    gather = Gather(tokens, full, send, recv)
    gather.first()
    mine = pltpu.make_async_copy(tokens, full.at[(y * 2 + x) * 2 + c], local.at[2])
    mine.start()
    for copy in tiny:
        copy.wait()
    tiny = []
    for f, peer in enumerate(others()):
        tiny.append(remote(line, smalls.at[me], send_s.at[f], recv_s.at[f], peer))
    tiny.append(pltpu.make_async_copy(line, smalls.at[me], local.at[0]))
    for copy in tiny:
        copy.start()
    for copy in in_copies:
        copy.wait()
    ahead = Line(planes, in_got, ins, send_l.at[0], recv_l.at[0], local.at[1])
    ahead.start()
    if planes > 2:
        out_line.step(1)
    wide = gate_up.shape[2] // (8 * planes)
    for j in (0, 1):
        for owner, member, zz in by_owner(planes):
            block = gate_up[j, :, owner * wide : (owner + 1) * wide].astype(BF16)
            gu_block[member, j, :, zz * wide : (zz + 1) * wide] = block
    gu_copies = swap(gu_block, gu_got, send_g, recv_g, local.at[3])
    for copy in tiny:
        copy.wait()
    for owner, member, zz in by_owner(planes):
        row = smalls[member, zz, 0:2, :].astype(BF16).astype(F32)
        gains[:, owner * own : (owner + 1) * own] = row
    for zz in range(planes):
        row = line[zz, 2:5, :].astype(BF16).astype(F32)
        taps[:, zz * own : (zz + 1) * own] = row
    ahead.step(1)
    gather.forward()
    for d in range(2, planes - 1):
        out_line.step(d)
        ahead.step(d)
    gather.second()
    gather.last()
    gather.arrived(*range(6, 14))
    gather.sent()
    for copy in gu_copies:
        copy.wait()
    mine.wait()
    ahead.finish()
    out_line.finish()


def params(collective_id, vmem=0):
    more = {"vmem_limit_bytes": vmem * 2**20} if vmem else {}
    return pltpu.CompilerParams(collective_id=collective_id, has_side_effects=True, **more)


def cost(micros):
    return pl.CostEstimate(flops=int(micros * 1e9), bytes_accessed=0, transcendentals=0)


def sems(*shape):
    return pltpu.SemaphoreType.DMA(shape)


def plane_gather(own, collective_id):
    return pl.pallas_call(
        gather_kernel,
        out_shape=jax.ShapeDtypeStruct((8,) + own.shape, own.dtype),
        in_specs=[ANY],
        out_specs=ANY,
        scratch_shapes=[sems(14), sems(14), pltpu.SemaphoreType.DMA],
        cost_estimate=cost(45),
        compiler_params=params(collective_id),
    )(own)


def early(planes, small, tokens, in_proj, gate_up, out_proj, collective_id):
    own, width = out_proj.shape
    in_block = (8, own, in_proj.shape[1] // 8)
    gu_block = (8, 2, own, gate_up.shape[2] // 8)
    return pl.pallas_call(
        functools.partial(early_kernel, planes),
        out_shape=[
            jax.ShapeDtypeStruct((8,) + tokens.shape, BF16),
            jax.ShapeDtypeStruct(gu_block, BF16),
            jax.ShapeDtypeStruct((planes,) + in_block, BF16),
            jax.ShapeDtypeStruct((planes, own, width), BF16),
            jax.ShapeDtypeStruct((2, width), F32),
            jax.ShapeDtypeStruct((3, planes * own), F32),
        ],
        in_specs=[VMEM, ANY, VMEM, VMEM, VMEM],
        out_specs=[ANY] * 4 + [VMEM] * 2,
        scratch_shapes=[
            pltpu.VMEM(in_block, BF16),
            pltpu.VMEM(in_block, BF16),
            pltpu.VMEM(gu_block, BF16),
            pltpu.VMEM((own, width), BF16),
            pltpu.VMEM((planes,) + small.shape, F32),
            pltpu.VMEM((8, planes) + small.shape, F32),
            sems(14),
            sems(14),
            sems(7),
            sems(7),
            sems(7),
            sems(7),
            sems(7),
            sems(7),
            sems(planes - 1),
            sems(planes - 1),
            sems(2, 2, planes - 1),
            sems(2, 2, planes - 1),
            sems(5),
        ],
        cost_estimate=cost(70),
        compiler_params=params(collective_id, 40),
    )(small, tokens, in_proj, gate_up, out_proj)


def finish_kernel(planes, ins, gus, gains, taps, outs, ins_got, gus_got, sums, out_sum, *scratch):
    parts, terms, got, outs_got, send, recv, send_g, recv_g = scratch[:8]
    send_z, recv_z, send_o, recv_o, local = scratch[8:]
    meet(others() + line_peers(planes))
    small = swap(gains, parts, send_g, recv_g, local.at[0])
    large = scatter_line(planes, outs, outs_got, send_o, recv_o, local.at[3])
    copies = swap(ins, ins_got, send.at[0], recv.at[0], local.at[1])
    copies += swap(gus, gus_got, send.at[1], recv.at[1], local.at[2])
    for copy in small:
        copy.wait()
    terms[:, 0:2, :] = jnp.sum(parts[...], axis=0)
    terms[:, 2:5, :] = taps[...]
    for copy in scatter_line(planes, terms, got, send_z, recv_z, local.at[0]):
        copy.wait()
    sums[...] = jnp.sum(got[...], axis=0)
    for copy in large:
        copy.wait()
    total = outs_got[0].astype(F32)
    for k in range(1, planes):
        total += outs_got[k].astype(F32)
    out_sum[...] = total
    for copy in copies:
        copy.wait()


def scatter_line(planes, terms, got, send, recv, local):
    z = lax.axis_index("z")
    copies = [
        remote(terms.at[peer["z"]], got.at[z], send.at[d], recv.at[d], peer)
        for d, peer in enumerate(line_peers(planes))
    ]
    copies.append(pltpu.make_async_copy(terms.at[z], got.at[z], local))
    for copy in copies:
        copy.start()
    return copies


def finish(planes, ins, gus, gains, taps, outs, collective_id):
    own = gains.shape[-1]
    return pl.pallas_call(
        functools.partial(finish_kernel, planes),
        out_shape=[
            jax.ShapeDtypeStruct(ins.shape, ins.dtype),
            jax.ShapeDtypeStruct(gus.shape, gus.dtype),
            jax.ShapeDtypeStruct((5, own), F32),
            jax.ShapeDtypeStruct(outs.shape[1:], F32),
        ],
        in_specs=[ANY, ANY, VMEM, VMEM, VMEM],
        out_specs=[ANY, ANY, VMEM, VMEM],
        scratch_shapes=[
            pltpu.VMEM(gains.shape, F32),
            pltpu.VMEM((planes, 5, own), F32),
            pltpu.VMEM((planes, 5, own), F32),
            pltpu.VMEM(outs.shape, BF16),
            sems(2, 7),
            sems(2, 7),
            sems(7),
            sems(7),
            sems(planes - 1),
            sems(planes - 1),
            sems(planes - 1),
            sems(planes - 1),
            sems(4),
        ],
        cost_estimate=cost(25),
        compiler_params=params(collective_id),
    )(ins, gus, gains, taps, outs)


def load_rows(planes, gathered, rows, sem):
    if len(gathered.shape) == 3:
        copy = pltpu.make_async_copy(gathered, rows, sem)
        copy.start()
        return [copy]
    own = gathered.shape[3]
    copies = []
    for z in range(planes):
        for m in range(8):
            start = (((m // 2) * planes + z) * 2 + m % 2) * own
            for j in (0, 1):
                src = gathered.at[z, m, j]
                copies.append(pltpu.make_async_copy(src, rows.at[j, pl.ds(start, own)], sem))
    for copy in copies:
        copy.start()
    return copies


def ffn_kernel(
    planes,
    cot,
    normed,
    gathered,
    down_most,
    down_own,
    act_out,
    dgate_out,
    dup_out,
    grad_out,
    down,
    down_rest,
    down_rows,
    full,
    near,
    weights,
    gates,
    ups,
    staged,
    total,
    send,
    recv,
    local,
    near_sem,
    out_sem,
    send_l,
    recv_l,
):
    y, c, _, x = place()
    piece, width = cot.shape[1:]
    part = down.shape[0]
    most = down_most.shape[1]
    chip_rows = 4 * piece
    half = 2 * piece
    chips = [flip(y, dy) * 2 + flip(x, dx) for dy, dx in ((0, 0), (0, 1), (1, 0), (1, 1))]
    loads = load_rows(planes, gathered, weights, local.at[0])
    mine = pltpu.make_async_copy(cot, full.at[(y * 2 + x) * 2 + c], local.at[1])
    mine.start()
    first_part = pltpu.make_async_copy(down_most, down.at[:, pl.ds(0, most)], local.at[2])

    def fetch(k):
        copy = pltpu.make_async_copy(
            normed.at[pl.ds(chips[k] * 2, 2)], near.at[k % 2], near_sem.at[k % 2]
        )
        copy.start()
        return copy

    fetched = {0: fetch(0), 1: fetch(1)}
    first_part.start()
    meet(neighbours() + list(ring()))
    ahead = Line(planes, down_own, down_rest, send_l, recv_l, local.at[3])
    ahead.start()
    gather = Gather(cot, full, send, recv)
    gather.first()
    for copy in loads:
        copy.wait()

    def gate_up(k, slot):
        fetched[k].wait()

        def body(i, _):
            rows = pl.ds(pl.multiple_of(i * half, half), half)
            left = near[k % 2, i].reshape(half, width)
            gates[slot, rows, :] = times(left, weights[0])
            ups[slot, rows, :] = times(left, weights[1])
            return 0

        lax.fori_loop(0, 2, body, 0)
        if k + 2 < 4:
            fetched[k + 2] = fetch(k + 2)

    written = {}

    def back(k, slot):
        if k >= 2:
            for copy in written[k - 2]:
                copy.wait()
        room = staged.at[k % 2]

        def body(i, _):
            rows = pl.ds(pl.multiple_of(i * half, half), half)
            grad = times_t(full[chips[k] * 2 + i].reshape(half, width), down[...])
            gate, up = gates[slot, rows, :], ups[slot, rows, :]
            sigma = jax.nn.sigmoid(gate)
            silu = gate * sigma
            room[0, i] = (silu * up).astype(BF16).reshape(2, piece, part)
            dgate = grad * up * sigma * (1.0 + gate * (1.0 - sigma))
            room[1, i] = dgate.astype(BF16).reshape(2, piece, part)
            room[2, i] = (grad * silu).astype(BF16).reshape(2, piece, part)
            return 0

        lax.fori_loop(0, 2, body, 0)
        written[k] = []
        for n, out in enumerate((act_out, dgate_out, dup_out)):
            copy = pltpu.make_async_copy(
                room.at[n], out.at[pl.ds(chips[k] * 2, 2)], out_sem.at[k % 2, n]
            )
            copy.start()
            written[k].append(copy)
        active = room[0].reshape(chip_rows, part)
        tile = width // 3

        def sum_up(n, _):
            columns = pl.ds(pl.multiple_of(n * tile, tile), tile)
            right = full[pl.ds(chips[k] * 2, 2), :, :, columns].reshape(chip_rows, tile)
            product = t_times(active, right)
            if k == 0:
                total[:, columns] = product
            elif k < 3:
                total[:, columns] += product
            else:
                product = total[:, columns] + product
                own = part // planes
                for z in range(planes):
                    grad_out[z, :, columns] = product[z * own : (z + 1) * own].astype(BF16)
            return 0

        lax.fori_loop(0, 3, sum_up, 0)

    gate_up(0, 0)
    if planes > 2:
        ahead.step(1)
    gate_up(1, 1)
    for d in range(2, planes - 1):
        ahead.step(d)
    gather.forward()
    gate_up(2, 2)
    mine.wait()
    gather.arrived(6, 7)
    first_part.wait()
    ahead.finish()
    for zz in range(planes):
        count = part // planes
        down_rows[zz * count : (zz + 1) * count, :] = down_rest[zz].astype(F32)
    down[:, most:] = down_rows[...].astype(BF16)
    back(0, 0)
    gather.second()
    gather.arrived(8, 9)
    back(1, 1)
    gate_up(3, 0)
    gather.arrived(10, 11)
    back(2, 2)
    gather.last()
    gather.arrived(12, 13)
    back(3, 0)
    gather.sent()
    for k in (2, 3):
        for copy in written[k]:
            copy.wait()


def ffn(planes, cot, normed, gathered, down_most, down_own, collective_id):
    _, piece, width = cot.shape
    part, most = down_most.shape
    rest = width - most
    wide = jax.ShapeDtypeStruct((8, 2, piece, part), BF16)
    return pl.pallas_call(
        functools.partial(ffn_kernel, planes),
        out_shape=[
            wide,
            wide,
            wide,
            jax.ShapeDtypeStruct((planes, part // planes, width), BF16),
            jax.ShapeDtypeStruct((part, width), BF16),
        ],
        in_specs=[ANY] * 5,
        out_specs=[ANY, ANY, ANY, VMEM, VMEM],
        scratch_shapes=[
            pltpu.VMEM((planes, part // planes, rest), BF16),
            pltpu.VMEM((part, rest), F32),
            pltpu.VMEM((8, 2, piece, width), BF16),
            pltpu.VMEM((2, 2, 2, piece, width), BF16),
            pltpu.VMEM((2, width, part), BF16),
            pltpu.VMEM((3, 4 * piece, part), F32),
            pltpu.VMEM((3, 4 * piece, part), F32),
            pltpu.VMEM((2, 3, 2, 2, piece, part), BF16),
            pltpu.VMEM((part, width), F32),
            sems(14),
            sems(14),
            sems(4),
            sems(2),
            sems(2, 3),
            sems(2, planes - 1),
            sems(2, planes - 1),
        ],
        cost_estimate=cost(55),
        compiler_params=params(collective_id, 62),
    )(cot, normed, gathered, down_most, down_own)


def room(piece, width):
    return [
        pltpu.VMEM((4, 2, piece, width), BF16),
        pltpu.VMEM((4, 2, piece, width), BF16),
        pltpu.VMEM((3, 2, piece, width), BF16),
        pltpu.VMEM((2, piece, width), F32),
        pltpu.VMEM((2, piece, width), BF16),
        pltpu.VMEM((2, piece, width), BF16),
        pltpu.VMEM((2, piece, width), BF16),
        sems(11),
        sems(11),
    ]


def scatter(lefts, rights, transposed, out, scratch, fills=(), loaded=None):
    staged, held, ready, keep, diag, from_x, from_y, send, recv = scratch
    y, c, _, x = place()
    _, piece, width = out.shape
    rows = 2 * piece
    tile = width // 3
    copies = []

    def go(src, dst, sem, device):
        copy = remote(src, dst, send.at[sem], recv.at[sem], device)
        copy.start()
        copies.append(copy)
        return copy

    def product(dy, dx, core, store, i=None):
        member = (flip(y, dy) * 2 + flip(x, dx)) * 2 + core

        def body(n, _):
            columns = pl.ds(pl.multiple_of(n * tile, tile), tile)
            value = None
            for left, right in zip(lefts, rights):
                a = left[member].reshape(rows, left.shape[-1]) if i is None else left[member, i]
                if transposed:
                    term = times_t(a, right[columns, :])
                else:
                    term = times(a, right[:, columns])
                value = term if value is None else value + term
            store(columns, value.reshape(2, piece, tile) if i is None else value)
            return 0

        lax.fori_loop(0, 3, body, 0)

    order = ((1, 1), (0, 1), (1, 0), (0, 0))
    over = []

    def to_other_core(n):
        dy, dx = order[n]

        def store(columns, value):
            staged[n, :, :, columns] = value.astype(BF16)

        product(dy, dx, 1 - c, store)
        over.append(go(staged.at[n], held.at[n], n, {"core": 1 - c}))

    def own_core(n, store):
        dy, dx = order[n]
        over[n].wait_recv()

        def add(columns, value):
            store(columns, value + held[n, :, :, columns].astype(F32))

        product(dy, dx, c, add)

    def store_x(columns, value):
        ready[1, 1, :, columns] = value[1].astype(BF16)
        keep[0, :, columns] = value[0]

    def store_y(columns, value):
        ready[2, 0, :, columns] = value[0].astype(BF16)
        keep[1, :, columns] = value[1]

    def store_own(columns, value):
        out[:, :, columns] = value

    def diag_half(i):
        dy, dx = order[0]

        def store(columns, value):
            staged[0, i, :, columns] = value.astype(BF16)

        product(dy, dx, 1 - c, store, i)
        return go(staged.at[0, i], held.at[0, i], 0 if i == 0 else 10, {"core": 1 - c})

    def diag_sum(i, copy):
        dy, dx = order[0]

        def store(columns, value):
            copy_in = held[0, i, :, columns].astype(F32)
            ready[0, i, :, columns] = (value + copy_in).astype(BF16)

        copy.wait_recv()
        product(dy, dx, c, store, i)

    if loaded:
        loaded(0)
    halves = [diag_half(0), diag_half(1)]
    diag_sum(0, halves[0])
    diag_y = go(ready.at[0, 0], diag.at[0], 4, {"y": 1 - y})
    diag_sum(1, halves[1])
    diag_x = go(ready.at[0, 1], diag.at[1], 5, {"x": 1 - x})
    over.append(None)
    if loaded:
        loaded(1)
    to_other_core(1)
    if loaded:
        loaded(2)
    to_other_core(2)
    own_core(1, store_x)
    x_one = go(ready.at[1, 1], from_x.at[1], 6, {"x": 1 - x})
    own_core(2, store_y)
    y_zero = go(ready.at[2, 0], from_y.at[0], 7, {"y": 1 - y})
    if loaded:
        loaded(3)
    to_other_core(3)
    own_core(3, store_own)
    if fills and fills[0]:
        fills[0]()
    diag_y.wait_recv()
    ready[1, 0] = (keep[0] + diag[0].astype(F32)).astype(BF16)
    x_zero = go(ready.at[1, 0], from_x.at[0], 8, {"x": 1 - x})
    diag_x.wait_recv()
    ready[2, 1] = (keep[1] + diag[1].astype(F32)).astype(BF16)
    y_one = go(ready.at[2, 1], from_y.at[1], 9, {"y": 1 - y})
    if fills:
        fills[1]()
    for i, (one, two) in enumerate(((x_zero, y_zero), (x_one, y_one))):
        one.wait_recv()
        two.wait_recv()
        out[i] += from_x[i].astype(F32) + from_y[i].astype(F32)
    for copy in copies:
        copy.wait_send()


def by_rows(piece, work):
    step = 32

    def body(n, _):
        rows = pl.ds(pl.multiple_of(n * step, step), step)
        for i in (0, 1):
            work(i, rows)
        return 0

    lax.fori_loop(0, piece // step, body, 0)


def norm_back(i, rows, source, gain, grad, base, sums):
    normal, scale = rms_parts(source)
    term = grad * normal
    sums[...] += (term[:8] + term[8:16]) + (term[16:24] + term[24:])
    return base + rms_back(grad * gain, normal, scale)


def load(pairs, sem):
    copies = [pltpu.make_async_copy(src, dst, sem.at[n]) for n, (src, dst) in enumerate(pairs)]
    for copy in copies:
        copy.start()
    return copies


def far_first():
    y, _, _, x = place()
    return [flip(y, dy) * 2 + flip(x, dx) for dy, dx in ((1, 1), (0, 1), (1, 0), (0, 0))]


def last_kernel(
    planes,
    left_in,
    right_in,
    tokens_in,
    dmiddle_in,
    ins,
    gain,
    token_grad,
    sums,
    in_sum,
    out,
    left,
    right,
    tokens,
    dmiddle,
    ins_got,
    sem,
    send_z,
    recv_z,
    *scratch,
):
    parts = [(right_in, right)]
    parts += [(left_in.at[pl.ds(n * 2, 2)], left.at[pl.ds(n * 2, 2)]) for n in far_first()]
    copies = load(parts + [(tokens_in, tokens), (dmiddle_in, dmiddle)], sem)
    meet(neighbours() + line_peers(planes))
    line = scatter_line(planes, ins, ins_got, send_z, recv_z, sem.at[7])
    copies[0].wait()
    scatter([left], [right], True, out, scratch, loaded=lambda n: copies[1 + n].wait())
    copies[5].wait()
    copies[6].wait()
    sums[...] = jnp.zeros_like(sums)

    def work(i, rows):
        source = tokens[i, rows, :].astype(F32)
        token_grad[i, rows, :] = norm_back(
            i, rows, source, gain[...], out[i, rows, :], dmiddle[i, rows, :], sums
        )

    by_rows(tokens.shape[1], work)
    for copy in line:
        copy.wait()
    for member in range(8):
        total = ins_got[0, member].astype(F32)
        for k in range(1, planes):
            total += ins_got[k, member].astype(F32)
        in_sum[member] = total.astype(BF16)


def last(planes, left, right, tokens, dmiddle, ins, gain, collective_id):
    piece, width = left.shape[2], right.shape[0]
    return pl.pallas_call(
        functools.partial(last_kernel, planes),
        out_shape=[
            jax.ShapeDtypeStruct((2, piece, width), F32),
            jax.ShapeDtypeStruct((8, width), F32),
            jax.ShapeDtypeStruct(ins.shape[1:], BF16),
        ],
        in_specs=[ANY] * 5 + [VMEM],
        out_specs=[VMEM] * 3,
        scratch_shapes=[
            pltpu.VMEM((2, piece, width), F32),
            pltpu.VMEM(left.shape, BF16),
            pltpu.VMEM(right.shape, BF16),
            pltpu.VMEM(tokens.shape, BF16),
            pltpu.VMEM(dmiddle.shape, F32),
            pltpu.VMEM(ins.shape, BF16),
            sems(8),
            sems(planes - 1),
            sems(planes - 1),
        ]
        + room(piece, width),
        cost_estimate=cost(50),
        compiler_params=params(collective_id, 50),
    )(left, right, tokens, dmiddle, ins, gain)


def ffn_back_kernel(
    planes,
    dgate_in,
    dup_in,
    gathered,
    normed,
    middle_in,
    cot_in,
    gain,
    grads,
    dmiddle,
    dmix,
    sums,
    out,
    weights,
    every,
    dgate,
    dup,
    middle,
    cot,
    local,
    sem,
    *scratch,
):
    loads = load_rows(planes, gathered, weights, local.at[0])
    lefts = (dgate, dup)
    parts = []
    for n in far_first():
        rows = pl.ds(n * 2, 2)
        parts += [(dgate_in.at[rows], dgate.at[rows]), (dup_in.at[rows], dup.at[rows])]
    copies = load(parts + [(middle_in, middle), (cot_in, cot)], sem)
    whole = pltpu.make_async_copy(normed, every, local.at[1])
    whole.start()
    meet(neighbours())
    width, part = weights.shape[1:]
    quarter = width // 4
    all_rows = 8 * 2 * normed.shape[2]

    def gradient(j):
        own = grads.shape[-2]

        def body(q, _):
            columns = pl.ds(pl.multiple_of(q * quarter, quarter), quarter)
            left = every[:, :, :, columns].reshape(all_rows, quarter)
            right = lefts[j][...].reshape(all_rows, part)
            value = t_times(left, right).astype(BF16)
            if len(grads.shape) == 3:
                grads[j, columns, :] = value
                return 0
            for z in range(planes):
                for xx in (0, 1):
                    start = (z * 2 + xx) * own
                    grads[z, q * 2 + xx, j] = value[start : start + own]
            return 0

        lax.fori_loop(0, 4, body, 0)

    def both():
        whole.wait()
        gradient(0)
        gradient(1)

    for copy in loads:
        copy.wait()
    rights = [weights.at[0], weights.at[1]]

    def loaded(n):
        copies[2 * n].wait()
        copies[2 * n + 1].wait()

    scatter(lefts, rights, True, out, scratch, (None, both), loaded)
    copies[8].wait()
    copies[9].wait()
    sums[...] = jnp.zeros_like(sums)

    def work(i, rows):
        value = norm_back(
            i,
            rows,
            middle[i, rows, :],
            gain[...],
            out[i, rows, :],
            cot[i, rows, :].astype(F32),
            sums,
        )
        dmiddle[i, rows, :] = value
        dmix[i, rows, :] = value.astype(BF16)

    by_rows(middle.shape[1], work)


def ffn_back(planes, dgate, dup, gathered, normed, middle, cot, gain, collective_id):
    piece, part = dgate.shape[2:]
    width = normed.shape[3]
    return pl.pallas_call(
        functools.partial(ffn_back_kernel, planes),
        out_shape=[
            jax.ShapeDtypeStruct(gathered.shape, BF16),
            jax.ShapeDtypeStruct((2, piece, width), F32),
            jax.ShapeDtypeStruct((2, piece, width), BF16),
            jax.ShapeDtypeStruct((8, width), F32),
        ],
        in_specs=[ANY] * 6 + [VMEM],
        out_specs=[VMEM] * 4,
        scratch_shapes=[
            pltpu.VMEM((2, piece, width), F32),
            pltpu.VMEM((2, width, part), BF16),
            pltpu.VMEM((8, 2, piece, width), BF16),
            pltpu.VMEM(dgate.shape, BF16),
            pltpu.VMEM(dup.shape, BF16),
            pltpu.VMEM(middle.shape, F32),
            pltpu.VMEM(cot.shape, BF16),
            sems(2),
            sems(10),
        ]
        + room(piece, width),
        cost_estimate=cost(60),
        compiler_params=params(collective_id, 60),
    )(dgate, dup, gathered, normed, middle, cot, gain)


def ring():
    z, planes = lax.axis_index("z"), lax.axis_size("z")
    return {"z": lax.rem(z + 1, planes)}, {"z": lax.rem(z + planes - 1, planes)}


def load_in(planes, gathered, rows, sem):
    if len(gathered.shape) == 2:
        copies = [pltpu.make_async_copy(gathered, rows, sem)]
    else:
        own = gathered.shape[2]
        copies = []
        for z in range(planes):
            for m in range(8):
                start = (((m // 2) * planes + z) * 2 + m % 2) * own
                to = rows.at[pl.ds(start, own)]
                copies.append(pltpu.make_async_copy(gathered.at[z, m], to, sem))
    for copy in copies:
        copy.start()
    return copies


def mixer_kernel(
    planes,
    tokens_all,
    gathered,
    taps,
    blocks,
    tokens,
    gain,
    out,
    normed_two,
    normed_out,
    proj_out,
    conv_out,
    gated_out,
    weights_out,
    right,
    rows_out,
    own,
    every,
    weights,
    proj,
    conv,
    gated,
    tall,
    ends,
    before,
    local,
    ends_sem,
    send,
    recv,
    rights,
    got,
    send_o,
    recv_o,
    send_s,
    recv_s,
):
    y, c, z, x = place()
    me = (y * 2 + x) * 2 + c
    _, _, piece, width = every.shape
    part = conv.shape[-1]
    loads = load_in(planes, gathered, weights, local.at[0])
    chips = {}
    for n, chip in enumerate((1, 3, 0, 2)):
        rows = pl.ds(chip * 2, 2)
        chips[chip] = pltpu.make_async_copy(tokens_all.at[rows], every.at[rows], local.at[1 + n])
        chips[chip].start()
    after, prior = ring()
    meet(others() + [after, prior])
    count = blocks.shape[1]
    for zz in range(planes):
        rows_out[zz * count : (zz + 1) * count, :] = blocks[zz].astype(F32)
    right[...] = rows_out[...].astype(BF16).reshape(right.shape)
    whole = Gather(right, rights, send_o, recv_o)
    whole.first()
    own_right = pltpu.make_async_copy(right, rights.at[me], local.at[11])
    own_right.start()
    for copy in loads:
        copy.wait()
    saved = [pltpu.make_async_copy(weights, weights_out, local.at[5])]

    def project(member):
        value = every[member].reshape(2 * piece, width).astype(F32)
        value = (rms_parts(value)[0] * gain[0:1, :]).astype(BF16)
        every[member] = value.reshape(2, piece, width)
        a = every[member].reshape(2 * piece, width)
        proj[member] = times(a, weights[...]).reshape(2, piece, 3 * part)

    def inner(member, i, rows):
        return proj[member, i, rows, :part] * proj[member, i, rows, 2 * part :]

    last = slice(piece - 2, piece)
    for yy in (0, 1):
        chips[yy * 2 + 1].wait()

        def second(core, _):
            member = (yy * 2 + 1) * 2 + core
            project(member)
            for i in (0, 1):
                ends[(yy * 2 + core) * 2 + i] = inner(member, i, last)
            return 0

        lax.fori_loop(0, 2, second, 0)
    to_next = remote(ends, before, ends_sem.at[0], ends_sem.at[1], after)
    to_next.start()
    for yy in (0, 1):
        chips[yy * 2].wait()

        def first(core, _):
            project((yy * 2) * 2 + core)
            return 0

        lax.fori_loop(0, 2, first, 0)
        if yy == 0:
            whole.forward()
    whole.second()
    saved.append(pltpu.make_async_copy(proj, proj_out, local.at[6]))
    saved.append(pltpu.make_async_copy(every, normed_out, local.at[10]))
    for copy in saved:
        copy.start()

    def convolve(member, i, start):
        tall[6:8, :] = start
        now = inner(member, i, slice(0, piece))
        tall[8 : 8 + piece, :] = now
        value = taps[0:1] * tall[6 : 6 + piece, :] + taps[1:2] * tall[7 : 7 + piece, :]
        value += taps[2:3] * now
        conv[member, i] = value
        gate = proj[member, i, :, part : 2 * part]
        gated[member, i] = (gate * value).astype(BF16)

    def right_half(n, _):
        member = (n // 2) * 4 + 2 + n % 2
        for i in (0, 1):
            convolve(member, i, inner(member - 2, i, last))
        return 0

    lax.fori_loop(0, 4, right_half, 0)
    whole.last()
    to_next.wait_recv()

    def left_half(n, _):
        member = (n // 2) * 4 + n % 2
        for i in (0, 1):
            start = before[n * 2 + i]
            convolve(member, i, jnp.where(z > 0, start, jnp.zeros_like(start)))
        return 0

    lax.fori_loop(0, 4, left_half, 0)
    swapped = [pltpu.make_async_copy(gated.at[me], got.at[me], local.at[12])]
    for f, peer in enumerate(others()):
        to = (peer["y"] * 2 + peer["x"]) * 2 + peer["core"]
        swapped.append(remote(gated.at[to], got.at[me], send_s.at[f], recv_s.at[f], peer))
    for copy in swapped:
        copy.start()
    for n, (src, dst) in enumerate(((conv, conv_out), (gated, gated_out))):
        saved.append(pltpu.make_async_copy(src, dst, local.at[7 + n]))
        saved[-1].start()
    whole.arrived(*range(6, 14))
    whole.sent()
    own_right.wait()
    for copy in swapped:
        copy.wait()
    third = width // 3

    def mix(n, _):
        columns = pl.ds(pl.multiple_of(n * third, third), third)
        total = tokens[:, :, columns].astype(F32).reshape(2 * piece, third)
        for member in range(8):
            left = got[member].reshape(2 * piece, part)
            total += times(left, rights[member, :, :, columns].reshape(part, third))
        out[:, :, columns] = total.reshape(2, piece, third)
        return 0

    lax.fori_loop(0, 3, mix, 0)

    def work(i, rows):
        own[i, rows, :] = (rms_parts(out[i, rows, :])[0] * gain[1:2, :]).astype(BF16)

    by_rows(piece, work)
    gather = Gather(own, normed_two, send, recv)
    gather.first()
    mine = pltpu.make_async_copy(own, normed_two.at[(y * 2 + x) * 2 + c], local.at[9])
    mine.start()
    saved.append(mine)
    gather.forward()
    gather.second()
    gather.last()
    gather.arrived(*range(6, 14))
    gather.sent()
    to_next.wait_send()
    for copy in saved:
        copy.wait()


def mixer_forward(planes, tokens_all, gathered, taps, blocks, tokens, gain, collective_id):
    _, _, piece, width = tokens_all.shape
    part = blocks.shape[1] * planes
    saved = [
        (tokens_all.shape, BF16),
        (tokens_all.shape, BF16),
        ((8, 2, piece, 3 * part), F32),
        ((8, 2, piece, part), F32),
        ((8, 2, piece, part), BF16),
        ((width, 3 * part), BF16),
    ]
    return pl.pallas_call(
        functools.partial(mixer_kernel, planes),
        out_shape=[jax.ShapeDtypeStruct((2, piece, width), F32)]
        + [jax.ShapeDtypeStruct(*item) for item in saved]
        + [jax.ShapeDtypeStruct((2, part // 2, width), BF16)],
        in_specs=[ANY, ANY] + [VMEM] * 4,
        out_specs=[VMEM] + [ANY] * 6 + [VMEM],
        scratch_shapes=[
            pltpu.VMEM((part, width), F32),
            pltpu.VMEM((2, piece, width), BF16),
            pltpu.VMEM((8, 2, piece, width), BF16),
            pltpu.VMEM((width, 3 * part), BF16),
            pltpu.VMEM((8, 2, piece, 3 * part), F32),
            pltpu.VMEM((8, 2, piece, part), F32),
            pltpu.VMEM((8, 2, piece, part), BF16),
            pltpu.VMEM((8 + piece, part), F32),
            pltpu.VMEM((8, 2, part), F32),
            pltpu.VMEM((8, 2, part), F32),
            sems(13),
            sems(2),
            sems(14),
            sems(14),
            pltpu.VMEM((8, 2, part // 2, width), BF16),
            pltpu.VMEM((8, 2, piece, part), BF16),
            sems(14),
            sems(14),
            sems(7),
            sems(7),
        ],
        cost_estimate=cost(95),
        compiler_params=params(collective_id, 60),
    )(tokens_all, gathered, taps, blocks, tokens, gain)


def branch_kernel(
    planes,
    active_in,
    down_in,
    own,
    right,
    proj_in,
    conv_in,
    gated_in,
    normed,
    taps,
    out,
    dmix,
    dproj,
    grad_in,
    grad_out,
    grad_taps,
    near,
    active,
    down,
    gated,
    proj,
    conv,
    tall,
    starts,
    beyond,
    total_out,
    total_in,
    near_sem,
    local,
    ends_sem,
    send,
    recv,
    *scratch,
):
    y, c, z, x = place()
    _, _, piece, part = conv.shape
    width = out.shape[2]
    chips = [flip(y, dy) * 2 + flip(x, dx) for dy, dx in ((0, 0), (0, 1), (1, 0), (1, 1))]
    half = 2 * piece

    def fetch(source, k):
        copy = pltpu.make_async_copy(
            source.at[pl.ds(chips[k] * 2, 2)], near.at[k % 2], near_sem.at[k % 2]
        )
        copy.start()
        return copy

    after, prior = ring()
    meet(neighbours() + [after, prior])
    gather = Gather(own, dmix, send, recv)
    gather.first()
    mine = pltpu.make_async_copy(own, dmix.at[(y * 2 + x) * 2 + c], local.at[5])
    mine.start()
    pairs = [(active_in, active), (down_in, down), (proj_in, proj), (conv_in, conv)]
    loads = load(pairs + [(gated_in, gated)], local)
    to_prior = remote(starts.at[0], beyond, ends_sem.at[0], ends_sem.at[1], prior)
    grad_taps[...] = jnp.zeros_like(grad_taps)
    third = width // 3

    def gradients(k):
        chip, other = chips[k], flip(x, k % 2)

        def body(core, _):
            member = chip * 2 + core
            grad = times_t(near[k % 2, core].reshape(half, width), right[...])
            grad = grad.reshape(2, piece, part)
            for i in (0, 1):
                dproj[member, i, :, part : 2 * part] = (grad[i] * conv[member, i]).astype(BF16)
                dconv = grad[i] * proj[member, i, :, part : 2 * part]
                conv[member, i] = dconv
                starts[other, (flip(y, k // 2) * 2 + core) * 2 + i] = dconv[:2]
            return 0

        lax.fori_loop(0, 2, body, 0)

        def sum_up(n, _):
            columns = pl.ds(pl.multiple_of(n * third, third), third)
            left = gated[pl.ds(chip * 2, 2)].reshape(2 * half, part)
            product = t_times(left, near[k % 2, :, :, :, columns].reshape(2 * half, third))
            if k == 0:
                total_out[:, columns] = product
            elif k < 3:
                total_out[:, columns] += product
            else:
                product = total_out[:, columns] + product
                own_rows = part // planes
                for zz in range(planes):
                    block = product[zz * own_rows : (zz + 1) * own_rows]
                    grad_out[zz, :, columns] = block.astype(BF16)
            return 0

        lax.fori_loop(0, 3, sum_up, 0)

    def through(member, i, end):
        tall[0:piece, :] = conv[member, i]
        tall[piece : piece + 2, :] = end
        now, one, two = conv[member, i], tall[1 : piece + 1, :], tall[2 : piece + 2, :]
        b_part, x_part = proj[member, i, :, :part], proj[member, i, :, 2 * part :]
        dmixed = taps[2:3] * now + taps[1:2] * one + taps[0:1] * two
        dproj[member, i, :, :part] = (dmixed * x_part).astype(BF16)
        dproj[member, i, :, 2 * part :] = (dmixed * b_part).astype(BF16)
        mixed = b_part * x_part
        for k, shifted in enumerate((two, one, now)):
            grad_taps[k : k + 1, :] += jnp.sum(mixed * shifted, axis=0, keepdims=True)

    def left_half(n, _):
        member = (n // 2) * 4 + n % 2
        for i in (0, 1):
            through(member, i, conv[member + 2, i, 0:2, :])
        return 0

    def right_half(n, _):
        member = (n // 2) * 4 + 2 + n % 2
        for i in (0, 1):
            end = beyond[n * 2 + i]
            through(member, i, jnp.where(z < planes - 1, end, jnp.zeros_like(end)))
        return 0

    def one():
        for copy in loads[2:]:
            copy.wait()
        mine.wait()
        gather.arrived(6, 7)
        fetch(dmix, 0).wait()
        gradients(0)
        gather.second()
        gather.arrived(8, 9)
        fetched = fetch(dmix, 1)
        gather.arrived(10, 11)
        following = fetch(dmix, 2)
        fetched.wait()
        gradients(1)
        following.wait()
        gradients(2)

    def one_more():
        gather.last()
        gather.arrived(12, 13)
        fetch(dmix, 3).wait()
        to_normed.append(fetch(normed, 0))
        gradients(3)
        to_normed.append(fetch(normed, 1))
        to_prior.start()
        lax.fori_loop(0, 4, left_half, 0)

    quarter = width // 4

    def two():
        one_more()
        to_prior.wait_recv()
        lax.fori_loop(0, 4, right_half, 0)
        for k in range(4):
            to_normed[k].wait()

            def sum_up(q, _):
                columns = pl.ds(pl.multiple_of(q * quarter, quarter), quarter)
                left = near[k % 2, :, :, :, columns].reshape(2 * half, quarter)
                right_side = dproj[pl.ds(chips[k] * 2, 2)].reshape(2 * half, 3 * part)
                product = t_times(left, right_side)
                if k == 0:
                    total_in[columns, :] = product
                elif k < 3:
                    total_in[columns, :] += product
                else:
                    product = (total_in[columns, :] + product).astype(BF16)
                    if len(grad_in.shape) == 2:
                        grad_in[columns, :] = product
                        return 0
                    own_rows = grad_in.shape[2]
                    for zz in range(planes):
                        for xx in (0, 1):
                            start = (zz * 2 + xx) * own_rows
                            grad_in[zz, q * 2 + xx] = product[start : start + own_rows]
                return 0

            lax.fori_loop(0, 4, sum_up, 0)
            if k < 2:
                to_normed.append(fetch(normed, k + 2))

    to_normed = []
    gather.forward()
    loads[0].wait()
    loads[1].wait()
    scatter([active], [down], False, out, scratch, (one, two))
    gather.sent()
    to_prior.wait_send()


def branch_forward(
    planes, active, down, dmix, right, proj, conv, gated, normed, taps, in_shape, collective_id
):
    _, piece, width = dmix.shape
    part = right.shape[0]
    outs = [
        ((2, piece, width), F32),
        (normed.shape, BF16),
        ((8, 2, piece, 3 * part), BF16),
        (in_shape, BF16),
        ((planes, part // planes, width), BF16),
        ((3, part), F32),
    ]
    got = pl.pallas_call(
        functools.partial(branch_kernel, planes),
        out_shape=[jax.ShapeDtypeStruct(*item) for item in outs],
        in_specs=[ANY, ANY, ANY, VMEM, ANY, ANY, ANY, ANY, VMEM],
        out_specs=[VMEM, ANY] + [VMEM] * 4,
        scratch_shapes=[
            pltpu.VMEM((2, 2, 2, piece, width), BF16),
            pltpu.VMEM(active.shape, BF16),
            pltpu.VMEM(down.shape, BF16),
            pltpu.VMEM(gated.shape, BF16),
            pltpu.VMEM((8, 2, piece, 3 * part), F32),
            pltpu.VMEM((8, 2, piece, part), F32),
            pltpu.VMEM((8 + piece, part), F32),
            pltpu.VMEM((2, 8, 2, part), F32),
            pltpu.VMEM((8, 2, part), F32),
            pltpu.VMEM((part, width), F32),
            pltpu.VMEM((width, 3 * part), F32),
            sems(2),
            sems(6),
            sems(2),
            sems(14),
            sems(14),
        ]
        + room(piece, width),
        cost_estimate=cost(90),
        compiler_params=params(collective_id, 62),
    )(active, down, dmix, right, proj, conv, gated, normed, taps)
    return got[:1] + got[2:]


def update_kernel(planes, three, rate, decay, got, weight, first, second, grad, moment, updated):
    wide = got.shape[-1] // planes
    parts = 1
    if three:
        wide, parts = wide // 3, 3
    for k in range(parts):
        for owner in range(8 * planes):
            pair, z, xx = owner // (2 * planes), owner // 2 % planes, owner % 2
            start = (k * planes + z) * wide
            to = (k * 8 * planes + owner) * wide
            if three:
                value = got[pair * 2 + xx, :, start : start + wide]
            else:
                value = got[pair * 2 + xx, 0, :, start : start + wide]
            if three:
                grad[:, to : to + wide] = value.astype(F32)
            else:
                grad[0, :, to : to + wide] = value.astype(F32)
    moment[...], updated[...] = adamw(
        weight[...], first[...], second[...], grad[...], rate, decay
    )


def update(planes, got, weight, first, second, rate, decay):
    three = weight.ndim == 2
    rows = weight.shape[-2]
    step = 16 if rows % 16 == 0 else rows
    part = got.shape[-1]
    columns = weight.shape[-1]
    if three:
        grid = (rows // step,)
        got_spec = pl.BlockSpec((8, step, part), lambda n: (0, n, 0))
        spec = pl.BlockSpec((step, columns), lambda n: (n, 0))
    else:
        grid = (2, rows // step)
        got_spec = pl.BlockSpec((8, 1, step, part), lambda j, n: (0, j, n, 0))
        spec = pl.BlockSpec((1, step, columns), lambda j, n: (j, n, 0))
    size = weight.size * 4
    return pl.pallas_call(
        functools.partial(update_kernel, planes, three, rate, decay),
        out_shape=[jax.ShapeDtypeStruct(weight.shape, F32)] * 3,
        grid=grid,
        in_specs=[got_spec, spec, spec, spec],
        out_specs=[spec] * 3,
        cost_estimate=pl.CostEstimate(
            flops=12 * size, bytes_accessed=7 * size, transcendentals=0
        ),
        compiler_params=pltpu.CompilerParams(vmem_limit_bytes=32 * 2**20),
    )(got, weight, first, second)


def rms_parts(values):
    scale = lax.rsqrt(jnp.mean(values * values, axis=-1, keepdims=True) + 1e-05)
    return (values * scale, scale)


def rms_back(grad_hat, normal, scale):
    return scale * (grad_hat - normal * jnp.mean(grad_hat * normal, axis=-1, keepdims=True))


def times(left, right):
    return jnp.dot(left, right, preferred_element_type=F32)


def times_t(left, right):
    return lax.dot_general(left, right, (((1,), (1,)), ((), ())), preferred_element_type=F32)


def t_times(left, right):
    return lax.dot_general(left, right, (((0,), (0,)), ((), ())), preferred_element_type=F32)


def adamw(weight, first_mom, second_mom, gradient, rate, decay):
    bias_one = 1.0 - 0.9**STEP
    bias_two = 1.0 - 0.95**STEP
    first_new = 0.9 * first_mom + 0.1 * gradient
    second_new = 0.95 * second_mom + 0.05 * gradient * gradient
    direction = first_new / bias_one / (jnp.sqrt(second_new / bias_two) + 1e-08)
    return (second_new, weight - rate * (direction + decay * weight))


def on_device(
    tokens,
    cotangent,
    norm_gains,
    in_proj,
    conv_taps,
    out_proj,
    gate_up,
    down_proj,
    first_gains,
    first_in,
    first_conv,
    first_out,
    first_gate_up,
    first_down,
    second_gains,
    second_in,
    second_conv,
    second_out,
    second_gate_up,
    second_down,
):
    planes = lax.axis_size("z")
    seqs, piece, width = tokens.shape
    rows = seqs * piece
    all_rows = 8 * rows
    own_d = in_proj.shape[0]
    own_f = down_proj.shape[0]
    ff = gate_up.shape[2]
    part_d = width // 8
    part_f = ff // 8

    in_tiles = own_d % 16 == 0

    def along_z(value):
        return lax.all_gather(value, "z", axis=0, tiled=False)

    most = width // 2
    down_low = down_proj.astype(BF16)
    down_most = along_z(down_low[:, :most]).reshape(part_f, most)
    small = jnp.concatenate([norm_gains, conv_taps], axis=0)
    tokens_all, gu_mine, in_t, out_blocks, gains, taps = early(
        planes, small, tokens, in_proj, gate_up, out_proj, 0
    )
    if not in_tiles:
        in_t = in_t.reshape(planes, 4, 2, own_d, 3 * part_d).transpose(1, 0, 2, 3, 4)
        in_t = in_t.reshape(width, 3 * part_d)
    gu_t = along_z(gu_mine)
    if not in_tiles:
        gu_t = gu_t.reshape(planes, 4, 2, 2, own_d, part_f).transpose(3, 1, 0, 2, 4, 5)
        gu_t = gu_t.reshape(2, width, part_f)

    middle, normed_two_all, normed_all, proj, conv, gated, in_whole, out_t = mixer_forward(
        planes, tokens_all, in_t, taps, out_blocks, tokens, gains, 2
    )
    out_t = out_t.reshape(part_d, width)
    active, dgate, dup, grad_down, down_t = ffn(
        planes, cotangent, normed_two_all, gu_t, down_most, down_low[:, most:], 4
    )

    def sum_z(value):
        return lax.psum_scatter(value, "z", scatter_dimension=0, tiled=False)

    g_down = sum_z(grad_down)
    grad_gu, dmiddle, dmix, gain_two = ffn_back(
        planes, dgate, dup, gu_t, normed_two_all, middle, cotangent, gains[1:], 5
    )
    if not in_tiles:
        grad_gu = grad_gu.reshape(2, 4, planes, 2, own_d, part_f).transpose(2, 1, 3, 0, 4, 5)
        grad_gu = grad_gu.reshape(planes, 8, 2, own_d, part_f)
    grad_gu, g_down = lax.optimization_barrier((grad_gu, g_down))
    g_down = g_down.astype(F32)
    gu_back = sum_z(grad_gu)

    branch, dproj, grad_in, grad_out, grad_taps = branch_forward(
        planes,
        active,
        down_t,
        dmix,
        out_t,
        proj,
        conv,
        gated,
        normed_all,
        taps,
        in_t.shape,
        7,
    )
    block_out = (middle + branch).astype(BF16)
    if not in_tiles:
        grad_in = grad_in.reshape(4, planes, 2, own_d, 3 * part_d).transpose(1, 0, 2, 3, 4)
        grad_in = grad_in.reshape(planes, 8, own_d, 3 * part_d)
    taps_parts = grad_taps.reshape(3, planes, own_d).transpose(1, 0, 2)

    token_grad, gain_one, in_back = last(
        planes, dproj, in_whole, tokens, dmiddle, grad_in, gains[:1], 8
    )
    grad_gains = jnp.stack([jnp.sum(gain_one, axis=0), jnp.sum(gain_two, axis=0)])
    gains_parts = grad_gains.reshape(2, 4, planes, 2, own_d).transpose(1, 3, 2, 0, 4)
    gains_parts = gains_parts.reshape(8, planes, 2, own_d)
    in_got, gu_got, sums, g_out = finish(
        planes, in_back, gu_back, gains_parts, taps_parts, grad_out, 9
    )
    g_gains, g_conv = sums[:2], sums[2:]
    m_gains, u_gains = adamw(norm_gains, first_gains, second_gains, g_gains, 0.4, 0.0)
    g_in, m_in, u_in = update(planes, in_got, in_proj, first_in, second_in, 0.02, 0.1)
    m_conv, u_conv = adamw(conv_taps, first_conv, second_conv, g_conv, 0.2, 0.1)
    m_out, u_out = adamw(out_proj, first_out, second_out, g_out, 0.02, 0.1)
    g_gu, m_gu, u_gu = update(
        planes, gu_got, gate_up, first_gate_up, second_gate_up, 0.02, 0.1
    )
    m_down, u_down = adamw(down_proj, first_down, second_down, g_down, 0.01, 0.1)
    return (
        block_out,
        token_grad,
        g_gains,
        g_in,
        g_conv,
        g_out,
        g_gu,
        g_down,
        m_gains,
        m_in,
        m_conv,
        m_out,
        m_gu,
        m_down,
        u_gains,
        u_in,
        u_conv,
        u_out,
        u_gu,
        u_down,
    )


def solution(mesh):
    lines = mesh.shape["seq"] // 2
    fine = Mesh(mesh.devices.reshape(2, 2, lines, 2), ("y", "core", "z", "x"))
    dp, seq = ("y", "core"), ("z", "x")
    every = dp + seq
    tokens = P(dp, seq, None)
    weights = (
        P(None, every),
        P(every, None),
        P(None, every),
        P(every, None),
        P(None, every, None),
        P(every, None),
    )
    return jax.shard_map(
        on_device,
        mesh=fine,
        in_specs=(tokens, tokens) + weights * 3,
        out_specs=(tokens, tokens) + weights * 3,
        check_vma=False,
    )
```
